512 devices in a mesh: brick: 128 (over y, z_hi, x, core), plane: 4 (over z_lo).
Axes of the slice: x: 4, y: 4, z: 16 (z_hi: 4, z_lo: 4; z = z_hi * 4 + z_lo), core: 2. Of those that a mesh axis runs over, the one named last changes fastest.
Arguments:
- positions: float32 [128, 4, 3, 4096], P('brick', 'plane'), may hold values from 0 to 64
- aux: float32 [128, 4, 4096], P('brick', 'plane'), may hold values from -1 to 1.8
- aux_prev: float32 [128, 4, 4096], P('brick', 'plane'), may hold values from -3 to 3
- resid: float32 [128, 4, 4096], P('brick', 'plane'), may hold values from -2 to 2
- types: int32 [128, 4, 4096], P('brick', 'plane'), may hold values from 0 to 7
- pair_tiles: int32 [128, 4, 1496], P('brick', 'plane'), may hold values from 0 to 63, as said below
- pair_cands: int32 [128, 4, 1496], P('brick', 'plane'), may hold values from 0 to 319, as said below
- pair_count: int32 [128, 4], P('brick', 'plane'), may hold values from 0 to 1496, as said below
- owner_tile: int32 [128, 4, 64], P('brick', 'plane'), may hold values from 0 to 255, as said below
- electroneg: float32 [8], replicated, may hold values from -3 to 3
- hardness: float32 [8], replicated, may hold values from 6 to 14
- widths: float32 [8], replicated, may hold values from 0.6 to 2
Outputs:
- charges: float32 [128, 4, 4096], P('brick', 'plane')
- next_aux: float32 [128, 4, 4096], P('brick', 'plane')
- resid_field: float32 [128, 4, 4096], P('brick', 'plane')
The draws below stay inside these ranges and needn't reach their ends.
Inputs may be any that keep to these rules, and one draw needn't show every extreme that they name: `pair_tiles`: entries after the first pair_count[b, p] of a brick's list are not used. `pair_cands`: A used pair never names a neighbour brick beyond the ends of the brick axis. `pair_count`: at most 1496 pairs a brick, reached by some brick. `owner_tile`: for each b the values over all p and t form a permutation of 0 to 255, and each brick (b, p) has exactly 16 tiles of each value // 64.
All inputs are finite; a program needn't handle non-finite values.
Results may differ from the reference program's by a relative error of at most 0.0003.
Values sent between devices are 32-bit elements; how exact they have to be, the bound alone decides.
A program may use at most 64 MiB of HBM per device.

```python
import math
import jax
import jax.numpy as jnp
from jax import lax

TX = 2
TY = 4
TZ = 8
TILE = 64
NTYPES = 8
BRICKS = 128
PLANES = 4
ATOMS_DEV = 4096
PAIR_CAP = 1496


def pair_lists(key):
    base_key = jax.random.fold_in(key, 7)
    portion_key, ranking_key = jax.random.split(base_key)
    tile_count = TX * TY * TZ
    entries = tile_count * 27
    flat_index = jnp.arange(entries, dtype=jnp.int32)
    tile_of = flat_index // 27
    offset_of = flat_index % 27
    step_x = offset_of // 9 - 1
    step_y = offset_of // 3 % 3 - 1
    step_z = offset_of % 3 - 1
    home_x = tile_of // (TY * TZ)
    home_y = tile_of // TZ % TY
    home_z = tile_of % TZ
    reach_x = home_x + step_x
    reach_y = home_y + step_y
    reach_z = home_z + step_z
    below_x = reach_x < 0
    beyond_x = reach_x >= TX
    below_y = reach_y < 0
    beyond_y = reach_y >= TY
    cross_x = below_x | beyond_x
    cross_y = below_y | beyond_y
    inside = (reach_z >= 0) & (reach_z < TZ) & jnp.logical_not(cross_x & cross_y)
    block_of = jnp.where(below_x, 1, jnp.where(beyond_x, 2, jnp.where(below_y, 3, jnp.where(beyond_y, 4, 0))))
    partner = block_of * tile_count + (reach_x % TX * TY + reach_y % TY) * TZ + jnp.clip(reach_z, 0, TZ - 1)
    brick_of = jnp.arange(BRICKS, dtype=jnp.int32)[:, None, None]
    usable = inside[None, None, :] & jnp.logical_not(below_x[None, None, :] & (brick_of == 0))
    usable = usable & jnp.logical_not(beyond_x[None, None, :] & (brick_of == BRICKS - 1))
    usable = jnp.broadcast_to(usable, (BRICKS, PLANES, entries))
    crowded = brick_of >= 3 * BRICKS // 4
    portion = jnp.where(crowded, 20, jax.random.randint(portion_key, (BRICKS, PLANES, 1), 3, 7))
    usable_int = usable.astype(jnp.int32)
    pair_total = jnp.sum(usable_int, axis=-1, keepdims=True) * portion // 20
    scores = jax.random.randint(ranking_key, (BRICKS, PLANES, entries), 0, entries) * entries + flat_index[None, None, :]
    ranking = jnp.argsort(-(usable_int * entries * entries + scores), axis=-1)[:, :, :PAIR_CAP]
    chosen_tiles = jnp.take(tile_of, ranking)
    chosen_partners = jnp.take(partner, ranking)
    return (chosen_tiles.astype(jnp.int32), chosen_partners.astype(jnp.int32), pair_total[:, :, 0].astype(jnp.int32))


def draw_pair_tiles(key, part):
    return pair_lists(key)[0]


def draw_pair_cands(key, part):
    return pair_lists(key)[1]


def draw_pair_count(key, part):
    return pair_lists(key)[2]


def draw_owner_tile(key, part):
    tile_count = TX * TY * TZ
    quarter = tile_count // PLANES

    def one_brick(brick_key):
        source_key, slot_key = jax.random.split(brick_key)
        orders = jax.vmap(lambda inner: jax.random.permutation(inner, tile_count))(jax.random.split(source_key, PLANES))
        slots = jax.vmap(lambda inner: jax.random.permutation(inner, tile_count))(jax.random.split(slot_key, PLANES))
        position = jnp.arange(tile_count, dtype=jnp.int32)
        owner = position // quarter
        within = position % quarter
        source = jnp.arange(PLANES, dtype=jnp.int32)[:, None]
        value = owner[None, :] * tile_count + slots[owner[None, :], source * quarter + within[None, :]]
        return jnp.zeros((PLANES, tile_count), jnp.int32).at[source, orders].set(value.astype(jnp.int32))
    return jax.vmap(one_brick)(jax.random.split(jax.random.fold_in(key, 11), BRICKS))


def draw_positions(key, part):
    tile_count = TX * TY * TZ
    atom_index = jnp.arange(tile_count * TILE, dtype=jnp.int32)
    tile_of = atom_index // TILE
    cell_index = jnp.stack([tile_of // (TY * TZ), tile_of // TZ % TY, tile_of % TZ]).astype(jnp.float32)
    jitter = jax.random.uniform(jax.random.fold_in(key, 3), (BRICKS, PLANES, 3, tile_count * TILE), jnp.float32)
    return (cell_index[None, None] + jitter) * 8.0


def draw_aux(key, part):
    full_shape = (BRICKS, PLANES, TX * TY * TZ * TILE)
    level = jnp.arange(BRICKS, dtype=jnp.float32)[:, None, None] / (BRICKS - 1)
    inner = jax.random.fold_in(key, 5)
    jitter = 0.3 * jnp.clip(jax.random.normal(inner, full_shape, jnp.float32), -4.0, 4.0)
    center = 0.2 + 0.4 * level
    return center + jitter


def touch_ends(result, stream_key, least, largest):
    longest = result.shape.index(max(result.shape))
    spots = []
    for shift in (0, 1):
        where = [jax.random.randint(jax.random.fold_in(stream_key, axis), (), 0, length) for axis, length in enumerate(result.shape)]
        where[longest] = (where[longest] + shift) % result.shape[longest]
        spots.append(tuple(where))
    return result.at[spots[0]].set(least).at[spots[1]].set(largest)


def block_levels(rng, dims, cuts, smallest, largest):
    factor_of = 1.0
    for dim, shards_of in cuts:
        steps = jax.random.uniform(jax.random.fold_in(jax.random.fold_in(rng, 6), dim), (shards_of,), jnp.float32, smallest / len(cuts), largest / len(cuts))
        factor_of = factor_of * jnp.repeat(jnp.exp(steps), dims[dim] // shards_of).reshape((-1,) + (1,) * (len(dims) - 1 - dim))
    return factor_of


def centred(own_key, extent, deviation, bound, shards=(), kind=jnp.bfloat16):
    result = deviation * jax.random.normal(own_key, extent, jnp.float32)
    if shards:
        result = result * block_levels(own_key, extent, shards, -0.22, 0.18)
    return jnp.clip(result, -bound, bound).astype(kind)


def setup_inputs(seed: int = 0) -> dict:
    key_list = jax.random.split(jax.random.key(seed), 13)
    return {
        "positions": draw_positions(jax.random.fold_in(key_list[12], 71), 0),
        "aux": draw_aux(jax.random.fold_in(key_list[12], 71), 0),
        "aux_prev": centred(key_list[2], (BRICKS, PLANES, ATOMS_DEV), 0.5, 3.0, ((0, 128), (1, 4)), jnp.float32),
        "resid": centred(key_list[3], (BRICKS, PLANES, ATOMS_DEV), 0.3, 2.0, ((0, 128), (1, 4)), jnp.float32),
        "types": touch_ends(jax.random.randint(key_list[4], (BRICKS, PLANES, ATOMS_DEV), 0, NTYPES), jax.random.fold_in(key_list[4], 1), 0, NTYPES - 1).astype(jnp.int32),
        "pair_tiles": draw_pair_tiles(jax.random.fold_in(key_list[12], 71), 0),
        "pair_cands": draw_pair_cands(jax.random.fold_in(key_list[12], 71), 0),
        "pair_count": draw_pair_count(jax.random.fold_in(key_list[12], 71), 0),
        "owner_tile": draw_owner_tile(jax.random.fold_in(key_list[12], 71), 0),
        "electroneg": jnp.clip(jax.random.uniform(key_list[9], (NTYPES,), jnp.float32, -3.0, 3.0), -3.0, 3.0),
        "hardness": jnp.clip(jnp.exp(jax.random.uniform(key_list[10], (NTYPES,), jnp.float32, math.log(6.0), math.log(14.0))), 6.0, 14.0),
        "widths": jnp.clip(jnp.exp(jax.random.uniform(key_list[11], (NTYPES,), jnp.float32, math.log(0.6), math.log(2.0))), 0.6, 2.0),
    }


cell_edge = 8.0
cutoff = 10.0
soften = 0.5
kappa = 1.86
pair_group = 256

def lookup(type_table, type_row):
    chosen = (type_row[None, :] == jnp.arange(type_table.shape[0], dtype=jnp.int32)[:, None]).astype(type_table.dtype)
    return lax.optimization_barrier(jnp.sum(type_table[:, None] * chosen, axis=0))

def candidates(blocks, tile_count):
    joined = jnp.stack(blocks, axis=1)
    offsets = jnp.zeros((6, 5), jnp.float32)
    offsets = offsets.at[0, 1].set(-TX * cell_edge).at[0, 2].set(TX * cell_edge)
    offsets = offsets.at[1, 3].set(-TY * cell_edge).at[1, 4].set(TY * cell_edge)
    joined = joined + offsets[:, :, None]
    return joined.reshape(6, 5 * tile_count, TILE)

def pair_terms(home_tiles, candidate, near_ids, far_ids, in_range):
    tile_count = home_tiles.shape[1]
    near_atoms = jnp.take(home_tiles, near_ids, axis=1)
    far_atoms = jnp.take(candidate, far_ids, axis=1)
    delta_x = near_atoms[0][:, :, None] - far_atoms[0][:, None, :]
    delta_y = near_atoms[1][:, :, None] - far_atoms[1][:, None, :]
    delta_z = near_atoms[2][:, :, None] - far_atoms[2][:, None, :]
    dist_sq = delta_x * delta_x + delta_y * delta_y + delta_z * delta_z
    spacing = jnp.sqrt(dist_sq + soften * soften)
    inv_width = lax.rsqrt(near_atoms[5][:, :, None] ** 2 + far_atoms[5][:, None, :] ** 2)
    taper = jnp.square(jnp.maximum(1.0 - dist_sq / (cutoff * cutoff), 0.0))
    kernel = jax.scipy.special.erf(inv_width * spacing) / spacing * taper
    diagonal = jnp.arange(TILE, dtype=jnp.int32)[:, None] == jnp.arange(TILE, dtype=jnp.int32)[None, :]
    self_pairs = (far_ids == near_ids)[:, None, None] & diagonal[None]
    kept_pairs = in_range[:, None, None] & jnp.logical_not(self_pairs)
    kernel = jnp.where(kept_pairs, kernel, 0.0)
    pair_fields = jnp.einsum('pij,cpj->cpi', kernel, far_atoms[3:5], precision=lax.Precision.HIGHEST)
    chosen = (near_ids[:, None] == jnp.arange(tile_count, dtype=jnp.int32)[None, :]).astype(pair_fields.dtype)
    return jnp.einsum('pt,cpi->cti', chosen, pair_fields, precision=lax.Precision.HIGHEST)

def sweep_all(home_tiles, candidate, near_list, far_list, pair_total):
    extra = -PAIR_CAP % pair_group
    near_pad = jnp.concatenate([near_list, jnp.zeros((extra,), jnp.int32)]).reshape(-1, pair_group)
    far_pad = jnp.concatenate([far_list, jnp.zeros((extra,), jnp.int32)]).reshape(-1, pair_group)
    index_pad = jnp.arange(PAIR_CAP + extra, dtype=jnp.int32).reshape(-1, pair_group)

    def advance(running, block):
        near_ids, far_ids, indices = block
        return (running + pair_terms(home_tiles, candidate, near_ids, far_ids, indices < pair_total), None)
    start_total = jnp.zeros((2, home_tiles.shape[1], TILE), jnp.float32)
    running, unused = lax.scan(advance, start_total, (near_pad, far_pad, index_pad))
    return running

def reference(positions, aux, aux_prev, resid, types, pair_tiles, pair_cands, pair_count, owner_tile, electroneg, hardness, widths):
    tile_count = TX * TY * TZ
    atom_count = tile_count * TILE
    negativity = lookup(electroneg, types.reshape(-1)).reshape(types.shape)
    hardness_row = lookup(hardness, types.reshape(-1)).reshape(types.shape)
    radius = lookup(widths, types.reshape(-1)).reshape(types.shape)
    packed = jnp.concatenate([positions, aux[:, :, None], resid[:, :, None], radius[:, :, None]], axis=2)

    def one_device(index):
        brick_of = index // PLANES
        plane_of = index % PLANES
        below = (brick_of - 1) % BRICKS
        above = (brick_of + 1) % BRICKS
        left_side = (plane_of - 1) % PLANES
        right_side = (plane_of + 1) % PLANES
        blocks = [packed[brick_of, plane_of], packed[below, plane_of], packed[above, plane_of], packed[brick_of, left_side], packed[brick_of, right_side]]
        candidate = candidates(blocks, tile_count)
        home_tiles = blocks[0].reshape(6, tile_count, TILE)
        return sweep_all(home_tiles, candidate, pair_tiles[brick_of, plane_of], pair_cands[brick_of, plane_of], pair_count[brick_of, plane_of])
    fields = lax.map(one_device, jnp.arange(BRICKS * PLANES, dtype=jnp.int32))
    fields = fields.reshape(BRICKS, PLANES, 2, atom_count)
    aux_field = fields[:, :, 0]
    resid_field = fields[:, :, 1]
    field = negativity + aux_field + resid_field
    potential_level = (jnp.sum(aux) + jnp.sum(field / hardness_row)) / jnp.sum(1.0 / hardness_row)
    charges = (potential_level - field) / hardness_row
    group_tiles = PLANES * tile_count
    both = jnp.stack([aux, charges]).reshape(2, BRICKS, group_tiles, TILE)
    target = owner_tile.reshape(BRICKS, group_tiles)
    rows = jnp.arange(BRICKS, dtype=jnp.int32)[:, None]
    placed = jnp.zeros_like(both).at[:, rows, target].set(both)
    previous = aux_prev.reshape(BRICKS, group_tiles, TILE)
    next_aux = 2.0 * placed[0] - previous + kappa * (placed[1] - placed[0])
    return (charges, next_aux.reshape(BRICKS, PLANES, atom_count), resid_field)
```

```python
import functools

import jax
import jax.numpy as jnp
from jax import lax
from jax.experimental import pallas as pl
from jax.experimental.pallas import tpu as pltpu
from jax.sharding import PartitionSpec as P

F32 = jnp.float32
BF = jnp.bfloat16
HI = lax.Precision.HIGHEST
MESH = pl.DeviceIdType.MESH
kappa = 1.86

PB = 12
SB = 13
NT = 320


def sort_kernel(tiles, cands, count, codes, total, selfs, tr, cr):
    n = tiles.shape[1]
    one = lax.broadcasted_iota(jnp.int32, (1, 128), 1)
    tr[...] = jnp.full((128, 128), 64.0, F32)
    cr[...] = jnp.zeros((16, 128), F32)
    for j in range(PB):
        w = min(128, n - 128 * j)
        tr[j : j + 1, :w] = tiles[:, 128 * j : 128 * j + w].astype(F32)
        cr[j : j + 1, :w] = cands[:, 128 * j : 128 * j + w].astype(F32)
    prow = lax.broadcasted_iota(jnp.int32, (16, 128), 0) * 128 + lax.broadcasted_iota(jnp.int32, (16, 128), 1)
    used = prow < count[0, 0]
    t = jnp.where(used, tr[:16], 64.0)
    c = jnp.where(used, cr[...], 0.0)
    tr[:16] = t
    tcol = tr[...].T
    lane = lax.broadcasted_iota(jnp.int32, (128, 128), 1)
    rowi = lax.broadcasted_iota(jnp.int32, (128, 128), 0)
    lanef = lane.astype(F32)
    before = jnp.where(lane < rowi, 1.0, 0.0).astype(BF)
    hot = [tcol[:, j : j + 1] == lanef for j in range(PB)]
    hotf = [jnp.where(h, 1.0, 0.0) for h in hot]
    sums = [jnp.sum(h, axis=0, keepdims=True) for h in hotf]
    counts = sum(sums)
    counts = jnp.where(one < 64, counts, 0.0)
    half = jnp.floor((counts + 1.0) * 0.5)
    starts = 2.0 * jnp.dot(jnp.broadcast_to(half, (8, 128)), jnp.where(rowi < lane, 1.0, 0.0), precision=HI, preferred_element_type=F32)[:1]
    starts = jnp.where(one < 64, starts, 8192.0)
    total[...] = jnp.broadcast_to(jnp.sum(half, axis=1, keepdims=True), (8, 128)).astype(jnp.int32)
    out = jnp.zeros((8, SB * 128), F32)
    slot = lax.broadcasted_iota(jnp.int32, (128, SB * 128), 1).astype(F32)
    selfrow = jnp.zeros((1, 128), F32)
    e = float(NT) - c
    e = jnp.where(used, e, 0.0)
    ehi = jnp.floor(e * 0.5)
    elo = e - 2.0 * ehi
    same = jnp.where(t == c, 1.0, 0.0)
    r8 = lax.broadcasted_iota(jnp.int32, (8, 128), 0)
    for j in range(PB):
        rank = jnp.dot(before, hotf[j].astype(BF), preferred_element_type=F32)
        pos = jnp.sum(jnp.where(hot[j], rank + starts, 0.0), axis=1, keepdims=True)
        starts = starts + sums[j]
        vals = jnp.where(r8 == 0, ehi[j : j + 1], jnp.where(r8 == 1, elo[j : j + 1], jnp.where(r8 == 2, t[j : j + 1], same[j : j + 1])))
        put = jnp.where(pos == slot, 1.0, 0.0).astype(BF)
        out = out + jnp.dot(vals.astype(BF), put, preferred_element_type=F32)
        selfrow = selfrow + jnp.dot(vals.astype(BF), hotf[j].astype(BF), preferred_element_type=F32)[3:4]
    code = out[2:3] * 512.0 + (float(NT) - (2.0 * out[0:1] + out[1:2]))
    codes[...] = code.astype(jnp.int32)
    selfs[...] = jnp.broadcast_to(selfrow, (8, 128))


def sort_call(tiles, cands, count):
    vm = pl.BlockSpec(memory_space=pltpu.VMEM)
    return pl.pallas_call(
        sort_kernel,
        out_shape=[jax.ShapeDtypeStruct((1, SB * 128), jnp.int32), jax.ShapeDtypeStruct((8, 128), jnp.int32), jax.ShapeDtypeStruct((8, 128), F32)],
        in_specs=[vm, vm, pl.BlockSpec(memory_space=pltpu.SMEM)],
        out_specs=[vm, vm, vm],
        scratch_shapes=[pltpu.VMEM((128, 128), F32), pltpu.VMEM((16, 128), F32)],
        name="pairs_sort",
    )(tiles, cands, count)

NR = 160
UN = 8


def pair_kernel(codes, total, widths, chi, hard, selfs, own, halo, fe, rf, G, C, HB, CH, acc, FR):
    lane = lax.broadcasted_iota(jnp.int32, (8, 128), 1)
    row = lax.broadcasted_iota(jnp.int32, (8, 128), 0)
    low = lane < 64
    for b in range(5):
        at = [own[c] if b == 0 else halo[b - 1, c] for c in range(6)]
        if b in (1, 2):
            at[0] = at[0] + (-16.0 if b == 1 else 16.0)
        if b in (3, 4):
            at[1] = at[1] + (-32.0 if b == 3 else 32.0)
        s = jnp.zeros((32, 128), F32)
        for t in range(8):
            s = jnp.where(at[5] == float(t), widths[t], s)
        for c, x in enumerate((at[0] * 0.1, at[1] * 0.1, at[2] * 0.1, at[3] * 0.1, at[4] * 0.1, s * s * 0.01)):
            G[pl.ds(c * NR + b * 32, 32), :] = x
    G[pl.ds(6 * NR, 2 * NR), :] = jnp.zeros((2 * NR, 128), F32)

    def halves(x):
        y = pltpu.roll(x, 64, 1)
        return jnp.where(low, x, y), jnp.where(low, y, x)

    def prep(g, carry):
        c0, c1 = halves(G[pl.ds(g, 8, stride=NR), :])
        C[g * 2] = c0
        C[g * 2 + 1] = c1
        return carry

    lax.fori_loop(0, NR, prep, 0, unroll=8)
    C[NT] = jnp.where((row == 3) | (row == 4), 0.0, C[0])

    def prep_home(r, carry):
        v = G[pl.ds(r, 8, stride=NR), :]
        x = v[:, 0:1]
        y = v[:, 64:65]
        cen = jnp.where(low, jnp.broadcast_to(x, (8, 128)), jnp.broadcast_to(y, (8, 128)))
        cen = jnp.where(row < 3, cen, 0.0)
        a = v - cen
        n = jnp.sum(jnp.where(row < 3, a * a, 0.0), axis=0, keepdims=True) + 0.0025
        f = jnp.where(row < 3, -2.0 * a, jnp.where(row == 3, n, jnp.where(row == 5, a, 0.0)))
        c0, c1 = halves(cen)
        CH[r * 2] = c0
        CH[r * 2 + 1] = c1
        FR[pl.ds(pl.multiple_of(r * 8, 8), 8), :] = f
        return carry

    lax.fori_loop(0, 32, prep_home, 0, unroll=4)
    for g in range(2):
        t = FR[pl.ds(128 * g, 128), :].T
        for r in range(16):
            for k, col in enumerate((0, 1, 2, 3, 5)):
                w = jnp.broadcast_to(t[:, 8 * r + col : 8 * r + col + 1], (128, 128))
                HB[k, 32 * g + 2 * r] = w[:64]
                HB[k, 32 * g + 2 * r + 1] = w[64:]
    acc[...] = jnp.zeros_like(acc)

    def step(i, carry):
        for u in range(UN):
            k1 = codes[0, 2 * UN * i + 2 * u]
            k2 = codes[0, 2 * UN * i + 2 * u + 1]
            h = lax.shift_right_logical(k1, 9)
            v = jnp.where(low, C[k1 & 511], C[k2 & 511]) - CH[h]
            n = jnp.sum(jnp.where(row < 3, v * v, 0.0), axis=0, keepdims=True)
            xs = [jnp.broadcast_to(v[k : k + 1], (8, 128)) for k in range(6)]
            n = jnp.broadcast_to(n, (8, 128))
            for q in range(8):
                rows = pl.ds(8 * q, 8)
                d = (HB[3, h, rows] + n) + HB[0, h, rows] * xs[0] + HB[1, h, rows] * xs[1] + HB[2, h, rows] * xs[2]
                w = lax.rsqrt(HB[4, h, rows] + xs[5])
                r = lax.rsqrt(d)
                e = lax.erf(d * r * w)
                m = jnp.maximum(1.0025 - d, 0.0)
                kk = (e * r) * (m * m)
                acc[0, h, rows] = acc[0, h, rows] + kk * xs[3]
                acc[1, h, rows] = acc[1, h, rows] + kk * xs[4]
        return carry

    lax.fori_loop(0, lax.div(total[0, 0] + UN - 1, UN), step, 0)
    def finish(r, carry):
        for f, ref in enumerate((fe, rf)):
            ref[pl.ds(r, 1), :] = jnp.sum(acc[f, pl.ds(2 * r, 2)].reshape(128, 128).T, axis=0, keepdims=True)
        return carry

    lax.fori_loop(0, 32, finish, 0, unroll=4)
    lane32 = lax.broadcasted_iota(jnp.int32, (32, 128), 1)
    row32 = lax.broadcasted_iota(jnp.int32, (32, 128), 0)
    n = jnp.broadcast_to(selfs[0:1], (32, 128))
    even = jnp.sum(jnp.where(lane32 == 2 * row32, n, 0.0), axis=1, keepdims=True)
    odd = jnp.sum(jnp.where(lane32 == 2 * row32 + 1, n, 0.0), axis=1, keepdims=True)
    times = jnp.where(lane32 < 64, even, odd)
    s2 = jnp.zeros((32, 128), F32)
    ch = jnp.zeros((32, 128), F32)
    eta = jnp.zeros((32, 128), F32)
    for t in range(8):
        hit = own[5] == float(t)
        s2 = jnp.where(hit, widths[t] * widths[t], s2)
        ch = jnp.where(hit, chi[t], ch)
        eta = jnp.where(hit, hard[t], eta)
    itself = times * (2.0 * lax.erf(0.5 * lax.rsqrt(s2 + s2)))
    residual = rf[...] - itself * own[4]
    field = ch + (fe[...] - itself * own[3]) + residual
    rf[...] = residual
    fe[...] = field / eta


def pair_call(codes, total, widths, chi, hard, selfs, own, halo):
    sm = pl.BlockSpec(memory_space=pltpu.SMEM)
    vm = pl.BlockSpec(memory_space=pltpu.VMEM)
    return pl.pallas_call(
        pair_kernel,
        out_shape=[jax.ShapeDtypeStruct((32, 128), F32)] * 2,
        in_specs=[sm] * 5 + [vm] * 3,
        out_specs=[vm, vm],
        scratch_shapes=[
            pltpu.VMEM((8 * NR, 128), F32),
            pltpu.VMEM((NT + 1, 8, 128), F32),
            pltpu.VMEM((5, 64, 64, 128), F32),
            pltpu.VMEM((64, 8, 128), F32),
            pltpu.VMEM((2, 64, 64, 128), F32),
            pltpu.VMEM((256, 128), F32),
        ],
        compiler_params=pltpu.CompilerParams(vmem_limit_bytes=40 * 2**20),
        name="pairs",
    )(codes, total, widths, chi, hard, selfs, own, halo)


def exchange_kernel(pos, aux, resid, types, owner, hard, own, halo, early, send, recv):
    nb, npl = lax.axis_size("brick"), lax.axis_size("plane")
    b, p = lax.axis_index("brick"), lax.axis_index("plane")
    below, above = lax.rem(b + nb - 1, nb), lax.rem(b + 1, nb)
    barrier = pltpu.get_barrier_semaphore()
    mates = [lax.rem(p + k, npl) for k in range(1, npl)]
    for d in [(below, p), (above, p)] + [(b, q) for q in mates]:
        pl.semaphore_signal(barrier, inc=1, device_id=d, device_id_type=MESH)
    for r in range(32):
        at = pl.ds(128 * r, 128)
        for c in range(3):
            own[c, r : r + 1, :] = pos[c : c + 1, at]
        own[3, r : r + 1, :] = aux[:, at]
        own[4, r : r + 1, :] = resid[:, at]
        own[5, r : r + 1, :] = types[:, at].astype(F32)
    inverse = jnp.zeros((32, 128), F32)
    ty = own[5]
    for t in range(8):
        inverse = jnp.where(ty == float(t), 1.0 / jnp.full((32, 128), hard[t], F32), inverse)
    early[p, 0] = own[3]
    early[p, 1] = inverse
    src = lax.broadcasted_iota(jnp.int32, (64, 128), 0)
    lane = lax.broadcasted_iota(jnp.int32, (64, 128), 1) - 32 * p
    inside = (lane >= 0) & (lane < 32)
    ids = jnp.broadcast_to(owner[...].astype(F32), (8, 64))
    evens = jnp.dot(ids, jnp.where(inside & (src == 2 * lane), 1.0, 0.0), precision=HI, preferred_element_type=F32)
    odds = jnp.dot(ids, jnp.where(inside & (src == 2 * lane + 1), 1.0, 0.0), precision=HI, preferred_element_type=F32)
    early[p, 2, 0:8, :] = evens
    early[p, 2, 8:16, :] = odds
    early[p, 2, 16:32, :] = jnp.zeros((16, 128), F32)
    pl.semaphore_wait(barrier, 1 + npl)

    def copy(s, d, k, to):
        return pltpu.make_async_remote_copy(
            src_ref=s, dst_ref=d, send_sem=send.at[k], recv_sem=recv.at[k], device_id=to, device_id_type=MESH
        )

    left, right = lax.rem(p + npl - 1, npl), lax.rem(p + 1, npl)
    copies = [
        copy(own, halo.at[2], 2, (b, right)),
        copy(own, halo.at[3], 3, (b, left)),
        copy(own, halo.at[0], 0, (above, p)),
        copy(own, halo.at[1], 1, (below, p)),
    ] + [copy(early.at[p], early.at[p], 4 + k, (b, q)) for k, q in enumerate(mates)]
    for c in copies:
        c.start()
    for c in copies:
        c.wait()


def exchange(pos, aux, resid, types, owner, hard):
    vm = pl.BlockSpec(memory_space=pltpu.VMEM)
    return pl.pallas_call(
        exchange_kernel,
        out_shape=[
            jax.ShapeDtypeStruct((6, 32, 128), F32),
            jax.ShapeDtypeStruct((4, 6, 32, 128), F32),
            jax.ShapeDtypeStruct((4, 3, 32, 128), F32),
        ],
        in_specs=[vm] * 5 + [pl.BlockSpec(memory_space=pltpu.SMEM)],
        out_specs=[vm] * 3,
        scratch_shapes=[pltpu.SemaphoreType.DMA((7,)), pltpu.SemaphoreType.DMA((7,))],
        compiler_params=pltpu.CompilerParams(collective_id=0, has_side_effects=True),
        name="exchange",
    )(pos, aux, resid, types, owner, hard)


LOW = 8


def level_kernel(fe, early, prev, charges, nxt, got, near, far, s1, r1, s2, r2, s3, r3):
    nb, npl = lax.axis_size("brick"), lax.axis_size("plane")
    high = nb // LOW
    b, p = lax.axis_index("brick"), lax.axis_index("plane")
    bl, bh = lax.rem(b, LOW), lax.div(b, LOW)
    mates = [lax.rem(p + k, npl) for k in range(1, npl)]
    lows = [lax.rem(bl + k, LOW) for k in range(1, LOW)]
    highs = [lax.rem(bh + k, high) for k in range(1, high)]
    barrier = pltpu.get_barrier_semaphore()
    for q in mates:
        pl.semaphore_signal(barrier, inc=1, device_id=(b, q), device_id_type=MESH)
    for q in lows:
        pl.semaphore_signal(barrier, inc=1, device_id=(bh * LOW + q, p), device_id_type=MESH)
    for q in highs:
        pl.semaphore_signal(barrier, inc=1, device_id=(q * LOW + bl, p), device_id_type=MESH)
    got[p] = fe[...]
    pl.semaphore_wait(barrier, npl - 1 + LOW - 1 + high - 1)

    def copy(s, d, ss, rs, to):
        return pltpu.make_async_remote_copy(
            src_ref=s, dst_ref=d, send_sem=ss, recv_sem=rs, device_id=to, device_id_type=MESH
        )

    first = [copy(got.at[p], got.at[p], s1.at[k], r1.at[k], (b, q)) for k, q in enumerate(mates)]
    for c in first:
        c.start()
    evens = sum(early[q, 2, 0:1, :] for q in range(4))
    odds = sum(early[q, 2, 8:9, :] for q in range(4))
    slot = (64 * p + 2 * lax.broadcasted_iota(jnp.int32, (32, 128), 0)).astype(F32)
    place = jnp.concatenate(
        [
            jnp.where(evens == slot, 1.0, 0.0),
            jnp.where(odds == slot + 1.0, 1.0, 0.0),
            jnp.where(evens == slot + 1.0, 1.0, 0.0),
            jnp.where(odds == slot, 1.0, 0.0),
        ],
        axis=0,
    )
    low = lax.broadcasted_iota(jnp.int32, (32, 128), 1) < 64

    def placed(x):
        y = jnp.dot(place, x, precision=HI, preferred_element_type=F32)
        return jnp.where(low, y[0:32], y[32:64]) + pltpu.roll(jnp.where(low, y[64:96], y[96:128]), 64, 1)

    aux = placed(early[:, 0].reshape(128, 128))
    inverse = placed(early[:, 1].reshape(128, 128))

    def fold(x):
        s = x[0:8]
        for k in range(1, 16):
            s = s + x[8 * k : 8 * k + 8]
        return s[0:4] + s[4:8]

    sum_aux = fold(early[:, 0].reshape(128, 128))
    sum_inv = fold(early[:, 1].reshape(128, 128))
    for c in first:
        c.wait()
    fes = got[...].reshape(128, 128)
    near[bl] = jnp.concatenate([sum_aux + fold(fes), sum_inv], axis=0)
    second = [copy(near.at[bl], near.at[bl], s2.at[k], r2.at[k], (bh * LOW + q, p)) for k, q in enumerate(lows)]
    for c in second:
        c.start()
    moved = placed(fes)
    for c in second:
        c.wait()
    total = near[0]
    for k in range(1, LOW):
        total = total + near[k]
    far[bh] = total
    third = [copy(far.at[bh], far.at[bh], s3.at[k], r3.at[k], (q * LOW + bl, p)) for k, q in enumerate(highs)]
    for c in third:
        c.start()
    for c in third:
        c.wait()
    total = far[0]
    for k in range(1, 16):
        total = total + far[k]
    top = jnp.sum(jnp.sum(total[0:4], axis=1, keepdims=True), axis=0, keepdims=True)
    bottom = jnp.sum(jnp.sum(total[4:8], axis=1, keepdims=True), axis=0, keepdims=True)
    level = jnp.broadcast_to(top / bottom, (32, 128))
    charges[...] = level * early[p, 1] - fe[...]
    nxt[...] = 2.0 * aux - prev[...] + kappa * (level * inverse - moved - aux)


def finish(fe, early, prev):
    vm = pl.BlockSpec(memory_space=pltpu.VMEM)
    dma = pltpu.SemaphoreType.DMA
    return pl.pallas_call(
        level_kernel,
        out_shape=[jax.ShapeDtypeStruct((32, 128), F32)] * 2,
        in_specs=[vm] * 3,
        out_specs=[vm] * 2,
        scratch_shapes=[
            pltpu.VMEM((4, 32, 128), F32),
            pltpu.VMEM((LOW, 8, 128), F32),
            pltpu.VMEM((16, 8, 128), F32),
            dma((3,)), dma((3,)), dma((7,)), dma((7,)), dma((15,)), dma((15,)),
        ],
        compiler_params=pltpu.CompilerParams(collective_id=1, has_side_effects=True),
        name="level",
    )(fe, early, prev)


def on_device(positions, aux, aux_prev, resid, types, pair_tiles, pair_cands, pair_count, owner_tile, electroneg, hardness, widths):
    own, halo, early = exchange(
        positions.reshape(3, -1), aux.reshape(1, -1), resid.reshape(1, -1), types.reshape(1, -1), owner_tile.reshape(1, -1), hardness
    )
    codes, total, selfs = sort_call(pair_tiles.reshape(1, -1), pair_cands.reshape(1, -1), pair_count)
    fe, rf = pair_call(codes, total, widths, electroneg, hardness, selfs, own, halo)
    charges, nxt = finish(fe, early, aux_prev.reshape(32, 128))
    return charges.reshape(aux.shape), nxt.reshape(aux.shape), rf.reshape(aux.shape)


def solution(mesh):
    s4, s3, s2 = P("brick", "plane", None, None), P("brick", "plane", None), P("brick", "plane")
    return jax.shard_map(
        on_device,
        mesh=mesh,
        in_specs=(s4, s3, s3, s3, s3, s3, s3, s2, s3, P(), P(), P()),
        out_specs=(s3, s3, s3),
        check_vma=False,
    )
```

```python
import functools

import jax
import jax.numpy as jnp
from jax import lax
from jax.experimental import pallas as pl
from jax.experimental.pallas import tpu as pltpu
from jax.sharding import PartitionSpec as P

F32 = jnp.float32
BF = jnp.bfloat16
HI = lax.Precision.HIGHEST
MESH = pl.DeviceIdType.MESH
kappa = 1.86

PB = 12
SB = 13
NT = 320


def order_pairs(tiles, cands, count, codes, tr, cr):
    n = tiles.shape[1]
    one = lax.broadcasted_iota(jnp.int32, (1, 128), 1)
    tr[...] = jnp.full((128, 128), 64.0, F32)
    cr[...] = jnp.zeros((16, 128), F32)
    for j in range(PB):
        w = min(128, n - 128 * j)
        tr[j : j + 1, :w] = tiles[:, 128 * j : 128 * j + w].astype(F32)
        cr[j : j + 1, :w] = cands[:, 128 * j : 128 * j + w].astype(F32)
    prow = lax.broadcasted_iota(jnp.int32, (16, 128), 0) * 128 + lax.broadcasted_iota(jnp.int32, (16, 128), 1)
    used = prow < count[0, 0]
    t = jnp.where(used, tr[:16], 64.0)
    c = jnp.where(used, cr[...], 0.0)
    tr[:16] = t
    tcol = tr[...].T
    lane = lax.broadcasted_iota(jnp.int32, (128, 128), 1)
    rowi = lax.broadcasted_iota(jnp.int32, (128, 128), 0)
    lanef = lane.astype(F32)
    before = jnp.where(lane < rowi, 1.0, 0.0).astype(BF)
    hot = [tcol[:, j : j + 1] == lanef for j in range(PB)]
    hotf = [jnp.where(h, 1.0, 0.0) for h in hot]
    sums = [jnp.sum(h, axis=0, keepdims=True) for h in hotf]
    counts = sum(sums)
    counts = jnp.where(one < 64, counts, 0.0)
    half = jnp.floor((counts + 1.0) * 0.5)
    starts = 2.0 * jnp.dot(jnp.broadcast_to(half, (8, 128)), jnp.where(rowi < lane, 1.0, 0.0), precision=HI, preferred_element_type=F32)[:1]
    starts = jnp.where(one < 64, starts, 8192.0)
    codes[:, SB * 128 :] = jnp.broadcast_to(jnp.sum(half, axis=1, keepdims=True), (1, 128)).astype(jnp.int32)
    out = jnp.zeros((8, SB * 128), F32)
    slot = lax.broadcasted_iota(jnp.int32, (128, SB * 128), 1).astype(F32)
    selfrow = jnp.zeros((1, 128), F32)
    e = float(NT) - c
    e = jnp.where(used, e, 0.0)
    ehi = jnp.floor(e * 0.5)
    elo = e - 2.0 * ehi
    same = jnp.where(t == c, 1.0, 0.0)
    r8 = lax.broadcasted_iota(jnp.int32, (8, 128), 0)
    for j in range(PB):
        rank = jnp.dot(before, hotf[j].astype(BF), preferred_element_type=F32)
        pos = jnp.sum(jnp.where(hot[j], rank + starts, 0.0), axis=1, keepdims=True)
        starts = starts + sums[j]
        vals = jnp.where(r8 == 0, ehi[j : j + 1], jnp.where(r8 == 1, elo[j : j + 1], jnp.where(r8 == 2, t[j : j + 1], same[j : j + 1])))
        put = jnp.where(pos == slot, 1.0, 0.0).astype(BF)
        out = out + jnp.dot(vals.astype(BF), put, preferred_element_type=F32)
        selfrow = selfrow + jnp.dot(vals.astype(BF), hotf[j].astype(BF), preferred_element_type=F32)[3:4]
    code = out[2:3] * 512.0 + (float(NT) - (2.0 * out[0:1] + out[1:2]))
    codes[:, : SB * 128] = code.astype(jnp.int32)
    lane32 = lax.broadcasted_iota(jnp.int32, (32, 128), 1)
    row32 = lax.broadcasted_iota(jnp.int32, (32, 128), 0)
    n = jnp.broadcast_to(selfrow, (32, 128))
    even = jnp.sum(jnp.where(lane32 == 2 * row32, n, 0.0), axis=1, keepdims=True)
    odd = jnp.sum(jnp.where(lane32 == 2 * row32 + 1, n, 0.0), axis=1, keepdims=True)
    return jnp.where(lane32 < 64, even, odd)


NR = 160
UN = 8


def pair_kernel(codes_h, widths, chi, hard, own_h, halo_h, fe, rf, codes, own, halo, sem, G, C, HB, CH, acc, FR):
    loads = [
        pltpu.make_async_copy(s, d, sem.at[k])
        for k, (s, d) in enumerate(((own_h, own), (halo_h, halo), (codes_h, codes)))
    ]
    for c in loads:
        c.start()
    lane = lax.broadcasted_iota(jnp.int32, (8, 128), 1)
    row = lax.broadcasted_iota(jnp.int32, (8, 128), 0)
    low = lane < 64
    for c in loads:
        c.wait()
    for b in range(5):
        at = [own[c] if b == 0 else halo[b - 1, c] for c in range(6)]
        if b in (1, 2):
            at[0] = at[0] + (-16.0 if b == 1 else 16.0)
        if b in (3, 4):
            at[1] = at[1] + (-32.0 if b == 3 else 32.0)
        s = jnp.zeros((32, 128), F32)
        for t in range(8):
            s = jnp.where(at[5] == float(t), widths[t], s)
        for c, x in enumerate((at[0] * 0.1, at[1] * 0.1, at[2] * 0.1, at[3] * 0.1, at[4] * 0.1, s * s * 0.01)):
            G[pl.ds(c * NR + b * 32, 32), :] = x
    G[pl.ds(6 * NR, 2 * NR), :] = jnp.zeros((2 * NR, 128), F32)

    def halves(x):
        y = pltpu.roll(x, 64, 1)
        return jnp.where(low, x, y), jnp.where(low, y, x)

    def prep(g, carry):
        c0, c1 = halves(G[pl.ds(g, 8, stride=NR), :])
        C[g * 2] = c0
        C[g * 2 + 1] = c1
        return carry

    lax.fori_loop(0, NR, prep, 0, unroll=8)
    C[NT] = jnp.where((row == 3) | (row == 4), 0.0, C[0])

    def prep_home(r, carry):
        v = G[pl.ds(r, 8, stride=NR), :]
        x = v[:, 0:1]
        y = v[:, 64:65]
        cen = jnp.where(low, jnp.broadcast_to(x, (8, 128)), jnp.broadcast_to(y, (8, 128)))
        cen = jnp.where(row < 3, cen, 0.0)
        a = v - cen
        n = jnp.sum(jnp.where(row < 3, a * a, 0.0), axis=0, keepdims=True) + 0.0025
        f = jnp.where(row < 3, -2.0 * a, jnp.where(row == 3, n, jnp.where(row == 5, a, 0.0)))
        c0, c1 = halves(cen)
        CH[r * 2] = c0
        CH[r * 2 + 1] = c1
        FR[pl.ds(pl.multiple_of(r * 8, 8), 8), :] = f
        acc[0, pl.ds(2 * r, 2)] = jnp.zeros((2, 64, 128), F32)
        acc[1, pl.ds(2 * r, 2)] = jnp.zeros((2, 64, 128), F32)
        return carry

    lax.fori_loop(0, 32, prep_home, 0, unroll=4)
    for g in range(2):
        t = FR[pl.ds(128 * g, 128), :].T
        for r in range(16):
            for k, col in enumerate((0, 1, 2, 3, 5)):
                w = jnp.broadcast_to(t[:, 8 * r + col : 8 * r + col + 1], (128, 128))
                HB[k, 32 * g + 2 * r] = w[:64]
                HB[k, 32 * g + 2 * r + 1] = w[64:]

    def step(i, carry):
        for u in range(UN):
            k1 = codes[0, 2 * UN * i + 2 * u]
            k2 = codes[0, 2 * UN * i + 2 * u + 1]
            h = lax.shift_right_logical(k1, 9)
            v = jnp.where(low, C[k1 & 511], C[k2 & 511]) - CH[h]
            n = jnp.sum(jnp.where(row < 3, v * v, 0.0), axis=0, keepdims=True)
            xs = [jnp.broadcast_to(v[k : k + 1], (8, 128)) for k in range(6)]
            n = jnp.broadcast_to(n, (8, 128))
            for q in range(8):
                rows = pl.ds(8 * q, 8)
                d = (HB[3, h, rows] + n) + HB[0, h, rows] * xs[0] + HB[1, h, rows] * xs[1] + HB[2, h, rows] * xs[2]
                w = lax.rsqrt(HB[4, h, rows] + xs[5])
                r = lax.rsqrt(d)
                e = lax.erf(d * r * w)
                m = jnp.maximum(1.0025 - d, 0.0)
                kk = (e * r) * (m * m)
                acc[0, h, rows] = acc[0, h, rows] + kk * xs[3]
                acc[1, h, rows] = acc[1, h, rows] + kk * xs[4]
        return carry

    lax.fori_loop(0, lax.div(codes[0, 1664] + UN - 1, UN), step, 0)
    def finish(r, carry):
        for f, ref in enumerate((fe, rf)):
            ref[pl.ds(r, 1), :] = jnp.sum(acc[f, pl.ds(2 * r, 2)].reshape(128, 128).T, axis=0, keepdims=True)
        return carry

    lax.fori_loop(0, 32, finish, 0, unroll=4)
    s2 = jnp.zeros((32, 128), F32)
    ch = jnp.zeros((32, 128), F32)
    eta = jnp.zeros((32, 128), F32)
    for t in range(8):
        hit = own[5] == float(t)
        s2 = jnp.where(hit, widths[t] * widths[t], s2)
        ch = jnp.where(hit, chi[t], ch)
        eta = jnp.where(hit, hard[t], eta)
    itself = own[6] * (2.0 * lax.erf(0.5 * lax.rsqrt(s2 + s2)))
    residual = rf[...] - itself * own[4]
    field = ch + (fe[...] - itself * own[3]) + residual
    rf[...] = residual
    fe[...] = field / eta


def pair_call(codes, widths, chi, hard, own, halo):
    sm = pl.BlockSpec(memory_space=pltpu.SMEM)
    vm = pl.BlockSpec(memory_space=pltpu.VMEM)
    hbm = pl.BlockSpec(memory_space=pl.ANY)
    return pl.pallas_call(
        pair_kernel,
        out_shape=[jax.ShapeDtypeStruct((32, 128), F32)] * 2,
        in_specs=[hbm] + [sm] * 3 + [hbm] * 2,
        out_specs=[vm, vm],
        scratch_shapes=[
            pltpu.SMEM(codes.shape, jnp.int32),
            pltpu.VMEM(own.shape, F32),
            pltpu.VMEM(halo.shape, F32),
            pltpu.SemaphoreType.DMA((3,)),
            pltpu.VMEM((8 * NR, 128), F32),
            pltpu.VMEM((NT + 1, 8, 128), F32),
            pltpu.VMEM((5, 64, 64, 128), F32),
            pltpu.VMEM((64, 8, 128), F32),
            pltpu.VMEM((2, 64, 64, 128), F32),
            pltpu.VMEM((256, 128), F32),
        ],
        compiler_params=pltpu.CompilerParams(vmem_limit_bytes=60 * 2**20),
        name="pairs",
    )(codes, widths, chi, hard, own, halo)


def exchange_kernel(
    pos, aux, resid, types, owner, tiles, cands, hard, count, own, halo, early, codes, send, recv, tr, cr
):
    nb, npl = lax.axis_size("brick"), lax.axis_size("plane")
    b, p = lax.axis_index("brick"), lax.axis_index("plane")
    below, above = lax.rem(b + nb - 1, nb), lax.rem(b + 1, nb)
    barrier = pltpu.get_barrier_semaphore()
    mates = [lax.rem(p + k, npl) for k in range(1, npl)]
    for d in [(below, p), (above, p)] + [(b, q) for q in mates]:
        pl.semaphore_signal(barrier, inc=1, device_id=d, device_id_type=MESH)
    for c in range(3):
        own[c] = pos[pl.ds(32 * c, 32), :]
    own[3] = aux[...]
    own[4] = resid[...]
    ty = types[...].astype(F32)
    own[5] = ty
    inverse = jnp.zeros((32, 128), F32)
    for t in range(8):
        inverse = jnp.where(ty == float(t), 1.0 / jnp.full((32, 128), hard[t], F32), inverse)
    early[p, 0:32, :] = aux[...]
    early[p, 32:64, :] = inverse
    src = lax.broadcasted_iota(jnp.int32, (64, 128), 0)
    lane = lax.broadcasted_iota(jnp.int32, (64, 128), 1) - 32 * p
    inside = (lane >= 0) & (lane < 32)
    ids = jnp.broadcast_to(owner[...].astype(F32), (8, 64))
    evens = jnp.dot(ids, jnp.where(inside & (src == 2 * lane), 1.0, 0.0), precision=HI, preferred_element_type=F32)
    odds = jnp.dot(ids, jnp.where(inside & (src == 2 * lane + 1), 1.0, 0.0), precision=HI, preferred_element_type=F32)
    r8 = lax.broadcasted_iota(jnp.int32, (8, 128), 0)
    early[p, 64:72, :] = jnp.where(r8 == 0, evens, odds)
    pl.semaphore_wait(barrier, 1 + npl)

    def copy(s, d, k, to):
        return pltpu.make_async_remote_copy(
            src_ref=s, dst_ref=d, send_sem=send.at[k], recv_sem=recv.at[k], device_id=to, device_id_type=MESH
        )

    left, right = lax.rem(p + npl - 1, npl), lax.rem(p + 1, npl)
    mine = own.at[pl.ds(0, 6)]
    copies = [
        copy(mine, halo.at[0], 0, (above, p)),
        copy(mine, halo.at[1], 1, (below, p)),
        copy(mine, halo.at[2], 2, (b, right)),
        copy(mine, halo.at[3], 3, (b, left)),
    ] + [copy(early.at[p], early.at[p], 4 + k, (b, q)) for k, q in enumerate(mates)]
    for c in copies:
        c.start()
    own[6] = order_pairs(tiles, cands, count, codes, tr, cr)
    for c in copies:
        c.wait()


def exchange(pos, aux, resid, types, owner, tiles, cands, hard, count):
    vm = pl.BlockSpec(memory_space=pltpu.VMEM)
    return pl.pallas_call(
        exchange_kernel,
        out_shape=[
            jax.ShapeDtypeStruct((7, 32, 128), F32),
            jax.ShapeDtypeStruct((4, 6, 32, 128), F32),
            jax.ShapeDtypeStruct((4, 72, 128), F32),
            jax.ShapeDtypeStruct((1, (SB + 1) * 128), jnp.int32),
        ],
        in_specs=[vm] * 7 + [pl.BlockSpec(memory_space=pltpu.SMEM)] * 2,
        out_specs=[vm] * 4,
        scratch_shapes=[
            pltpu.SemaphoreType.DMA((7,)),
            pltpu.SemaphoreType.DMA((7,)),
            pltpu.VMEM((128, 128), F32),
            pltpu.VMEM((16, 128), F32),
        ],
        compiler_params=pltpu.CompilerParams(collective_id=0, has_side_effects=True),
        name="exchange",
    )(pos, aux, resid, types, owner, tiles, cands, hard, count)


LINE, SHEET = 16, 32


def level_kernel(fe, early, prev, charges, nxt, got, near, far, s1, r1, s2, r2, s3, r3):
    npl = lax.axis_size("plane")
    b, p = lax.axis_index("brick"), lax.axis_index("plane")
    zhi = lax.rem(lax.div(b, 8), 4)
    z = npl * zhi + p
    w = 8 * lax.div(b, 32) + lax.rem(b, 8)

    def line(q):
        return (b + 8 * (lax.div(q, npl) - zhi), lax.rem(q, npl))

    def sheet(q):
        return (32 * lax.div(q, 8) + 8 * zhi + lax.rem(q, 8), p)

    lines = [lax.rem(z + k, LINE) for k in range(1, LINE)]
    sheets = [lax.rem(w + k, SHEET) for k in range(1, SHEET)]
    mates = [lax.rem(p + k, npl) for k in range(1, npl)]
    barrier = pltpu.get_barrier_semaphore()
    for q in lines:
        pl.semaphore_signal(barrier, inc=1, device_id=line(q), device_id_type=MESH)
    for q in sheets:
        pl.semaphore_signal(barrier, inc=1, device_id=sheet(q), device_id_type=MESH)
    got[p] = fe[...]

    def fold(x):
        s = x[0:8] + x[8:16] + x[16:24] + x[24:32]
        return s[0:4] + s[4:8]

    near[w] = jnp.concatenate([fold(early[p, 0:32, :] + fe[...]), fold(early[p, 32:64, :])], axis=0)
    pl.semaphore_wait(barrier, LINE + SHEET - 2)

    def copy(s, d, ss, rs, to):
        return pltpu.make_async_remote_copy(
            src_ref=s, dst_ref=d, send_sem=ss, recv_sem=rs, device_id=to, device_id_type=MESH
        )

    first = [copy(near.at[w], near.at[w], s1.at[k], r1.at[k], sheet(q)) for k, q in enumerate(sheets)]
    for c in first:
        c.start()
    tiles = [copy(got.at[p], got.at[p], s2.at[k], r2.at[k], (b, q)) for k, q in enumerate(mates)]
    for c in tiles:
        c.start()
    evens = early[0, 64:65, :] + early[1, 64:65, :] + early[2, 64:65, :] + early[3, 64:65, :]
    odds = early[0, 65:66, :] + early[1, 65:66, :] + early[2, 65:66, :] + early[3, 65:66, :]
    slot = (64 * p + 2 * lax.broadcasted_iota(jnp.int32, (32, 128), 0)).astype(F32)
    place = jnp.concatenate(
        [
            jnp.where(evens == slot, 1.0, 0.0),
            jnp.where(odds == slot + 1.0, 1.0, 0.0),
            jnp.where(evens == slot + 1.0, 1.0, 0.0),
            jnp.where(odds == slot, 1.0, 0.0),
        ],
        axis=0,
    )
    low = lax.broadcasted_iota(jnp.int32, (32, 128), 1) < 64

    def placed(x):
        y = jnp.dot(place, x, precision=HI, preferred_element_type=F32)
        return jnp.where(low, y[0:32], y[32:64]) + pltpu.roll(jnp.where(low, y[64:96], y[96:128]), 64, 1)

    aux = placed(early[:, 0:32, :].reshape(128, 128))
    inverse = placed(early[:, 32:64, :].reshape(128, 128))
    for c in first:
        c.wait()
    total = near[0]
    for k in range(1, SHEET):
        total = total + near[k]
    far[z] = total
    second = [copy(far.at[z], far.at[z], s3.at[k], r3.at[k], line(q)) for k, q in enumerate(lines)]
    for c in second:
        c.start()
    for c in tiles:
        c.wait()
    moved = placed(got[...].reshape(128, 128))
    for c in second:
        c.wait()
    total = far[0]
    for k in range(1, LINE):
        total = total + far[k]
    top = jnp.sum(jnp.sum(total[0:4], axis=1, keepdims=True), axis=0, keepdims=True)
    bottom = jnp.sum(jnp.sum(total[4:8], axis=1, keepdims=True), axis=0, keepdims=True)
    level = jnp.broadcast_to(top / bottom, (32, 128))
    charges[...] = level * early[p, 32:64, :] - fe[...]
    nxt[...] = 2.0 * aux - prev[...] + kappa * (level * inverse - moved - aux)


def finish(fe, early, prev):
    vm = pl.BlockSpec(memory_space=pltpu.VMEM)
    dma = pltpu.SemaphoreType.DMA
    return pl.pallas_call(
        level_kernel,
        out_shape=[jax.ShapeDtypeStruct((32, 128), F32)] * 2,
        in_specs=[vm] * 3,
        out_specs=[vm] * 2,
        scratch_shapes=[
            pltpu.VMEM((4, 32, 128), F32),
            pltpu.VMEM((SHEET, 8, 128), F32),
            pltpu.VMEM((LINE, 8, 128), F32),
            dma((SHEET - 1,)), dma((SHEET - 1,)), dma((3,)), dma((3,)), dma((LINE - 1,)), dma((LINE - 1,)),
        ],
        compiler_params=pltpu.CompilerParams(collective_id=1, has_side_effects=True),
        name="level",
    )(fe, early, prev)


def on_device(positions, aux, aux_prev, resid, types, pair_tiles, pair_cands, pair_count, owner_tile, electroneg, hardness, widths):
    own, halo, early, codes = exchange(
        positions.transpose(0, 2, 1, 3).reshape(96, 128),
        aux.reshape(32, 128),
        resid.reshape(32, 128),
        types.reshape(32, 128),
        owner_tile.reshape(1, -1),
        pair_tiles.reshape(1, -1),
        pair_cands.reshape(1, -1),
        hardness,
        pair_count,
    )
    fe, rf = pair_call(codes, widths, electroneg, hardness, own, halo)
    charges, nxt = finish(fe, early, aux_prev.reshape(32, 128))
    return charges.reshape(aux.shape), nxt.reshape(aux.shape), rf.reshape(aux.shape)


def solution(mesh):
    s4, s3, s2 = P("brick", "plane", None, None), P("brick", "plane", None), P("brick", "plane")
    return jax.shard_map(
        on_device,
        mesh=mesh,
        in_specs=(s4, s3, s3, s3, s3, s3, s3, s2, s3, P(), P(), P()),
        out_specs=(s3, s3, s3),
        check_vma=False,
    )
```

```python
import functools

import jax
import jax.numpy as jnp
from jax import lax
from jax.experimental import pallas as pl
from jax.experimental.pallas import tpu as pltpu
from jax.sharding import PartitionSpec as P

F32 = jnp.float32
BF = jnp.bfloat16
HI = lax.Precision.HIGHEST
MESH = pl.DeviceIdType.MESH
kappa = 1.86

PB = 12
SB = 13
NT = 320


def order_pairs(tiles, cands, count, codes, tr, cr):
    n = tiles.shape[1]
    one = lax.broadcasted_iota(jnp.int32, (1, 128), 1)
    tr[...] = jnp.full((128, 128), 64.0, F32)
    cr[...] = jnp.zeros((16, 128), F32)
    for j in range(PB):
        w = min(128, n - 128 * j)
        tr[j : j + 1, :w] = tiles[:, 128 * j : 128 * j + w].astype(F32)
        cr[j : j + 1, :w] = cands[:, 128 * j : 128 * j + w].astype(F32)
    prow = lax.broadcasted_iota(jnp.int32, (16, 128), 0) * 128 + lax.broadcasted_iota(jnp.int32, (16, 128), 1)
    used = prow < count[0, 0]
    t = jnp.where(used, tr[:16], 64.0)
    c = jnp.where(used, cr[...], 0.0)
    tr[:16] = t
    tcol = tr[...].T
    lane = lax.broadcasted_iota(jnp.int32, (128, 128), 1)
    rowi = lax.broadcasted_iota(jnp.int32, (128, 128), 0)
    lanef = lane.astype(F32)
    before = jnp.where(lane < rowi, 1.0, 0.0).astype(BF)
    hot = [tcol[:, j : j + 1] == lanef for j in range(PB)]
    hotf = [jnp.where(h, 1.0, 0.0) for h in hot]
    sums = [jnp.sum(h, axis=0, keepdims=True) for h in hotf]
    counts = sum(sums)
    counts = jnp.where(one < 64, counts, 0.0)
    half = jnp.floor((counts + 1.0) * 0.5)
    starts = 2.0 * jnp.dot(jnp.broadcast_to(half, (8, 128)), jnp.where(rowi < lane, 1.0, 0.0), precision=HI, preferred_element_type=F32)[:1]
    starts = jnp.where(one < 64, starts, 8192.0)
    codes[:, SB * 128 :] = jnp.broadcast_to(jnp.sum(half, axis=1, keepdims=True), (1, 128)).astype(jnp.int32)
    out = jnp.zeros((8, SB * 128), F32)
    slot = lax.broadcasted_iota(jnp.int32, (128, SB * 128), 1).astype(F32)
    selfrow = jnp.zeros((1, 128), F32)
    e = float(NT) - c
    e = jnp.where(used, e, 0.0)
    ehi = jnp.floor(e * 0.5)
    elo = e - 2.0 * ehi
    same = jnp.where(t == c, 1.0, 0.0)
    r8 = lax.broadcasted_iota(jnp.int32, (8, 128), 0)
    for j in range(PB):
        rank = jnp.dot(before, hotf[j].astype(BF), preferred_element_type=F32)
        pos = jnp.sum(jnp.where(hot[j], rank + starts, 0.0), axis=1, keepdims=True)
        starts = starts + sums[j]
        vals = jnp.where(r8 == 0, ehi[j : j + 1], jnp.where(r8 == 1, elo[j : j + 1], jnp.where(r8 == 2, t[j : j + 1], same[j : j + 1])))
        put = jnp.where(pos == slot, 1.0, 0.0).astype(BF)
        out = out + jnp.dot(vals.astype(BF), put, preferred_element_type=F32)
        selfrow = selfrow + jnp.dot(vals.astype(BF), hotf[j].astype(BF), preferred_element_type=F32)[3:4]
    code = out[2:3] * 512.0 + (float(NT) - (2.0 * out[0:1] + out[1:2]))
    codes[:, : SB * 128] = code.astype(jnp.int32)
    lane32 = lax.broadcasted_iota(jnp.int32, (32, 128), 1)
    row32 = lax.broadcasted_iota(jnp.int32, (32, 128), 0)
    n = jnp.broadcast_to(selfrow, (32, 128))
    even = jnp.sum(jnp.where(lane32 == 2 * row32, n, 0.0), axis=1, keepdims=True)
    odd = jnp.sum(jnp.where(lane32 == 2 * row32 + 1, n, 0.0), axis=1, keepdims=True)
    return jnp.where(lane32 < 64, even, odd)


NR = 160
UN = 8
NB = 2


def split3(x):
    a = x.astype(BF).astype(F32)
    r = x - a
    b = r.astype(BF).astype(F32)
    return a, b, r - b


def pair_kernel(codes_h, widths, chi, hard, own_h, halo_h, fe, rf, codes, own, halo, sem, G, C, HS, CH, acc, FR, L, *bufs):
    loads = [
        pltpu.make_async_copy(s, d, sem.at[k])
        for k, (s, d) in enumerate(((own_h, own), (halo_h, halo), (codes_h, codes)))
    ]
    for c in loads:
        c.start()
    lane = lax.broadcasted_iota(jnp.int32, (8, 128), 1)
    row = lax.broadcasted_iota(jnp.int32, (8, 128), 0)
    low = lane < 64
    for c in loads:
        c.wait()
    for b in range(5):
        at = [own[c] if b == 0 else halo[b - 1, c] for c in range(6)]
        if b in (1, 2):
            at[0] = at[0] + (-16.0 if b == 1 else 16.0)
        if b in (3, 4):
            at[1] = at[1] + (-32.0 if b == 3 else 32.0)
        s = jnp.zeros((32, 128), F32)
        for t in range(8):
            s = jnp.where(at[5] == float(t), widths[t], s)
        for c, x in enumerate((at[0] * 0.1, at[1] * 0.1, at[2] * 0.1, at[3] * 0.1, at[4] * 0.1, s * s * 0.01)):
            G[pl.ds(c * NR + b * 32, 32), :] = x
    G[pl.ds(6 * NR, 2 * NR), :] = jnp.zeros((2 * NR, 128), F32)
    DS, VS = bufs[:NB], bufs[NB:]
    for k in range(NB):
        DS[k][...] = jnp.ones_like(DS[k])
        VS[k][...] = jnp.zeros_like(VS[k])

    def halves(x):
        y = pltpu.roll(x, 64, 1)
        return jnp.where(low, x, y), jnp.where(low, y, x)

    def prep(g, carry):
        c0, c1 = halves(G[pl.ds(g, 8, stride=NR), :])
        C[g * 2] = c0
        C[g * 2 + 1] = c1
        return carry

    lax.fori_loop(0, NR, prep, 0, unroll=8)
    C[NT] = jnp.where((row == 3) | (row == 4), 0.0, C[0])

    def prep_home(r, carry):
        v = G[pl.ds(r, 8, stride=NR), :]
        x = v[:, 0:1]
        y = v[:, 64:65]
        cen = jnp.where(low, jnp.broadcast_to(x, (8, 128)), jnp.broadcast_to(y, (8, 128)))
        cen = jnp.where(row < 3, cen, 0.0)
        a = v - cen
        n = jnp.sum(jnp.where(row < 3, a * a, 0.0), axis=0, keepdims=True) + 0.0025
        f = jnp.where(row < 3, -2.0 * a, jnp.where(row < 6, 1.0, jnp.where(row == 6, n, 0.0)))
        f1, f2, f3 = split3(f)
        t = jnp.concatenate([f1, f1, f1, f2, f2, f3, jnp.zeros((80, 128), F32)], axis=0).T.astype(BF)
        L[r * 2] = t[:64]
        L[r * 2 + 1] = t[64:]
        c0, c1 = halves(cen)
        CH[r * 2] = c0
        CH[r * 2 + 1] = c1
        FR[pl.ds(r, 1), :] = v[5:6, :]
        acc[0, pl.ds(2 * r, 2)] = jnp.zeros((2, 64, 128), F32)
        acc[1, pl.ds(2 * r, 2)] = jnp.zeros((2, 64, 128), F32)
        return carry

    lax.fori_loop(0, 32, prep_home, 0, unroll=4)
    t = FR[...].T
    for r in range(32):
        w = jnp.broadcast_to(t[:, r : r + 1], (128, 128))
        HS[2 * r] = w[:64]
        HS[2 * r + 1] = w[64:]
    last = jnp.where(row == 6, 1.0, 0.0)

    def terms(i, D, V):
        for u in range(UN):
            h = lax.shift_right_logical(codes[0, 2 * UN * i + 2 * u], 9)
            xs = [jnp.broadcast_to(V[u, k : k + 1], (8, 128)) for k in range(3, 6)]
            for q in range(8):
                rows = pl.ds(8 * q, 8)
                d = D[u, rows]
                w = lax.rsqrt(HS[h, rows] + xs[2])
                r = lax.rsqrt(d)
                e = lax.erf(d * r * w)
                m = jnp.maximum(1.0025 - d, 0.0)
                kk = (e * r) * (m * m)
                acc[0, h, rows] = acc[0, h, rows] + kk * xs[0]
                acc[1, h, rows] = acc[1, h, rows] + kk * xs[1]

    def distances(i, D, V):
        for u in range(UN):
            k1 = codes[0, 2 * UN * i + 2 * u]
            k2 = codes[0, 2 * UN * i + 2 * u + 1]
            h = lax.shift_right_logical(k1, 9)
            v = jnp.where(low, C[k1 & 511], C[k2 & 511]) - CH[h]
            V[u] = v
            f = jnp.where(row < 3, v, jnp.where(row < 6, pltpu.roll(v * v, 3, 0), last))
            s1, s2, s3 = split3(f)
            g = jnp.concatenate([s1, s2, s3, s1, s2, s1], axis=0).astype(BF)
            D[u] = jnp.dot(L[h, :, pl.ds(0, 48)], g, preferred_element_type=F32)

    def step(i, carry):
        for k in range(NB):
            terms(jnp.maximum(NB * i + k - 1, 0), DS[k - 1], VS[k - 1])
            distances(NB * i + k, DS[k], VS[k])
        return carry

    blocks = lax.div(codes[0, 1664] + UN - 1, UN)
    lax.fori_loop(0, lax.div(blocks + NB, NB), step, 0)

    def finish(r, carry):
        for f, ref in enumerate((fe, rf)):
            ref[pl.ds(r, 1), :] = jnp.sum(acc[f, pl.ds(2 * r, 2)].reshape(128, 128).T, axis=0, keepdims=True)
        return carry

    lax.fori_loop(0, 32, finish, 0, unroll=4)
    s2 = jnp.zeros((32, 128), F32)
    ch = jnp.zeros((32, 128), F32)
    eta = jnp.zeros((32, 128), F32)
    for t in range(8):
        hit = own[5] == float(t)
        s2 = jnp.where(hit, widths[t] * widths[t], s2)
        ch = jnp.where(hit, chi[t], ch)
        eta = jnp.where(hit, hard[t], eta)
    itself = own[6] * (2.0 * lax.erf(0.5 * lax.rsqrt(s2 + s2)))
    residual = rf[...] - itself * own[4]
    field = ch + (fe[...] - itself * own[3]) + residual
    rf[...] = residual
    fe[...] = field / eta


def pair_call(codes, widths, chi, hard, own, halo):
    sm = pl.BlockSpec(memory_space=pltpu.SMEM)
    vm = pl.BlockSpec(memory_space=pltpu.VMEM)
    hbm = pl.BlockSpec(memory_space=pl.ANY)
    return pl.pallas_call(
        pair_kernel,
        out_shape=[jax.ShapeDtypeStruct((32, 128), F32)] * 2,
        in_specs=[hbm] + [sm] * 3 + [hbm] * 2,
        out_specs=[vm, vm],
        scratch_shapes=[
            pltpu.SMEM(codes.shape, jnp.int32),
            pltpu.VMEM(own.shape, F32),
            pltpu.VMEM(halo.shape, F32),
            pltpu.SemaphoreType.DMA((3,)),
            pltpu.VMEM((8 * NR, 128), F32),
            pltpu.VMEM((NT + 1, 8, 128), F32),
            pltpu.VMEM((64, 64, 128), F32),
            pltpu.VMEM((64, 8, 128), F32),
            pltpu.VMEM((2, 64, 64, 128), F32),
            pltpu.VMEM((128, 128), F32),
            pltpu.VMEM((64, 64, 128), BF),
            *[pltpu.VMEM((UN, 64, 128), F32)] * NB,
            *[pltpu.VMEM((UN, 8, 128), F32)] * NB,
        ],
        compiler_params=pltpu.CompilerParams(vmem_limit_bytes=60 * 2**20),
        name="pairs",
    )(codes, widths, chi, hard, own, halo)


def exchange_kernel(
    pos, aux, resid, types, owner, tiles, cands, hard, count, own, halo, early, codes, send, recv, tr, cr
):
    nb, npl = lax.axis_size("brick"), lax.axis_size("plane")
    b, p = lax.axis_index("brick"), lax.axis_index("plane")
    below, above = lax.rem(b + nb - 1, nb), lax.rem(b + 1, nb)
    barrier = pltpu.get_barrier_semaphore()
    left, right = lax.rem(p + npl - 1, npl), lax.rem(p + 1, npl)
    for d in [(below, p), (above, p), (b, left), (b, right)]:
        pl.semaphore_signal(barrier, inc=1, device_id=d, device_id_type=MESH)
    for c in range(3):
        own[c] = pos[pl.ds(32 * c, 32), :]
    own[3] = aux[...]
    own[4] = resid[...]
    ty = types[...].astype(F32)
    own[5] = ty
    inverse = jnp.zeros((32, 128), F32)
    for t in range(8):
        inverse = jnp.where(ty == float(t), 1.0 / jnp.full((32, 128), hard[t], F32), inverse)
    early[0:32, :] = aux[...]
    early[32:64, :] = inverse
    src = lax.broadcasted_iota(jnp.int32, (64, 128), 0)
    lane = lax.broadcasted_iota(jnp.int32, (64, 128), 1) - 32 * p
    inside = (lane >= 0) & (lane < 32)
    ids = jnp.broadcast_to(owner[...].astype(F32), (8, 64))
    evens = jnp.dot(ids, jnp.where(inside & (src == 2 * lane), 1.0, 0.0), precision=HI, preferred_element_type=F32)
    odds = jnp.dot(ids, jnp.where(inside & (src == 2 * lane + 1), 1.0, 0.0), precision=HI, preferred_element_type=F32)
    r8 = lax.broadcasted_iota(jnp.int32, (8, 128), 0)
    early[64:72, :] = jnp.where(r8 == 0, evens, odds)
    pl.semaphore_wait(barrier, 4)

    def copy(s, d, k, to):
        return pltpu.make_async_remote_copy(
            src_ref=s, dst_ref=d, send_sem=send.at[k], recv_sem=recv.at[k], device_id=to, device_id_type=MESH
        )

    mine = own.at[pl.ds(0, 6)]
    copies = [
        copy(mine, halo.at[0], 0, (above, p)),
        copy(mine, halo.at[1], 1, (below, p)),
        copy(mine, halo.at[2], 2, (b, right)),
        copy(mine, halo.at[3], 3, (b, left)),
    ]
    for c in copies:
        c.start()
    own[6] = order_pairs(tiles, cands, count, codes, tr, cr)
    for c in copies:
        c.wait()


def exchange(pos, aux, resid, types, owner, tiles, cands, hard, count):
    vm = pl.BlockSpec(memory_space=pltpu.VMEM)
    return pl.pallas_call(
        exchange_kernel,
        out_shape=[
            jax.ShapeDtypeStruct((7, 32, 128), F32),
            jax.ShapeDtypeStruct((4, 6, 32, 128), F32),
            jax.ShapeDtypeStruct((72, 128), F32),
            jax.ShapeDtypeStruct((1, (SB + 1) * 128), jnp.int32),
        ],
        in_specs=[vm] * 7 + [pl.BlockSpec(memory_space=pltpu.SMEM)] * 2,
        out_specs=[vm] * 4,
        scratch_shapes=[
            pltpu.SemaphoreType.DMA((4,)),
            pltpu.SemaphoreType.DMA((4,)),
            pltpu.VMEM((128, 128), F32),
            pltpu.VMEM((16, 128), F32),
        ],
        compiler_params=pltpu.CompilerParams(collective_id=0, has_side_effects=True),
        name="exchange",
    )(pos, aux, resid, types, owner, tiles, cands, hard, count)


LINE, SHEET = 16, 32


def level_kernel(fe, early, prev, charges, nxt, got, near, far, s1, r1, s2, r2, s3, r3):
    npl = lax.axis_size("plane")
    b, p = lax.axis_index("brick"), lax.axis_index("plane")
    zhi = lax.rem(lax.div(b, 8), 4)
    z = npl * zhi + p
    w = 8 * lax.div(b, 32) + lax.rem(b, 8)

    def line(q):
        return (b + 8 * (lax.div(q, npl) - zhi), lax.rem(q, npl))

    def sheet(q):
        return (32 * lax.div(q, 8) + 8 * zhi + lax.rem(q, 8), p)

    lines = [lax.rem(z + k, LINE) for k in range(1, LINE)]
    sheets = [lax.rem(w + k, SHEET) for k in range(1, SHEET)]
    mates = [lax.rem(p + k, npl) for k in range(1, npl)]
    barrier = pltpu.get_barrier_semaphore()
    for q in lines:
        pl.semaphore_signal(barrier, inc=1, device_id=line(q), device_id_type=MESH)
    for q in sheets:
        pl.semaphore_signal(barrier, inc=1, device_id=sheet(q), device_id_type=MESH)
    got[p, 0:72, :] = early[...]
    got[p, 72:104, :] = fe[...]

    def fold(x):
        s = x[0:8] + x[8:16] + x[16:24] + x[24:32]
        return s[0:4] + s[4:8]

    near[w] = jnp.concatenate([fold(early[0:32, :] + fe[...]), fold(early[32:64, :])], axis=0)
    pl.semaphore_wait(barrier, LINE + SHEET - 2)

    def copy(s, d, ss, rs, to):
        return pltpu.make_async_remote_copy(
            src_ref=s, dst_ref=d, send_sem=ss, recv_sem=rs, device_id=to, device_id_type=MESH
        )

    first = [copy(near.at[w], near.at[w], s1.at[k], r1.at[k], sheet(q)) for k, q in enumerate(sheets)]
    for c in first:
        c.start()
    tiles = [copy(got.at[p], got.at[p], s2.at[k], r2.at[k], (b, q)) for k, q in enumerate(mates)]
    for c in tiles:
        c.start()
    for c in first:
        c.wait()
    total = near[0]
    for k in range(1, SHEET):
        total = total + near[k]
    far[z] = total
    second = [copy(far.at[z], far.at[z], s3.at[k], r3.at[k], line(q)) for k, q in enumerate(lines)]
    for c in second:
        c.start()
    for c in tiles:
        c.wait()
    evens = got[0, 64:65, :] + got[1, 64:65, :] + got[2, 64:65, :] + got[3, 64:65, :]
    odds = got[0, 65:66, :] + got[1, 65:66, :] + got[2, 65:66, :] + got[3, 65:66, :]
    slot = (64 * p + 2 * lax.broadcasted_iota(jnp.int32, (32, 128), 0)).astype(F32)
    place = jnp.concatenate(
        [
            jnp.where(evens == slot, 1.0, 0.0),
            jnp.where(odds == slot + 1.0, 1.0, 0.0),
            jnp.where(evens == slot + 1.0, 1.0, 0.0),
            jnp.where(odds == slot, 1.0, 0.0),
        ],
        axis=0,
    )
    low = lax.broadcasted_iota(jnp.int32, (32, 128), 1) < 64

    def placed(x):
        y = jnp.dot(place, x, precision=HI, preferred_element_type=F32)
        return jnp.where(low, y[0:32], y[32:64]) + pltpu.roll(jnp.where(low, y[64:96], y[96:128]), 64, 1)

    aux = placed(got[:, 0:32, :].reshape(128, 128))
    inverse = placed(got[:, 32:64, :].reshape(128, 128))
    moved = placed(got[:, 72:104, :].reshape(128, 128))
    for c in second:
        c.wait()
    total = far[0]
    for k in range(1, LINE):
        total = total + far[k]
    top = jnp.sum(jnp.sum(total[0:4], axis=1, keepdims=True), axis=0, keepdims=True)
    bottom = jnp.sum(jnp.sum(total[4:8], axis=1, keepdims=True), axis=0, keepdims=True)
    level = jnp.broadcast_to(top / bottom, (32, 128))
    charges[...] = level * early[32:64, :] - fe[...]
    nxt[...] = 2.0 * aux - prev[...] + kappa * (level * inverse - moved - aux)


def finish(fe, early, prev):
    vm = pl.BlockSpec(memory_space=pltpu.VMEM)
    dma = pltpu.SemaphoreType.DMA
    return pl.pallas_call(
        level_kernel,
        out_shape=[jax.ShapeDtypeStruct((32, 128), F32)] * 2,
        in_specs=[vm] * 3,
        out_specs=[vm] * 2,
        scratch_shapes=[
            pltpu.VMEM((4, 104, 128), F32),
            pltpu.VMEM((SHEET, 8, 128), F32),
            pltpu.VMEM((LINE, 8, 128), F32),
            dma((SHEET - 1,)), dma((SHEET - 1,)), dma((3,)), dma((3,)), dma((LINE - 1,)), dma((LINE - 1,)),
        ],
        compiler_params=pltpu.CompilerParams(collective_id=1, has_side_effects=True),
        name="level",
    )(fe, early, prev)


def on_device(positions, aux, aux_prev, resid, types, pair_tiles, pair_cands, pair_count, owner_tile, electroneg, hardness, widths):
    own, halo, early, codes = exchange(
        positions.transpose(0, 2, 1, 3).reshape(96, 128),
        aux.reshape(32, 128),
        resid.reshape(32, 128),
        types.reshape(32, 128),
        owner_tile.reshape(1, -1),
        pair_tiles.reshape(1, -1),
        pair_cands.reshape(1, -1),
        hardness,
        pair_count,
    )
    fe, rf = pair_call(codes, widths, electroneg, hardness, own, halo)
    charges, nxt = finish(fe, early, aux_prev.reshape(32, 128))
    return charges.reshape(aux.shape), nxt.reshape(aux.shape), rf.reshape(aux.shape)


def solution(mesh):
    s4, s3, s2 = P("brick", "plane", None, None), P("brick", "plane", None), P("brick", "plane")
    return jax.shard_map(
        on_device,
        mesh=mesh,
        in_specs=(s4, s3, s3, s3, s3, s3, s3, s2, s3, P(), P(), P()),
        out_specs=(s3, s3, s3),
        check_vma=False,
    )
```

```python
import functools

import jax
import jax.numpy as jnp
from jax import lax
from jax.experimental import pallas as pl
from jax.experimental.pallas import tpu as pltpu
from jax.sharding import PartitionSpec as P

F32 = jnp.float32
BF = jnp.bfloat16
HI = lax.Precision.HIGHEST
MESH = pl.DeviceIdType.MESH
kappa = 1.86

PB = 12
SB = 13
NT = 320


def order_pairs(tiles, cands, count, codes, tr, cr):
    n = tiles.shape[1]
    one = lax.broadcasted_iota(jnp.int32, (1, 128), 1)
    tr[...] = jnp.full((128, 128), 64.0, F32)
    cr[...] = jnp.zeros((16, 128), F32)
    for j in range(PB):
        w = min(128, n - 128 * j)
        tr[j : j + 1, :w] = tiles[:, 128 * j : 128 * j + w].astype(F32)
        cr[j : j + 1, :w] = cands[:, 128 * j : 128 * j + w].astype(F32)
    prow = lax.broadcasted_iota(jnp.int32, (16, 128), 0) * 128 + lax.broadcasted_iota(jnp.int32, (16, 128), 1)
    used = prow < count[0, 0]
    t = jnp.where(used, tr[:16], 64.0)
    c = jnp.where(used, cr[...], 0.0)
    tr[:16] = t
    tcol = tr[...].T
    lane = lax.broadcasted_iota(jnp.int32, (128, 128), 1)
    rowi = lax.broadcasted_iota(jnp.int32, (128, 128), 0)
    lanef = lane.astype(F32)
    before = jnp.where(lane < rowi, 1.0, 0.0).astype(BF)
    hot = [tcol[:, j : j + 1] == lanef for j in range(PB)]
    hotf = [jnp.where(h, 1.0, 0.0) for h in hot]
    sums = [jnp.sum(h, axis=0, keepdims=True) for h in hotf]
    counts = sum(sums)
    counts = jnp.where(one < 64, counts, 0.0)
    half = jnp.floor((counts + 1.0) * 0.5)
    starts = 2.0 * jnp.dot(jnp.broadcast_to(half, (8, 128)), jnp.where(rowi < lane, 1.0, 0.0), precision=HI, preferred_element_type=F32)[:1]
    starts = jnp.where(one < 64, starts, 8192.0)
    codes[:, SB * 128 :] = jnp.broadcast_to(jnp.sum(half, axis=1, keepdims=True), (1, 128)).astype(jnp.int32)
    out = jnp.zeros((8, SB * 128), F32)
    slot = lax.broadcasted_iota(jnp.int32, (128, SB * 128), 1).astype(F32)
    selfrow = jnp.zeros((1, 128), F32)
    e = float(NT) - c
    e = jnp.where(used, e, 0.0)
    ehi = jnp.floor(e * 0.5)
    elo = e - 2.0 * ehi
    same = jnp.where(t == c, 1.0, 0.0)
    r8 = lax.broadcasted_iota(jnp.int32, (8, 128), 0)
    for j in range(PB):
        rank = jnp.dot(before, hotf[j].astype(BF), preferred_element_type=F32)
        pos = jnp.sum(jnp.where(hot[j], rank + starts, 0.0), axis=1, keepdims=True)
        starts = starts + sums[j]
        vals = jnp.where(r8 == 0, ehi[j : j + 1], jnp.where(r8 == 1, elo[j : j + 1], jnp.where(r8 == 2, t[j : j + 1], same[j : j + 1])))
        put = jnp.where(pos == slot, 1.0, 0.0).astype(BF)
        out = out + jnp.dot(vals.astype(BF), put, preferred_element_type=F32)
        selfrow = selfrow + jnp.dot(vals.astype(BF), hotf[j].astype(BF), preferred_element_type=F32)[3:4]
    code = out[2:3] * 512.0 + (float(NT) - (2.0 * out[0:1] + out[1:2]))
    codes[:, : SB * 128] = code.astype(jnp.int32)
    lane32 = lax.broadcasted_iota(jnp.int32, (32, 128), 1)
    row32 = lax.broadcasted_iota(jnp.int32, (32, 128), 0)
    n = jnp.broadcast_to(selfrow, (32, 128))
    even = jnp.sum(jnp.where(lane32 == 2 * row32, n, 0.0), axis=1, keepdims=True)
    odd = jnp.sum(jnp.where(lane32 == 2 * row32 + 1, n, 0.0), axis=1, keepdims=True)
    return jnp.where(lane32 < 64, even, odd)


NR = 160
UN = 8
NB = 2


def split3(x):
    a = x.astype(BF).astype(F32)
    r = x - a
    b = r.astype(BF).astype(F32)
    return a, b, r - b


def pair_kernel(codes_h, widths, chi, hard, own_h, halo_h, fe, rf, codes, own, halo, sem, G, C, CH, acc, L, *bufs):
    loads = [
        pltpu.make_async_copy(s, d, sem.at[k])
        for k, (s, d) in enumerate(((own_h, own), (halo_h, halo), (codes_h, codes)))
    ]
    for c in loads:
        c.start()
    lane = lax.broadcasted_iota(jnp.int32, (8, 128), 1)
    row = lax.broadcasted_iota(jnp.int32, (8, 128), 0)
    low = lane < 64
    for c in loads:
        c.wait()
    for b in range(5):
        at = [own[c] if b == 0 else halo[b - 1, c] for c in range(6)]
        if b in (1, 2):
            at[0] = at[0] + (-16.0 if b == 1 else 16.0)
        if b in (3, 4):
            at[1] = at[1] + (-32.0 if b == 3 else 32.0)
        for c, x in enumerate((at[0] * 0.1, at[1] * 0.1, at[2] * 0.1, at[3] * 0.1, at[4] * 0.1, at[5])):
            G[pl.ds(c * NR + b * 32, 32), :] = x
    G[pl.ds(6 * NR, 2 * NR), :] = jnp.zeros((2 * NR, 128), F32)
    DS, VS = bufs[:NB], bufs[NB:]
    for k in range(NB):
        DS[k][...] = jnp.ones_like(DS[k])
        VS[k][...] = jnp.zeros_like(VS[k])

    def halves(x):
        y = pltpu.roll(x, 64, 1)
        return jnp.where(low, x, y), jnp.where(low, y, x)

    def prep(g, carry):
        c0, c1 = halves(G[pl.ds(g, 8, stride=NR), :])
        C[g * 2] = c0
        C[g * 2 + 1] = c1
        return carry

    lax.fori_loop(0, NR, prep, 0, unroll=16)
    C[NT] = jnp.where((row == 3) | (row == 4), 0.0, C[0])

    st = jnp.zeros((8, 128), F32)
    for t in range(8):
        st = jnp.where(row == t, widths[t], st)
    st = st * st * 0.01

    def prep_home(r, carry):
        v = G[pl.ds(r, 8, stride=NR), :]
        x = v[:, 0:1]
        y = v[:, 64:65]
        cen = jnp.where(low, jnp.broadcast_to(x, (8, 128)), jnp.broadcast_to(y, (8, 128)))
        cen = jnp.where(row < 3, cen, 0.0)
        a = v - cen
        n = jnp.sum(jnp.where(row < 3, a * a, 0.0), axis=0, keepdims=True) + 0.0025
        f = jnp.where(row < 3, -2.0 * a, jnp.where(row < 6, 1.0, jnp.where(row == 6, n, 0.0)))
        f1, f2, f3 = split3(f)
        si = jnp.sum(jnp.where(row.astype(F32) == v[5:6], st, 0.0), axis=0, keepdims=True)
        w1, w2, w3 = split3(lax.rsqrt(st + si))
        t = jnp.concatenate([f1, f1, f1, f2, f2, f3, w1, w2, jnp.zeros((64, 128), F32)], axis=0).T.astype(BF)
        L[r * 2] = t[:64]
        L[r * 2 + 1] = t[64:]
        c0, c1 = halves(cen)
        CH[r * 2] = c0
        CH[r * 2 + 1] = c1
        acc[0, pl.ds(2 * r, 2)] = jnp.zeros((2, 64, 128), F32)
        acc[1, pl.ds(2 * r, 2)] = jnp.zeros((2, 64, 128), F32)
        return carry

    lax.fori_loop(0, 32, prep_home, 0, unroll=8)
    types8 = row.astype(F32)
    zeros16 = jnp.zeros((16, 128), BF)
    zeros48 = jnp.zeros((48, 128), BF)
    last = jnp.where(row == 6, 1.0, 0.0)

    def terms(i, D, V):
        for u in range(UN):
            h = lax.shift_right_logical(codes[0, 2 * UN * i + 2 * u], 9)
            xs = [jnp.broadcast_to(V[u, k : k + 1], (8, 128)) for k in range(3, 5)]
            for q in range(8):
                rows = pl.ds(8 * q, 8)
                d = D[u, rows, pl.ds(0, 128)]
                w = D[u, rows, pl.ds(128, 128)]
                r = lax.rsqrt(d)
                e = lax.erf(d * r * w)
                m = jnp.maximum(1.0025 - d, 0.0)
                kk = (e * r) * (m * m)
                acc[0, h, rows] = acc[0, h, rows] + kk * xs[0]
                acc[1, h, rows] = acc[1, h, rows] + kk * xs[1]

    def distances(i, D, V):
        for u in range(UN):
            k1 = codes[0, 2 * UN * i + 2 * u]
            k2 = codes[0, 2 * UN * i + 2 * u + 1]
            h = lax.shift_right_logical(k1, 9)
            v = jnp.where(low, C[k1 & 511], C[k2 & 511]) - CH[h]
            V[u] = v
            f = jnp.where(row < 3, v, jnp.where(row < 6, pltpu.roll(v * v, 3, 0), last))
            s1, s2, s3 = split3(f)
            g = jnp.concatenate([s1, s2, s3, s1, s2, s1], axis=0).astype(BF)
            oh = jnp.where(types8 == v[5:6], 1.0, 0.0)
            oh = jnp.concatenate([oh, oh], axis=0).astype(BF)
            g = jnp.concatenate(
                [jnp.concatenate([g, zeros16], axis=0), jnp.concatenate([zeros48, oh], axis=0)], axis=1
            )
            D[u] = jnp.dot(L[h, :, pl.ds(0, 64)], g, preferred_element_type=F32)

    def step(i, carry):
        for k in range(NB):
            terms(jnp.maximum(NB * i + k - 1, 0), DS[k - 1], VS[k - 1])
            distances(NB * i + k, DS[k], VS[k])
        return carry

    blocks = lax.div(codes[0, 1664] + UN - 1, UN)
    lax.fori_loop(0, lax.div(blocks + NB, NB), step, 0)

    def finish(r, carry):
        for f, ref in enumerate((fe, rf)):
            ref[pl.ds(r, 1), :] = jnp.sum(acc[f, pl.ds(2 * r, 2)].reshape(128, 128).T, axis=0, keepdims=True)
        return carry

    lax.fori_loop(0, 32, finish, 0, unroll=8)
    s2 = jnp.zeros((32, 128), F32)
    ch = jnp.zeros((32, 128), F32)
    eta = jnp.zeros((32, 128), F32)
    for t in range(8):
        hit = own[5] == float(t)
        s2 = jnp.where(hit, widths[t] * widths[t], s2)
        ch = jnp.where(hit, chi[t], ch)
        eta = jnp.where(hit, hard[t], eta)
    itself = own[6] * (2.0 * lax.erf(0.5 * lax.rsqrt(s2 + s2)))
    residual = rf[...] - itself * own[4]
    field = ch + (fe[...] - itself * own[3]) + residual
    rf[...] = residual
    fe[...] = field / eta


def pair_call(codes, widths, chi, hard, own, halo):
    sm = pl.BlockSpec(memory_space=pltpu.SMEM)
    vm = pl.BlockSpec(memory_space=pltpu.VMEM)
    hbm = pl.BlockSpec(memory_space=pl.ANY)
    return pl.pallas_call(
        pair_kernel,
        out_shape=[jax.ShapeDtypeStruct((32, 128), F32)] * 2,
        in_specs=[hbm] + [sm] * 3 + [hbm] * 2,
        out_specs=[vm, vm],
        scratch_shapes=[
            pltpu.SMEM(codes.shape, jnp.int32),
            pltpu.VMEM(own.shape, F32),
            pltpu.VMEM(halo.shape, F32),
            pltpu.SemaphoreType.DMA((3,)),
            pltpu.VMEM((8 * NR, 128), F32),
            pltpu.VMEM((NT + 1, 8, 128), F32),
            pltpu.VMEM((64, 8, 128), F32),
            pltpu.VMEM((2, 64, 64, 128), F32),
            pltpu.VMEM((64, 64, 128), BF),
            *[pltpu.VMEM((UN, 64, 256), F32)] * NB,
            *[pltpu.VMEM((UN, 8, 128), F32)] * NB,
        ],
        compiler_params=pltpu.CompilerParams(vmem_limit_bytes=60 * 2**20),
        name="pairs",
    )(codes, widths, chi, hard, own, halo)


def exchange_kernel(
    pos, aux, resid, types, owner, tiles, cands, hard, count, own, halo, early, codes, send, recv, tr, cr
):
    nb, npl = lax.axis_size("brick"), lax.axis_size("plane")
    b, p = lax.axis_index("brick"), lax.axis_index("plane")
    below, above = lax.rem(b + nb - 1, nb), lax.rem(b + 1, nb)
    barrier = pltpu.get_barrier_semaphore()
    left, right = lax.rem(p + npl - 1, npl), lax.rem(p + 1, npl)
    for d in [(below, p), (above, p), (b, left), (b, right)]:
        pl.semaphore_signal(barrier, inc=1, device_id=d, device_id_type=MESH)
    for c in range(3):
        own[c] = pos[pl.ds(32 * c, 32), :]
    own[3] = aux[...]
    own[4] = resid[...]
    ty = types[...].astype(F32)
    own[5] = ty
    inverse = jnp.zeros((32, 128), F32)
    for t in range(8):
        inverse = jnp.where(ty == float(t), 1.0 / jnp.full((32, 128), hard[t], F32), inverse)
    early[0:32, :] = aux[...]
    early[32:64, :] = inverse
    src = lax.broadcasted_iota(jnp.int32, (64, 128), 0)
    lane = lax.broadcasted_iota(jnp.int32, (64, 128), 1) - 32 * p
    inside = (lane >= 0) & (lane < 32)
    ids = jnp.broadcast_to(owner[...].astype(F32), (8, 64))
    evens = jnp.dot(ids, jnp.where(inside & (src == 2 * lane), 1.0, 0.0), precision=HI, preferred_element_type=F32)
    odds = jnp.dot(ids, jnp.where(inside & (src == 2 * lane + 1), 1.0, 0.0), precision=HI, preferred_element_type=F32)
    r8 = lax.broadcasted_iota(jnp.int32, (8, 128), 0)
    early[64:72, :] = jnp.where(r8 == 0, evens, odds)
    pl.semaphore_wait(barrier, 4)

    def copy(s, d, k, to):
        return pltpu.make_async_remote_copy(
            src_ref=s, dst_ref=d, send_sem=send.at[k], recv_sem=recv.at[k], device_id=to, device_id_type=MESH
        )

    mine = own.at[pl.ds(0, 6)]
    copies = [
        copy(mine, halo.at[0], 0, (above, p)),
        copy(mine, halo.at[1], 1, (below, p)),
        copy(mine, halo.at[2], 2, (b, right)),
        copy(mine, halo.at[3], 3, (b, left)),
    ]
    for c in copies:
        c.start()
    own[6] = order_pairs(tiles, cands, count, codes, tr, cr)
    for c in copies:
        c.wait()


def exchange(pos, aux, resid, types, owner, tiles, cands, hard, count):
    vm = pl.BlockSpec(memory_space=pltpu.VMEM)
    return pl.pallas_call(
        exchange_kernel,
        out_shape=[
            jax.ShapeDtypeStruct((7, 32, 128), F32),
            jax.ShapeDtypeStruct((4, 6, 32, 128), F32),
            jax.ShapeDtypeStruct((72, 128), F32),
            jax.ShapeDtypeStruct((1, (SB + 1) * 128), jnp.int32),
        ],
        in_specs=[vm] * 7 + [pl.BlockSpec(memory_space=pltpu.SMEM)] * 2,
        out_specs=[vm] * 4,
        scratch_shapes=[
            pltpu.SemaphoreType.DMA((4,)),
            pltpu.SemaphoreType.DMA((4,)),
            pltpu.VMEM((128, 128), F32),
            pltpu.VMEM((16, 128), F32),
        ],
        compiler_params=pltpu.CompilerParams(collective_id=0, has_side_effects=True),
        name="exchange",
    )(pos, aux, resid, types, owner, tiles, cands, hard, count)


LINE, SHEET = 16, 32


def level_kernel(fe, early, prev, charges, nxt, got, near, far, s1, r1, s2, r2, s3, r3, ready):
    npl = lax.axis_size("plane")
    b, p = lax.axis_index("brick"), lax.axis_index("plane")
    zhi = lax.rem(lax.div(b, 8), 4)
    z = npl * zhi + p
    w = 8 * lax.div(b, 32) + lax.rem(b, 8)

    def line(q):
        return (b + 8 * (lax.div(q, npl) - zhi), lax.rem(q, npl))

    def sheet(q):
        return (32 * lax.div(q, 8) + 8 * zhi + lax.rem(q, 8), p)

    lines = [lax.rem(z + k, LINE) for k in range(1, LINE)]
    sheets = [lax.rem(w + k, SHEET) for k in range(1, SHEET)]
    mates = [lax.rem(p + k, npl) for k in range(1, npl)]
    barrier = pltpu.get_barrier_semaphore()
    for k in (1, 2, 3, 4, 12, 13, 14, 15):
        pl.semaphore_signal(barrier, inc=1, device_id=line(lax.rem(z + k, LINE)), device_id_type=MESH)
    for q in sheets:
        pl.semaphore_signal(barrier, inc=1, device_id=sheet(q), device_id_type=MESH)
    got[p, 0:72, :] = early[...]
    got[p, 72:104, :] = fe[...]

    def fold(x):
        s = x[0:8] + x[8:16] + x[16:24] + x[24:32]
        return s[0:4] + s[4:8]

    near[w] = jnp.concatenate([fold(early[0:32, :] + fe[...]), fold(early[32:64, :])], axis=0)
    pl.semaphore_wait(barrier, 8 + SHEET - 1)
    for k in (4, 12):
        pl.semaphore_signal(ready, inc=1, device_id=line(lax.rem(z + k, LINE)), device_id_type=MESH)

    def copy(s, d, ss, rs, to):
        return pltpu.make_async_remote_copy(
            src_ref=s, dst_ref=d, send_sem=ss, recv_sem=rs, device_id=to, device_id_type=MESH
        )

    first = [copy(near.at[w], near.at[w], s1.at[k], r1.at[k], sheet(q)) for k, q in enumerate(sheets)]
    for c in first:
        c.start()
    tiles = [copy(got.at[p], got.at[p], s2.at[k], r2.at[k], (b, q)) for k, q in enumerate(mates)]
    for c in tiles:
        c.start()
    for c in first:
        c.wait()
    total = near[0]
    for k in range(1, SHEET):
        total = total + near[k]
    far[z] = total
    pl.semaphore_wait(ready, 2)
    second = [copy(far.at[z], far.at[z], s3.at[k], r3.at[k], line(q)) for k, q in enumerate(lines)]
    for c in second:
        c.start()
    for c in tiles:
        c.wait()
    evens = got[0, 64:65, :] + got[1, 64:65, :] + got[2, 64:65, :] + got[3, 64:65, :]
    odds = got[0, 65:66, :] + got[1, 65:66, :] + got[2, 65:66, :] + got[3, 65:66, :]
    slot = (64 * p + 2 * lax.broadcasted_iota(jnp.int32, (32, 128), 0)).astype(F32)
    place = jnp.concatenate(
        [
            jnp.where(evens == slot, 1.0, 0.0),
            jnp.where(odds == slot + 1.0, 1.0, 0.0),
            jnp.where(evens == slot + 1.0, 1.0, 0.0),
            jnp.where(odds == slot, 1.0, 0.0),
        ],
        axis=0,
    )
    low = lax.broadcasted_iota(jnp.int32, (32, 128), 1) < 64

    def placed(x):
        y = jnp.dot(place, x, precision=HI, preferred_element_type=F32)
        return jnp.where(low, y[0:32], y[32:64]) + pltpu.roll(jnp.where(low, y[64:96], y[96:128]), 64, 1)

    aux = placed(got[:, 0:32, :].reshape(128, 128))
    inverse = placed(got[:, 32:64, :].reshape(128, 128))
    moved = placed(got[:, 72:104, :].reshape(128, 128))
    for c in second:
        c.wait()
    total = far[0]
    for k in range(1, LINE):
        total = total + far[k]
    top = jnp.sum(jnp.sum(total[0:4], axis=1, keepdims=True), axis=0, keepdims=True)
    bottom = jnp.sum(jnp.sum(total[4:8], axis=1, keepdims=True), axis=0, keepdims=True)
    level = jnp.broadcast_to(top / bottom, (32, 128))
    charges[...] = level * early[32:64, :] - fe[...]
    nxt[...] = 2.0 * aux - prev[...] + kappa * (level * inverse - moved - aux)


def finish(fe, early, prev):
    vm = pl.BlockSpec(memory_space=pltpu.VMEM)
    dma = pltpu.SemaphoreType.DMA
    return pl.pallas_call(
        level_kernel,
        out_shape=[jax.ShapeDtypeStruct((32, 128), F32)] * 2,
        in_specs=[vm] * 3,
        out_specs=[vm] * 2,
        scratch_shapes=[
            pltpu.VMEM((4, 104, 128), F32),
            pltpu.VMEM((SHEET, 8, 128), F32),
            pltpu.VMEM((LINE, 8, 128), F32),
            dma((SHEET - 1,)), dma((SHEET - 1,)), dma((3,)), dma((3,)), dma((LINE - 1,)), dma((LINE - 1,)),
            pltpu.SemaphoreType.REGULAR,
        ],
        compiler_params=pltpu.CompilerParams(collective_id=1, has_side_effects=True),
        name="level",
    )(fe, early, prev)


def on_device(positions, aux, aux_prev, resid, types, pair_tiles, pair_cands, pair_count, owner_tile, electroneg, hardness, widths):
    own, halo, early, codes = exchange(
        positions.transpose(0, 2, 1, 3).reshape(96, 128),
        aux.reshape(32, 128),
        resid.reshape(32, 128),
        types.reshape(32, 128),
        owner_tile.reshape(1, -1),
        pair_tiles.reshape(1, -1),
        pair_cands.reshape(1, -1),
        hardness,
        pair_count,
    )
    fe, rf = pair_call(codes, widths, electroneg, hardness, own, halo)
    charges, nxt = finish(fe, early, aux_prev.reshape(32, 128))
    return charges.reshape(aux.shape), nxt.reshape(aux.shape), rf.reshape(aux.shape)


def solution(mesh):
    s4, s3, s2 = P("brick", "plane", None, None), P("brick", "plane", None), P("brick", "plane")
    return jax.shard_map(
        on_device,
        mesh=mesh,
        in_specs=(s4, s3, s3, s3, s3, s3, s3, s2, s3, P(), P(), P()),
        out_specs=(s3, s3, s3),
        check_vma=False,
    )
```

```python
import functools

import jax
import jax.numpy as jnp
from jax import lax
from jax.experimental import pallas as pl
from jax.experimental.pallas import tpu as pltpu
from jax.sharding import PartitionSpec as P

F32 = jnp.float32
BF = jnp.bfloat16
HI = lax.Precision.HIGHEST
MESH = pl.DeviceIdType.MESH
kappa = 1.86

PB = 12
SB = 13
NT = 320


def order_pairs(tiles, cands, count, codes, tr, cr):
    n = tiles.shape[1]
    one = lax.broadcasted_iota(jnp.int32, (1, 128), 1)
    tr[...] = jnp.full((128, 128), 64.0, F32)
    cr[...] = jnp.zeros((16, 128), F32)
    for j in range(PB):
        w = min(128, n - 128 * j)
        tr[j : j + 1, :w] = tiles[:, 128 * j : 128 * j + w].astype(F32)
        cr[j : j + 1, :w] = cands[:, 128 * j : 128 * j + w].astype(F32)
    prow = lax.broadcasted_iota(jnp.int32, (16, 128), 0) * 128 + lax.broadcasted_iota(jnp.int32, (16, 128), 1)
    used = prow < count[0, 0]
    t = jnp.where(used, tr[:16], 64.0)
    c = jnp.where(used, cr[...], 0.0)
    tr[:16] = t
    tcol = tr[...].T
    lane = lax.broadcasted_iota(jnp.int32, (128, 128), 1)
    rowi = lax.broadcasted_iota(jnp.int32, (128, 128), 0)
    lanef = lane.astype(F32)
    before = jnp.where(lane < rowi, 1.0, 0.0).astype(BF)
    hot = [tcol[:, j : j + 1] == lanef for j in range(PB)]
    hotf = [jnp.where(h, 1.0, 0.0) for h in hot]
    sums = [jnp.sum(h, axis=0, keepdims=True) for h in hotf]
    counts = sum(sums)
    counts = jnp.where(one < 64, counts, 0.0)
    half = jnp.floor((counts + 1.0) * 0.5)
    starts = 2.0 * jnp.dot(jnp.broadcast_to(half, (8, 128)), jnp.where(rowi < lane, 1.0, 0.0), precision=HI, preferred_element_type=F32)[:1]
    starts = jnp.where(one < 64, starts, 8192.0)
    codes[:, SB * 128 :] = jnp.broadcast_to(jnp.sum(half, axis=1, keepdims=True), (1, 128)).astype(jnp.int32)
    out = jnp.zeros((8, SB * 128), F32)
    slot = lax.broadcasted_iota(jnp.int32, (128, SB * 128), 1).astype(F32)
    selfrow = jnp.zeros((1, 128), F32)
    e = float(NT) - c
    e = jnp.where(used, e, 0.0)
    ehi = jnp.floor(e * 0.5)
    elo = e - 2.0 * ehi
    same = jnp.where(t == c, 1.0, 0.0)
    r8 = lax.broadcasted_iota(jnp.int32, (8, 128), 0)
    for j in range(PB):
        rank = jnp.dot(before, hotf[j].astype(BF), preferred_element_type=F32)
        pos = jnp.sum(jnp.where(hot[j], rank + starts, 0.0), axis=1, keepdims=True)
        starts = starts + sums[j]
        vals = jnp.where(r8 == 0, ehi[j : j + 1], jnp.where(r8 == 1, elo[j : j + 1], jnp.where(r8 == 2, t[j : j + 1], same[j : j + 1])))
        put = jnp.where(pos == slot, 1.0, 0.0).astype(BF)
        out = out + jnp.dot(vals.astype(BF), put, preferred_element_type=F32)
        selfrow = selfrow + jnp.dot(vals.astype(BF), hotf[j].astype(BF), preferred_element_type=F32)[3:4]
    code = out[2:3] * 512.0 + (float(NT) - (2.0 * out[0:1] + out[1:2]))
    codes[:, : SB * 128] = code.astype(jnp.int32)
    lane32 = lax.broadcasted_iota(jnp.int32, (32, 128), 1)
    row32 = lax.broadcasted_iota(jnp.int32, (32, 128), 0)
    n = jnp.broadcast_to(selfrow, (32, 128))
    even = jnp.sum(jnp.where(lane32 == 2 * row32, n, 0.0), axis=1, keepdims=True)
    odd = jnp.sum(jnp.where(lane32 == 2 * row32 + 1, n, 0.0), axis=1, keepdims=True)
    return jnp.where(lane32 < 64, even, odd)


NR = 160
UN = 8
NB = 2


def split3(x):
    a = x.astype(BF).astype(F32)
    r = x - a
    b = r.astype(BF).astype(F32)
    return a, b, r - b


def home_features(own, widths, L, CH):
    lane = lax.broadcasted_iota(jnp.int32, (8, 128), 1)
    row = lax.broadcasted_iota(jnp.int32, (8, 128), 0)
    low = lane < 64

    def halves(x):
        y = pltpu.roll(x, 64, 1)
        return jnp.where(low, x, y), jnp.where(low, y, x)

    st = jnp.zeros((8, 128), F32)
    for t in range(8):
        st = jnp.where(row == t, widths[t], st)
    st = st * st * 0.01

    def prep_home(r, carry):
        v = own[pl.ds(r, 8, stride=32), :]
        v = jnp.where(row < 3, v * 0.1, v)
        x = v[:, 0:1]
        y = v[:, 64:65]
        cen = jnp.where(low, jnp.broadcast_to(x, (8, 128)), jnp.broadcast_to(y, (8, 128)))
        cen = jnp.where(row < 3, cen, 0.0)
        a = v - cen
        n = jnp.sum(jnp.where(row < 3, a * a, 0.0), axis=0, keepdims=True) + 0.0025
        f = jnp.where(row < 3, -2.0 * a, jnp.where(row < 6, 1.0, jnp.where(row == 6, n, 0.0)))
        f1, f2, f3 = split3(f)
        si = jnp.sum(jnp.where(row.astype(F32) == v[5:6], st, 0.0), axis=0, keepdims=True)
        w1, w2, w3 = split3(lax.rsqrt(st + si))
        t = jnp.concatenate([f1, f1, f1, f2, f2, f3, w1, w2, jnp.zeros((64, 128), F32)], axis=0).T.astype(BF)
        L[r * 2] = t[:64]
        L[r * 2 + 1] = t[64:]
        c0, c1 = halves(cen)
        CH[r * 2] = c0
        CH[r * 2 + 1] = c1
        return carry

    lax.fori_loop(0, 32, prep_home, 0, unroll=8)


def pair_kernel(codes_h, widths, chi, hard, own_h, halo_h, feat_h, centre_h, fe, rf, codes, own, halo, L, CH, sem, G, C, acc, *bufs):
    loads = [
        pltpu.make_async_copy(s, d, sem.at[k])
        for k, (s, d) in enumerate(((own_h, own), (halo_h, halo), (codes_h, codes), (feat_h, L), (centre_h, CH)))
    ]
    for c in loads:
        c.start()
    lane = lax.broadcasted_iota(jnp.int32, (8, 128), 1)
    row = lax.broadcasted_iota(jnp.int32, (8, 128), 0)
    low = lane < 64
    for c in loads[:2]:
        c.wait()
    for b in range(5):
        at = [own[pl.ds(32 * c, 32), :] if b == 0 else halo[b - 1, pl.ds(32 * c, 32), :] for c in range(6)]
        if b in (1, 2):
            at[0] = at[0] + (-16.0 if b == 1 else 16.0)
        if b in (3, 4):
            at[1] = at[1] + (-32.0 if b == 3 else 32.0)
        for c, x in enumerate((at[0] * 0.1, at[1] * 0.1, at[2] * 0.1, at[3] * 0.1, at[4] * 0.1, at[5])):
            G[pl.ds(c * NR + b * 32, 32), :] = x
    G[pl.ds(6 * NR, 2 * NR), :] = jnp.zeros((2 * NR, 128), F32)
    DS, VS = bufs[:NB], bufs[NB:]
    for k in range(NB):
        DS[k][...] = jnp.ones_like(DS[k])
        VS[k][...] = jnp.zeros_like(VS[k])

    def halves(x):
        y = pltpu.roll(x, 64, 1)
        return jnp.where(low, x, y), jnp.where(low, y, x)

    def prep(g, carry):
        c0, c1 = halves(G[pl.ds(g, 8, stride=NR), :])
        C[g * 2] = c0
        C[g * 2 + 1] = c1
        return carry

    lax.fori_loop(0, NR, prep, 0, unroll=16)

    def clear(h, carry):
        acc[0, h] = jnp.zeros((64, 128), F32)
        acc[1, h] = jnp.zeros((64, 128), F32)
        return carry

    lax.fori_loop(0, 64, clear, 0, unroll=4)
    C[NT] = jnp.where((row == 3) | (row == 4), 0.0, C[0])

    for c in loads[2:]:
        c.wait()
    types8 = row.astype(F32)
    zeros16 = jnp.zeros((16, 128), BF)
    zeros48 = jnp.zeros((48, 128), BF)
    last = jnp.where(row == 6, 1.0, 0.0)

    def terms(i, D, V):
        for u in range(UN):
            h = lax.shift_right_logical(codes[0, 2 * UN * i + 2 * u], 9)
            xs = [jnp.broadcast_to(V[u, k : k + 1], (8, 128)) for k in range(3, 5)]
            for q in range(8):
                rows = pl.ds(8 * q, 8)
                d = D[u, rows, pl.ds(0, 128)]
                w = D[u, rows, pl.ds(128, 128)]
                r = lax.rsqrt(d)
                e = lax.erf(d * r * w)
                m = jnp.maximum(1.0025 - d, 0.0)
                kk = (e * r) * (m * m)
                acc[0, h, rows] = acc[0, h, rows] + kk * xs[0]
                acc[1, h, rows] = acc[1, h, rows] + kk * xs[1]

    def distances(i, D, V):
        for u in range(UN):
            k1 = codes[0, 2 * UN * i + 2 * u]
            k2 = codes[0, 2 * UN * i + 2 * u + 1]
            h = lax.shift_right_logical(k1, 9)
            v = jnp.where(low, C[k1 & 511], C[k2 & 511]) - CH[h]
            V[u] = v
            f = jnp.where(row < 3, v, jnp.where(row < 6, pltpu.roll(v * v, 3, 0), last))
            s1, s2, s3 = split3(f)
            g = jnp.concatenate([s1, s2, s3, s1, s2, s1], axis=0).astype(BF)
            oh = jnp.where(types8 == v[5:6], 1.0, 0.0)
            oh = jnp.concatenate([oh, oh], axis=0).astype(BF)
            g = jnp.concatenate(
                [jnp.concatenate([g, zeros16], axis=0), jnp.concatenate([zeros48, oh], axis=0)], axis=1
            )
            D[u] = jnp.dot(L[h, :, pl.ds(0, 64)], g, preferred_element_type=F32)

    def step(i, carry):
        for k in range(NB):
            terms(jnp.maximum(NB * i + k - 1, 0), DS[k - 1], VS[k - 1])
            distances(NB * i + k, DS[k], VS[k])
        return carry

    blocks = lax.div(codes[0, 1664] + UN - 1, UN)
    lax.fori_loop(0, lax.div(blocks + NB, NB), step, 0)

    def finish(r, carry):
        for f, ref in enumerate((fe, rf)):
            ref[pl.ds(r, 1), :] = jnp.sum(acc[f, pl.ds(2 * r, 2)].reshape(128, 128).T, axis=0, keepdims=True)
        return carry

    lax.fori_loop(0, 32, finish, 0, unroll=8)
    s2 = jnp.zeros((32, 128), F32)
    ch = jnp.zeros((32, 128), F32)
    eta = jnp.zeros((32, 128), F32)
    for t in range(8):
        hit = own[160:192] == float(t)
        s2 = jnp.where(hit, widths[t] * widths[t], s2)
        ch = jnp.where(hit, chi[t], ch)
        eta = jnp.where(hit, hard[t], eta)
    itself = own[192:224] * (2.0 * lax.erf(0.5 * lax.rsqrt(s2 + s2)))
    residual = rf[...] - itself * own[128:160]
    field = ch + (fe[...] - itself * own[96:128]) + residual
    rf[...] = residual
    fe[...] = field / eta


def pair_call(codes, widths, chi, hard, own, halo, feats, centres):
    sm = pl.BlockSpec(memory_space=pltpu.SMEM)
    vm = pl.BlockSpec(memory_space=pltpu.VMEM)
    hbm = pl.BlockSpec(memory_space=pl.ANY)
    return pl.pallas_call(
        pair_kernel,
        out_shape=[jax.ShapeDtypeStruct((32, 128), F32)] * 2,
        in_specs=[hbm] + [sm] * 3 + [hbm] * 4,
        out_specs=[vm, vm],
        scratch_shapes=[
            pltpu.SMEM(codes.shape, jnp.int32),
            pltpu.VMEM(own.shape, F32),
            pltpu.VMEM(halo.shape, F32),
            pltpu.VMEM(feats.shape, BF),
            pltpu.VMEM(centres.shape, F32),
            pltpu.SemaphoreType.DMA((5,)),
            pltpu.VMEM((8 * NR, 128), F32),
            pltpu.VMEM((NT + 1, 8, 128), F32),
            pltpu.VMEM((2, 64, 64, 128), F32),
            *[pltpu.VMEM((UN, 64, 256), F32)] * NB,
            *[pltpu.VMEM((UN, 8, 128), F32)] * NB,
        ],
        compiler_params=pltpu.CompilerParams(vmem_limit_bytes=60 * 2**20),
        name="pairs",
    )(codes, widths, chi, hard, own, halo, feats, centres)


def exchange_kernel(
    pos_h, aux_h, resid_h, types_h, owner_h, tiles_h, cands_h, hard, widths, count,
    own_h, halo_h, early_h, codes_h, feat_h, centre_h,
    pos, aux, resid, types, owner, tiles, cands, own, early, codes, L, CH, tr, cr, load, send, recv, store,
):
    nb, npl = lax.axis_size("brick"), lax.axis_size("plane")
    b, p = lax.axis_index("brick"), lax.axis_index("plane")
    below, above = lax.rem(b + nb - 1, nb), lax.rem(b + 1, nb)
    barrier = pltpu.get_barrier_semaphore()
    left, right = lax.rem(p + npl - 1, npl), lax.rem(p + 1, npl)
    for d in [(below, p), (above, p), (b, left), (b, right)]:
        pl.semaphore_signal(barrier, inc=1, device_id=d, device_id_type=MESH)
    ins = ((pos_h, pos), (aux_h, aux), (resid_h, resid), (types_h, types), (owner_h, owner), (tiles_h, tiles), (cands_h, cands))
    loads = [pltpu.make_async_copy(x, y, load.at[k]) for k, (x, y) in enumerate(ins)]
    for c in loads:
        c.start()
    for c in loads:
        c.wait()
    own[0:96, :] = pos[...]
    own[96:128, :] = aux[...]
    own[128:160, :] = resid[...]
    ty = types[...].astype(F32)
    own[160:192, :] = ty
    own[192:256, :] = jnp.zeros((64, 128), F32)
    pl.semaphore_wait(barrier, 4)

    def copy(s, d, k, to):
        return pltpu.make_async_remote_copy(
            src_ref=s, dst_ref=d, send_sem=send.at[k], recv_sem=recv.at[k], device_id=to, device_id_type=MESH
        )

    mine = own.at[pl.ds(0, 192)]
    copies = [
        copy(mine, halo_h.at[0], 0, (above, p)),
        copy(mine, halo_h.at[1], 1, (below, p)),
        copy(mine, halo_h.at[2], 2, (b, right)),
        copy(mine, halo_h.at[3], 3, (b, left)),
    ]
    for c in copies:
        c.start()
    inverse = jnp.zeros((32, 128), F32)
    for t in range(8):
        inverse = jnp.where(ty == float(t), 1.0 / jnp.full((32, 128), hard[t], F32), inverse)
    early[0:32, :] = aux[...]
    early[32:64, :] = inverse
    src = lax.broadcasted_iota(jnp.int32, (64, 128), 0)
    lane = lax.broadcasted_iota(jnp.int32, (64, 128), 1) - 32 * p
    inside = (lane >= 0) & (lane < 32)
    ids = jnp.broadcast_to(owner[...].astype(F32), (8, 64))
    evens = jnp.dot(ids, jnp.where(inside & (src == 2 * lane), 1.0, 0.0), precision=HI, preferred_element_type=F32)
    odds = jnp.dot(ids, jnp.where(inside & (src == 2 * lane + 1), 1.0, 0.0), precision=HI, preferred_element_type=F32)
    r8 = lax.broadcasted_iota(jnp.int32, (8, 128), 0)
    early[64:72, :] = jnp.where(r8 == 0, evens, odds)
    home_features(own, widths, L, CH)
    own[192:224, :] = order_pairs(tiles, cands, count, codes, tr, cr)
    outs = ((own, own_h), (early, early_h), (codes, codes_h), (L, feat_h), (CH, centre_h))
    stores = [pltpu.make_async_copy(x, y, store.at[k]) for k, (x, y) in enumerate(outs)]
    for c in stores:
        c.start()
    for c in stores:
        c.wait()
    for c in copies:
        c.wait()


def exchange(pos, aux, resid, types, owner, tiles, cands, hard, widths, count):
    hbm = pl.BlockSpec(memory_space=pl.ANY)
    dma = pltpu.SemaphoreType.DMA
    shape = jax.ShapeDtypeStruct
    ncodes = (SB + 1) * 128
    return pl.pallas_call(
        exchange_kernel,
        out_shape=[
            shape((256, 128), F32),
            shape((4, 192, 128), F32),
            shape((72, 128), F32),
            shape((1, ncodes), jnp.int32),
            shape((64, 64, 128), BF),
            shape((64, 8, 128), F32),
        ],
        in_specs=[hbm] * 7 + [pl.BlockSpec(memory_space=pltpu.SMEM)] * 3,
        out_specs=[hbm] * 6,
        scratch_shapes=[pltpu.VMEM(x.shape, x.dtype) for x in (pos, aux, resid, types, owner, tiles, cands)]
        + [
            pltpu.VMEM((256, 128), F32),
            pltpu.VMEM((72, 128), F32),
            pltpu.VMEM((1, ncodes), jnp.int32),
            pltpu.VMEM((64, 64, 128), BF),
            pltpu.VMEM((64, 8, 128), F32),
            pltpu.VMEM((128, 128), F32),
            pltpu.VMEM((16, 128), F32),
            dma((7,)), dma((4,)), dma((4,)), dma((5,)),
        ],
        compiler_params=pltpu.CompilerParams(collective_id=0, has_side_effects=True, vmem_limit_bytes=60 * 2**20),
        name="exchange",
    )(pos, aux, resid, types, owner, tiles, cands, hard, widths, count)


LINE, SHEET = 16, 32


def level_kernel(fe_h, early_h, prev_h, charges, nxt, fe, early, prev, load, got, near, far, s1, r1, s2, r2, s3, r3, ready):
    npl = lax.axis_size("plane")
    b, p = lax.axis_index("brick"), lax.axis_index("plane")
    zhi = lax.rem(lax.div(b, 8), 4)
    z = npl * zhi + p
    w = 8 * lax.div(b, 32) + lax.rem(b, 8)

    def line(q):
        return (b + 8 * (lax.div(q, npl) - zhi), lax.rem(q, npl))

    def sheet(q):
        return (32 * lax.div(q, 8) + 8 * zhi + lax.rem(q, 8), p)

    lines = [lax.rem(z + k, LINE) for k in range(1, LINE)]
    sheets = [lax.rem(w + k, SHEET) for k in range(1, SHEET)]
    mates = [lax.rem(p + k, npl) for k in range(1, npl)]
    barrier = pltpu.get_barrier_semaphore()
    for k in (1, 2, 3, 4, 12, 13, 14, 15):
        pl.semaphore_signal(barrier, inc=1, device_id=line(lax.rem(z + k, LINE)), device_id_type=MESH)
    for q in sheets:
        pl.semaphore_signal(barrier, inc=1, device_id=sheet(q), device_id_type=MESH)
    ins = ((fe_h, fe), (early_h, early), (prev_h, prev))
    loads = [pltpu.make_async_copy(x, y, load.at[k]) for k, (x, y) in enumerate(ins)]
    for c in loads:
        c.start()
    for c in loads:
        c.wait()
    got[p, 0:72, :] = early[...]
    got[p, 72:104, :] = fe[...]

    def fold(x):
        s = x[0:8] + x[8:16] + x[16:24] + x[24:32]
        return s[0:4] + s[4:8]

    near[w] = jnp.concatenate([fold(early[0:32, :] + fe[...]), fold(early[32:64, :])], axis=0)
    pl.semaphore_wait(barrier, 8 + SHEET - 1)
    for k in (4, 12):
        pl.semaphore_signal(ready, inc=1, device_id=line(lax.rem(z + k, LINE)), device_id_type=MESH)

    def copy(s, d, ss, rs, to):
        return pltpu.make_async_remote_copy(
            src_ref=s, dst_ref=d, send_sem=ss, recv_sem=rs, device_id=to, device_id_type=MESH
        )

    first = [copy(near.at[w], near.at[w], s1.at[k], r1.at[k], sheet(q)) for k, q in enumerate(sheets)]
    for c in first:
        c.start()
    tiles = [copy(got.at[p], got.at[p], s2.at[k], r2.at[k], (b, q)) for k, q in enumerate(mates)]
    for c in tiles:
        c.start()
    for c in first:
        c.wait()
    total = near[0]
    for k in range(1, SHEET):
        total = total + near[k]
    far[z] = total
    pl.semaphore_wait(ready, 2)
    second = [copy(far.at[z], far.at[z], s3.at[k], r3.at[k], line(q)) for k, q in enumerate(lines)]
    for c in second:
        c.start()
    for c in tiles:
        c.wait()
    evens = got[0, 64:65, :] + got[1, 64:65, :] + got[2, 64:65, :] + got[3, 64:65, :]
    odds = got[0, 65:66, :] + got[1, 65:66, :] + got[2, 65:66, :] + got[3, 65:66, :]
    slot = (64 * p + 2 * lax.broadcasted_iota(jnp.int32, (32, 128), 0)).astype(F32)
    place = jnp.concatenate(
        [
            jnp.where(evens == slot, 1.0, 0.0),
            jnp.where(odds == slot + 1.0, 1.0, 0.0),
            jnp.where(evens == slot + 1.0, 1.0, 0.0),
            jnp.where(odds == slot, 1.0, 0.0),
        ],
        axis=0,
    )
    low = lax.broadcasted_iota(jnp.int32, (32, 128), 1) < 64

    def placed(x):
        y = jnp.dot(place, x, precision=HI, preferred_element_type=F32)
        return jnp.where(low, y[0:32], y[32:64]) + pltpu.roll(jnp.where(low, y[64:96], y[96:128]), 64, 1)

    aux = placed(got[:, 0:32, :].reshape(128, 128))
    inverse = placed(got[:, 32:64, :].reshape(128, 128))
    moved = placed(got[:, 72:104, :].reshape(128, 128))
    for c in second:
        c.wait()
    total = far[0]
    for k in range(1, LINE):
        total = total + far[k]
    top = jnp.sum(jnp.sum(total[0:4], axis=1, keepdims=True), axis=0, keepdims=True)
    bottom = jnp.sum(jnp.sum(total[4:8], axis=1, keepdims=True), axis=0, keepdims=True)
    level = jnp.broadcast_to(top / bottom, (32, 128))
    charges[...] = level * early[32:64, :] - fe[...]
    nxt[...] = 2.0 * aux - prev[...] + kappa * (level * inverse - moved - aux)


def finish(fe, early, prev):
    vm = pl.BlockSpec(memory_space=pltpu.VMEM)
    dma = pltpu.SemaphoreType.DMA
    return pl.pallas_call(
        level_kernel,
        out_shape=[jax.ShapeDtypeStruct((32, 128), F32)] * 2,
        in_specs=[pl.BlockSpec(memory_space=pl.ANY)] * 3,
        out_specs=[vm] * 2,
        scratch_shapes=[
            pltpu.VMEM((32, 128), F32),
            pltpu.VMEM((72, 128), F32),
            pltpu.VMEM((32, 128), F32),
            dma((3,)),
            pltpu.VMEM((4, 104, 128), F32),
            pltpu.VMEM((SHEET, 8, 128), F32),
            pltpu.VMEM((LINE, 8, 128), F32),
            dma((SHEET - 1,)), dma((SHEET - 1,)), dma((3,)), dma((3,)), dma((LINE - 1,)), dma((LINE - 1,)),
            pltpu.SemaphoreType.REGULAR,
        ],
        compiler_params=pltpu.CompilerParams(collective_id=1, has_side_effects=True, vmem_limit_bytes=60 * 2**20),
        name="level",
    )(fe, early, prev)


def on_device(positions, aux, aux_prev, resid, types, pair_tiles, pair_cands, pair_count, owner_tile, electroneg, hardness, widths):
    own, halo, early, codes, feats, centres = exchange(
        positions.transpose(0, 2, 1, 3).reshape(96, 128),
        aux.reshape(32, 128),
        resid.reshape(32, 128),
        types.reshape(32, 128),
        owner_tile.reshape(1, -1),
        pair_tiles.reshape(1, -1),
        pair_cands.reshape(1, -1),
        hardness,
        widths,
        pair_count,
    )
    fe, rf = pair_call(codes, widths, electroneg, hardness, own, halo, feats, centres)
    charges, nxt = finish(fe, early, aux_prev.reshape(32, 128))
    return charges.reshape(aux.shape), nxt.reshape(aux.shape), rf.reshape(aux.shape)


def solution(mesh):
    s4, s3, s2 = P("brick", "plane", None, None), P("brick", "plane", None), P("brick", "plane")
    return jax.shard_map(
        on_device,
        mesh=mesh,
        in_specs=(s4, s3, s3, s3, s3, s3, s3, s2, s3, P(), P(), P()),
        out_specs=(s3, s3, s3),
        check_vma=False,
    )
```

```python
import functools

import jax
import jax.numpy as jnp
from jax import lax
from jax.experimental import pallas as pl
from jax.experimental.pallas import tpu as pltpu
from jax.sharding import PartitionSpec as P

F32 = jnp.float32
BF = jnp.bfloat16
HI = lax.Precision.HIGHEST
MESH = pl.DeviceIdType.MESH
kappa = 1.86

PB = 12
SB = 13
NT = 320


def order_pairs(tiles, cands, count, codes, tr, cr):
    n = tiles.shape[1]
    one = lax.broadcasted_iota(jnp.int32, (1, 128), 1)
    tr[...] = jnp.full((128, 128), 64.0, F32)
    cr[...] = jnp.zeros((16, 128), F32)
    for j in range(PB):
        w = min(128, n - 128 * j)
        tr[j : j + 1, :w] = tiles[:, 128 * j : 128 * j + w].astype(F32)
        cr[j : j + 1, :w] = cands[:, 128 * j : 128 * j + w].astype(F32)
    prow = lax.broadcasted_iota(jnp.int32, (16, 128), 0) * 128 + lax.broadcasted_iota(jnp.int32, (16, 128), 1)
    used = prow < count[0, 0]
    t = jnp.where(used, tr[:16], 64.0)
    c = jnp.where(used, cr[...], 0.0)
    tr[:16] = t
    tcol = tr[...].T
    lane = lax.broadcasted_iota(jnp.int32, (128, 128), 1)
    rowi = lax.broadcasted_iota(jnp.int32, (128, 128), 0)
    lanef = lane.astype(F32)
    before = jnp.where(lane < rowi, 1.0, 0.0).astype(BF)
    hot = [tcol[:, j : j + 1] == lanef for j in range(PB)]
    hotf = [jnp.where(h, 1.0, 0.0) for h in hot]
    sums = [jnp.sum(h, axis=0, keepdims=True) for h in hotf]
    counts = sum(sums)
    counts = jnp.where(one < 64, counts, 0.0)
    half = jnp.floor((counts + 1.0) * 0.5)
    starts = 2.0 * jnp.dot(jnp.broadcast_to(half, (8, 128)), jnp.where(rowi < lane, 1.0, 0.0), precision=HI, preferred_element_type=F32)[:1]
    starts = jnp.where(one < 64, starts, 8192.0)
    codes[:, SB * 128 :] = jnp.broadcast_to(jnp.sum(half, axis=1, keepdims=True), (1, 128)).astype(jnp.int32)
    out = jnp.zeros((8, SB * 128), F32)
    slot = lax.broadcasted_iota(jnp.int32, (128, SB * 128), 1).astype(F32)
    selfrow = jnp.zeros((1, 128), F32)
    e = float(NT) - c
    e = jnp.where(used, e, 0.0)
    ehi = jnp.floor(e * 0.5)
    elo = e - 2.0 * ehi
    same = jnp.where(t == c, 1.0, 0.0)
    r8 = lax.broadcasted_iota(jnp.int32, (8, 128), 0)
    for j in range(PB):
        rank = jnp.dot(before, hotf[j].astype(BF), preferred_element_type=F32)
        pos = jnp.sum(jnp.where(hot[j], rank + starts, 0.0), axis=1, keepdims=True)
        starts = starts + sums[j]
        vals = jnp.where(r8 == 0, ehi[j : j + 1], jnp.where(r8 == 1, elo[j : j + 1], jnp.where(r8 == 2, t[j : j + 1], same[j : j + 1])))
        put = jnp.where(pos == slot, 1.0, 0.0).astype(BF)
        out = out + jnp.dot(vals.astype(BF), put, preferred_element_type=F32)
        selfrow = selfrow + jnp.dot(vals.astype(BF), hotf[j].astype(BF), preferred_element_type=F32)[3:4]
    code = out[2:3] * 512.0 + (float(NT) - (2.0 * out[0:1] + out[1:2]))
    codes[:, : SB * 128] = code.astype(jnp.int32)
    lane32 = lax.broadcasted_iota(jnp.int32, (32, 128), 1)
    row32 = lax.broadcasted_iota(jnp.int32, (32, 128), 0)
    n = jnp.broadcast_to(selfrow, (32, 128))
    even = jnp.sum(jnp.where(lane32 == 2 * row32, n, 0.0), axis=1, keepdims=True)
    odd = jnp.sum(jnp.where(lane32 == 2 * row32 + 1, n, 0.0), axis=1, keepdims=True)
    return jnp.where(lane32 < 64, even, odd)


NR = 160
UN = 8
NB = 2


def split3(x):
    a = x.astype(BF).astype(F32)
    r = x - a
    b = r.astype(BF).astype(F32)
    return a, b, r - b


def home_features(own, widths, L, CH):
    lane = lax.broadcasted_iota(jnp.int32, (8, 128), 1)
    row = lax.broadcasted_iota(jnp.int32, (8, 128), 0)
    low = lane < 64

    def halves(x):
        y = pltpu.roll(x, 64, 1)
        return jnp.where(low, x, y), jnp.where(low, y, x)

    st = jnp.zeros((8, 128), F32)
    for t in range(8):
        st = jnp.where(row == t, widths[t], st)
    st = st * st * 0.01

    def prep_home(r, carry):
        v = own[pl.ds(r, 8, stride=32), :]
        v = jnp.where(row < 3, v * 0.1, v)
        x = v[:, 0:1]
        y = v[:, 64:65]
        cen = jnp.where(low, jnp.broadcast_to(x, (8, 128)), jnp.broadcast_to(y, (8, 128)))
        cen = jnp.where(row < 3, cen, 0.0)
        a = v - cen
        n = jnp.sum(jnp.where(row < 3, a * a, 0.0), axis=0, keepdims=True) + 0.0025
        f = jnp.where(row < 3, -2.0 * a, jnp.where(row < 6, 1.0, jnp.where(row == 6, n, 0.0)))
        f1, f2, f3 = split3(f)
        si = jnp.sum(jnp.where(row.astype(F32) == v[5:6], st, 0.0), axis=0, keepdims=True)
        w1, w2, w3 = split3(lax.rsqrt(st + si))
        t = jnp.concatenate([f1, f1, f1, f2, f2, f3, w1, w2, jnp.zeros((64, 128), F32)], axis=0).T.astype(BF)
        L[r * 2] = t[:64]
        L[r * 2 + 1] = t[64:]
        c0, c1 = halves(cen)
        CH[r * 2] = c0
        CH[r * 2 + 1] = c1
        return carry

    lax.fori_loop(0, 32, prep_home, 0, unroll=8)


def pair_kernel(codes_h, widths, chi, hard, own_h, halo_h, feat_h, centre_h, fe, rf, codes, own, halo, L, CH, sem, G, C, acc, *bufs):
    loads = [
        pltpu.make_async_copy(s, d, sem.at[k])
        for k, (s, d) in enumerate(((own_h, own), (halo_h, halo), (codes_h, codes), (feat_h, L), (centre_h, CH)))
    ]
    for c in loads:
        c.start()
    lane = lax.broadcasted_iota(jnp.int32, (8, 128), 1)
    row = lax.broadcasted_iota(jnp.int32, (8, 128), 0)
    low = lane < 64
    for c in loads[:2]:
        c.wait()
    for b in range(5):
        at = [own[pl.ds(32 * c, 32), :] if b == 0 else halo[b - 1, pl.ds(32 * c, 32), :] for c in range(6)]
        if b in (1, 2):
            at[0] = at[0] + (-16.0 if b == 1 else 16.0)
        if b in (3, 4):
            at[1] = at[1] + (-32.0 if b == 3 else 32.0)
        for c, x in enumerate((at[0] * 0.1, at[1] * 0.1, at[2] * 0.1, at[3] * 0.1, at[4] * 0.1, at[5])):
            G[pl.ds(c * NR + b * 32, 32), :] = x
    G[pl.ds(6 * NR, 2 * NR), :] = jnp.zeros((2 * NR, 128), F32)
    DS, VS = bufs[:NB], bufs[NB:]
    for k in range(NB):
        DS[k][...] = jnp.ones_like(DS[k])
        VS[k][...] = jnp.zeros_like(VS[k])

    def halves(x):
        y = pltpu.roll(x, 64, 1)
        return jnp.where(low, x, y), jnp.where(low, y, x)

    def prep(g, carry):
        c0, c1 = halves(G[pl.ds(g, 8, stride=NR), :])
        C[g * 2] = c0
        C[g * 2 + 1] = c1
        return carry

    lax.fori_loop(0, NR, prep, 0, unroll=16)

    def clear(h, carry):
        acc[0, h] = jnp.zeros((64, 128), F32)
        acc[1, h] = jnp.zeros((64, 128), F32)
        return carry

    lax.fori_loop(0, 64, clear, 0, unroll=4)
    C[NT] = jnp.where((row == 3) | (row == 4), 0.0, C[0])

    for c in loads[2:]:
        c.wait()
    types8 = row.astype(F32)
    zeros16 = jnp.zeros((16, 128), BF)
    zeros48 = jnp.zeros((48, 128), BF)
    last = jnp.where(row == 6, 1.0, 0.0)

    def terms(i, D, V):
        for u in range(UN):
            h = lax.shift_right_logical(codes[0, 2 * UN * i + 2 * u], 9)
            xs = [jnp.broadcast_to(V[u, k : k + 1], (8, 128)) for k in range(3, 5)]
            for q in range(8):
                rows = pl.ds(8 * q, 8)
                d = D[u, rows, pl.ds(0, 128)]
                w = D[u, rows, pl.ds(128, 128)]
                r = lax.rsqrt(d)
                e = lax.erf(d * r * w)
                m = jnp.maximum(1.0025 - d, 0.0)
                kk = (e * r) * (m * m)
                acc[0, h, rows] = acc[0, h, rows] + kk * xs[0]
                acc[1, h, rows] = acc[1, h, rows] + kk * xs[1]

    def distances(i, D, V):
        for u in range(UN):
            k1 = codes[0, 2 * UN * i + 2 * u]
            k2 = codes[0, 2 * UN * i + 2 * u + 1]
            h = lax.shift_right_logical(k1, 9)
            v = jnp.where(low, C[k1 & 511], C[k2 & 511]) - CH[h]
            V[u] = v
            f = jnp.where(row < 3, v, jnp.where(row < 6, pltpu.roll(v * v, 3, 0), last))
            s1, s2, s3 = split3(f)
            g = jnp.concatenate([s1, s2, s3, s1, s2, s1], axis=0).astype(BF)
            oh = jnp.where(types8 == v[5:6], 1.0, 0.0)
            oh = jnp.concatenate([oh, oh], axis=0).astype(BF)
            g = jnp.concatenate(
                [jnp.concatenate([g, zeros16], axis=0), jnp.concatenate([zeros48, oh], axis=0)], axis=1
            )
            D[u] = jnp.dot(L[h, :, pl.ds(0, 64)], g, preferred_element_type=F32)

    def step(i, carry):
        for k in range(NB):
            terms(jnp.maximum(NB * i + k - 1, 0), DS[k - 1], VS[k - 1])
            distances(NB * i + k, DS[k], VS[k])
        return carry

    blocks = lax.div(codes[0, 1664] + UN - 1, UN)
    lax.fori_loop(0, lax.div(blocks + NB, NB), step, 0)

    def finish(r, carry):
        for f, ref in enumerate((fe, rf)):
            ref[pl.ds(r, 1), :] = jnp.sum(acc[f, pl.ds(2 * r, 2)].reshape(128, 128).T, axis=0, keepdims=True)
        return carry

    lax.fori_loop(0, 32, finish, 0, unroll=8)
    s2 = jnp.zeros((32, 128), F32)
    ch = jnp.zeros((32, 128), F32)
    eta = jnp.zeros((32, 128), F32)
    for t in range(8):
        hit = own[160:192] == float(t)
        s2 = jnp.where(hit, widths[t] * widths[t], s2)
        ch = jnp.where(hit, chi[t], ch)
        eta = jnp.where(hit, hard[t], eta)
    itself = own[192:224] * (2.0 * lax.erf(0.5 * lax.rsqrt(s2 + s2)))
    residual = rf[...] - itself * own[128:160]
    field = ch + (fe[...] - itself * own[96:128]) + residual
    rf[...] = residual
    fe[...] = field / eta


def pair_call(codes, widths, chi, hard, own, halo, feats, centres):
    sm = pl.BlockSpec(memory_space=pltpu.SMEM)
    vm = pl.BlockSpec(memory_space=pltpu.VMEM)
    hbm = pl.BlockSpec(memory_space=pl.ANY)
    return pl.pallas_call(
        pair_kernel,
        out_shape=[jax.ShapeDtypeStruct((32, 128), F32)] * 2,
        in_specs=[hbm] + [sm] * 3 + [hbm] * 4,
        out_specs=[vm, vm],
        scratch_shapes=[
            pltpu.SMEM(codes.shape, jnp.int32),
            pltpu.VMEM(own.shape, F32),
            pltpu.VMEM(halo.shape, F32),
            pltpu.VMEM(feats.shape, BF),
            pltpu.VMEM(centres.shape, F32),
            pltpu.SemaphoreType.DMA((5,)),
            pltpu.VMEM((8 * NR, 128), F32),
            pltpu.VMEM((NT + 1, 8, 128), F32),
            pltpu.VMEM((2, 64, 64, 128), F32),
            *[pltpu.VMEM((UN, 64, 256), F32)] * NB,
            *[pltpu.VMEM((UN, 8, 128), F32)] * NB,
        ],
        compiler_params=pltpu.CompilerParams(vmem_limit_bytes=60 * 2**20),
        name="pairs",
    )(codes, widths, chi, hard, own, halo, feats, centres)


def exchange_kernel(
    pos_h, aux_h, resid_h, types_h, owner_h, tiles_h, cands_h, hard, widths, count,
    own_h, halo_h, early_h, codes_h, feat_h, centre_h,
    pos, aux, resid, types, owner, tiles, cands, own, early, codes, L, CH, tr, cr, load, send, recv, store,
):
    nb, npl = lax.axis_size("brick"), lax.axis_size("plane")
    b, p = lax.axis_index("brick"), lax.axis_index("plane")
    below, above = lax.rem(b + nb - 1, nb), lax.rem(b + 1, nb)
    barrier = pltpu.get_barrier_semaphore()
    left, right = lax.rem(p + npl - 1, npl), lax.rem(p + 1, npl)
    for d in [(below, p), (above, p), (b, left), (b, right)]:
        pl.semaphore_signal(barrier, inc=1, device_id=d, device_id_type=MESH)
    ins = ((pos_h, pos), (aux_h, aux), (resid_h, resid), (types_h, types), (owner_h, owner), (tiles_h, tiles), (cands_h, cands))
    loads = [pltpu.make_async_copy(x, y, load.at[k]) for k, (x, y) in enumerate(ins)]
    for c in loads:
        c.start()
    for c in loads:
        c.wait()
    own[0:96, :] = pos[...]
    own[96:128, :] = aux[...]
    own[128:160, :] = resid[...]
    ty = types[...].astype(F32)
    own[160:192, :] = ty
    own[192:256, :] = jnp.zeros((64, 128), F32)
    pl.semaphore_wait(barrier, 4)

    def copy(s, d, k, to):
        return pltpu.make_async_remote_copy(
            src_ref=s, dst_ref=d, send_sem=send.at[k], recv_sem=recv.at[k], device_id=to, device_id_type=MESH
        )

    mine = own.at[pl.ds(0, 192)]
    copies = [
        copy(mine, halo_h.at[0], 0, (above, p)),
        copy(mine, halo_h.at[1], 1, (below, p)),
        copy(mine, halo_h.at[2], 2, (b, right)),
        copy(mine, halo_h.at[3], 3, (b, left)),
    ]
    for c in copies:
        c.start()
    inverse = jnp.zeros((32, 128), F32)
    for t in range(8):
        inverse = jnp.where(ty == float(t), 1.0 / jnp.full((32, 128), hard[t], F32), inverse)
    early[0:32, :] = aux[...]
    early[32:64, :] = inverse
    src = lax.broadcasted_iota(jnp.int32, (64, 128), 0)
    lane = lax.broadcasted_iota(jnp.int32, (64, 128), 1) - 32 * p
    inside = (lane >= 0) & (lane < 32)
    ids = jnp.broadcast_to(owner[...].astype(F32), (8, 64))
    evens = jnp.dot(ids, jnp.where(inside & (src == 2 * lane), 1.0, 0.0), precision=HI, preferred_element_type=F32)
    odds = jnp.dot(ids, jnp.where(inside & (src == 2 * lane + 1), 1.0, 0.0), precision=HI, preferred_element_type=F32)
    r8 = lax.broadcasted_iota(jnp.int32, (8, 128), 0)
    early[64:72, :] = jnp.where(r8 == 0, evens, odds)
    home_features(own, widths, L, CH)
    own[192:224, :] = order_pairs(tiles, cands, count, codes, tr, cr)
    outs = ((own, own_h), (early, early_h), (codes, codes_h), (L, feat_h), (CH, centre_h))
    stores = [pltpu.make_async_copy(x, y, store.at[k]) for k, (x, y) in enumerate(outs)]
    for c in stores:
        c.start()
    for c in stores:
        c.wait()
    for c in copies:
        c.wait()


def exchange(pos, aux, resid, types, owner, tiles, cands, hard, widths, count):
    hbm = pl.BlockSpec(memory_space=pl.ANY)
    dma = pltpu.SemaphoreType.DMA
    shape = jax.ShapeDtypeStruct
    ncodes = (SB + 1) * 128
    return pl.pallas_call(
        exchange_kernel,
        out_shape=[
            shape((256, 128), F32),
            shape((4, 192, 128), F32),
            shape((72, 128), F32),
            shape((1, ncodes), jnp.int32),
            shape((64, 64, 128), BF),
            shape((64, 8, 128), F32),
        ],
        in_specs=[hbm] * 7 + [pl.BlockSpec(memory_space=pltpu.SMEM)] * 3,
        out_specs=[hbm] * 6,
        scratch_shapes=[pltpu.VMEM(x.shape, x.dtype) for x in (pos, aux, resid, types, owner, tiles, cands)]
        + [
            pltpu.VMEM((256, 128), F32),
            pltpu.VMEM((72, 128), F32),
            pltpu.VMEM((1, ncodes), jnp.int32),
            pltpu.VMEM((64, 64, 128), BF),
            pltpu.VMEM((64, 8, 128), F32),
            pltpu.VMEM((128, 128), F32),
            pltpu.VMEM((16, 128), F32),
            dma((7,)), dma((4,)), dma((4,)), dma((5,)),
        ],
        compiler_params=pltpu.CompilerParams(collective_id=0, has_side_effects=True, vmem_limit_bytes=60 * 2**20),
        name="exchange",
    )(pos, aux, resid, types, owner, tiles, cands, hard, widths, count)


LINE, SHEET = 16, 32


def level_kernel(fe_h, early_h, out, fe, early, load, got, near, far, s1, r1, s2, r2, s3, r3, ready):
    npl = lax.axis_size("plane")
    b, p = lax.axis_index("brick"), lax.axis_index("plane")
    zhi = lax.rem(lax.div(b, 8), 4)
    z = npl * zhi + p
    w = 8 * lax.div(b, 32) + lax.rem(b, 8)

    def line(q):
        return (b + 8 * (lax.div(q, npl) - zhi), lax.rem(q, npl))

    def sheet(q):
        return (32 * lax.div(q, 8) + 8 * zhi + lax.rem(q, 8), p)

    lines = [lax.rem(z + k, LINE) for k in range(1, LINE)]
    sheets = [lax.rem(w + k, SHEET) for k in range(1, SHEET)]
    mates = [lax.rem(p + k, npl) for k in range(1, npl)]
    barrier = pltpu.get_barrier_semaphore()
    for k in (1, 2, 3, 4, 12, 13, 14, 15):
        pl.semaphore_signal(barrier, inc=1, device_id=line(lax.rem(z + k, LINE)), device_id_type=MESH)
    for q in sheets:
        pl.semaphore_signal(barrier, inc=1, device_id=sheet(q), device_id_type=MESH)
    ins = ((fe_h, fe), (early_h, early))
    loads = [pltpu.make_async_copy(x, y, load.at[k]) for k, (x, y) in enumerate(ins)]
    for c in loads:
        c.start()
    for c in loads:
        c.wait()
    got[p, 0:72, :] = early[...]
    got[p, 72:104, :] = fe[...]

    def fold(x):
        s = jnp.sum(x, axis=0, keepdims=True)
        return s + pltpu.roll(s, 64, 1)

    first_half = lax.broadcasted_iota(jnp.int32, (1, 128), 1) < 64
    near[w] = jnp.where(first_half, fold(early[0:32, :] + fe[...]), fold(early[32:64, :]))
    pl.semaphore_wait(barrier, 8 + SHEET - 1)
    for k in (4, 12):
        pl.semaphore_signal(ready, inc=1, device_id=line(lax.rem(z + k, LINE)), device_id_type=MESH)

    def copy(s, d, ss, rs, to):
        return pltpu.make_async_remote_copy(
            src_ref=s, dst_ref=d, send_sem=ss, recv_sem=rs, device_id=to, device_id_type=MESH
        )

    first = [copy(near.at[w], near.at[w], s1.at[k], r1.at[k], sheet(q)) for k, q in enumerate(sheets)]
    for c in first:
        c.start()
    tiles = [copy(got.at[p], got.at[p], s2.at[k], r2.at[k], (b, q)) for k, q in enumerate(mates)]
    for c in tiles:
        c.start()
    for c in first:
        c.wait()
    total = near[0]
    for k in range(1, SHEET):
        total = total + near[k]
    far[z] = total
    pl.semaphore_wait(ready, 2)
    second = [copy(far.at[z], far.at[z], s3.at[k], r3.at[k], line(q)) for k, q in enumerate(lines)]
    for c in second:
        c.start()
    for c in tiles:
        c.wait()
    evens = got[0, 64:65, :] + got[1, 64:65, :] + got[2, 64:65, :] + got[3, 64:65, :]
    odds = got[0, 65:66, :] + got[1, 65:66, :] + got[2, 65:66, :] + got[3, 65:66, :]
    slot = (64 * p + 2 * lax.broadcasted_iota(jnp.int32, (32, 128), 0)).astype(F32)
    place = jnp.concatenate(
        [
            jnp.where(evens == slot, 1.0, 0.0),
            jnp.where(odds == slot + 1.0, 1.0, 0.0),
            jnp.where(evens == slot + 1.0, 1.0, 0.0),
            jnp.where(odds == slot, 1.0, 0.0),
        ],
        axis=0,
    )
    low = lax.broadcasted_iota(jnp.int32, (32, 128), 1) < 64

    def placed(x):
        y = jnp.dot(place, x, precision=HI, preferred_element_type=F32)
        return jnp.where(low, y[0:32], y[32:64]) + pltpu.roll(jnp.where(low, y[64:96], y[96:128]), 64, 1)

    aux = placed(got[:, 0:32, :].reshape(128, 128))
    inverse = placed(got[:, 32:64, :].reshape(128, 128))
    moved = placed(got[:, 72:104, :].reshape(128, 128))
    out[0:32, :] = 2.0 * aux - kappa * (moved + aux)
    out[32:64, :] = kappa * inverse
    for c in second:
        c.wait()
    total = far[0]
    for k in range(1, LINE):
        total = total + far[k]
    top = jnp.sum(jnp.where(first_half, total, 0.0), axis=1, keepdims=True)
    bottom = jnp.sum(jnp.where(first_half, 0.0, total), axis=1, keepdims=True)
    out[64:72, :] = jnp.broadcast_to(top / bottom, (8, 128))


def finish(fe, early):
    vm = pl.BlockSpec(memory_space=pltpu.VMEM)
    dma = pltpu.SemaphoreType.DMA
    return pl.pallas_call(
        level_kernel,
        out_shape=jax.ShapeDtypeStruct((72, 128), F32),
        in_specs=[pl.BlockSpec(memory_space=pl.ANY)] * 2,
        out_specs=vm,
        scratch_shapes=[
            pltpu.VMEM((32, 128), F32),
            pltpu.VMEM((72, 128), F32),
            dma((2,)),
            pltpu.VMEM((4, 104, 128), F32),
            pltpu.VMEM((SHEET, 1, 128), F32),
            pltpu.VMEM((LINE, 1, 128), F32),
            dma((SHEET - 1,)), dma((SHEET - 1,)), dma((3,)), dma((3,)), dma((LINE - 1,)), dma((LINE - 1,)),
            pltpu.SemaphoreType.REGULAR,
        ],
        compiler_params=pltpu.CompilerParams(collective_id=1, has_side_effects=True, vmem_limit_bytes=60 * 2**20),
        name="level",
    )(fe, early)


def on_device(positions, aux, aux_prev, resid, types, pair_tiles, pair_cands, pair_count, owner_tile, electroneg, hardness, widths):
    own, halo, early, codes, feats, centres = exchange(
        positions.transpose(0, 2, 1, 3).reshape(96, 128),
        aux.reshape(32, 128),
        resid.reshape(32, 128),
        types.reshape(32, 128),
        owner_tile.reshape(1, -1),
        pair_tiles.reshape(1, -1),
        pair_cands.reshape(1, -1),
        hardness,
        widths,
        pair_count,
    )
    fe, rf = pair_call(codes, widths, electroneg, hardness, own, halo, feats, centres)
    out = finish(fe, early)
    level = out[64, 0]
    charges = level * early[32:64] - fe
    nxt = out[0:32] - aux_prev.reshape(32, 128) + level * out[32:64]
    return charges.reshape(aux.shape), nxt.reshape(aux.shape), rf.reshape(aux.shape)


def solution(mesh):
    s4, s3, s2 = P("brick", "plane", None, None), P("brick", "plane", None), P("brick", "plane")
    return jax.shard_map(
        on_device,
        mesh=mesh,
        in_specs=(s4, s3, s3, s3, s3, s3, s3, s2, s3, P(), P(), P()),
        out_specs=(s3, s3, s3),
        check_vma=False,
    )
```

```python
import functools

import jax
import jax.numpy as jnp
from jax import lax
from jax.experimental import pallas as pl
from jax.experimental.pallas import tpu as pltpu
from jax.sharding import PartitionSpec as P

F32 = jnp.float32
BF = jnp.bfloat16
HI = lax.Precision.HIGHEST
MESH = pl.DeviceIdType.MESH
kappa = 1.86

PB = 12
SB = 13
NT = 320


def order_pairs(tiles, cands, count, codes, tr, cr):
    n = tiles.shape[1]
    one = lax.broadcasted_iota(jnp.int32, (1, 128), 1)
    tr[...] = jnp.full((128, 128), 64.0, F32)
    cr[...] = jnp.zeros((16, 128), F32)
    for j in range(PB):
        w = min(128, n - 128 * j)
        tr[j : j + 1, :w] = tiles[:, 128 * j : 128 * j + w].astype(F32)
        cr[j : j + 1, :w] = cands[:, 128 * j : 128 * j + w].astype(F32)
    prow = lax.broadcasted_iota(jnp.int32, (16, 128), 0) * 128 + lax.broadcasted_iota(jnp.int32, (16, 128), 1)
    used = prow < count[0, 0]
    t = jnp.where(used, tr[:16], 64.0)
    c = jnp.where(used, cr[...], 0.0)
    tr[:16] = t
    tcol = tr[...].T
    lane = lax.broadcasted_iota(jnp.int32, (128, 128), 1)
    rowi = lax.broadcasted_iota(jnp.int32, (128, 128), 0)
    lanef = lane.astype(F32)
    before = jnp.where(lane < rowi, 1.0, 0.0).astype(BF)
    hot = [tcol[:, j : j + 1] == lanef for j in range(PB)]
    hotf = [jnp.where(h, 1.0, 0.0) for h in hot]
    sums = [jnp.sum(h, axis=0, keepdims=True) for h in hotf]
    counts = sum(sums)
    counts = jnp.where(one < 64, counts, 0.0)
    half = jnp.floor((counts + 1.0) * 0.5)
    starts = 2.0 * jnp.dot(jnp.broadcast_to(half, (8, 128)), jnp.where(rowi < lane, 1.0, 0.0), precision=HI, preferred_element_type=F32)[:1]
    starts = jnp.where(one < 64, starts, 8192.0)
    codes[:, SB * 128 :] = jnp.broadcast_to(jnp.sum(half, axis=1, keepdims=True), (1, 128)).astype(jnp.int32)
    out = jnp.zeros((8, SB * 128), F32)
    slot = lax.broadcasted_iota(jnp.int32, (128, SB * 128), 1).astype(F32)
    selfrow = jnp.zeros((1, 128), F32)
    e = float(NT) - c
    e = jnp.where(used, e, 0.0)
    ehi = jnp.floor(e * 0.5)
    elo = e - 2.0 * ehi
    same = jnp.where(t == c, 1.0, 0.0)
    r8 = lax.broadcasted_iota(jnp.int32, (8, 128), 0)
    for j in range(PB):
        rank = jnp.dot(before, hotf[j].astype(BF), preferred_element_type=F32)
        pos = jnp.sum(jnp.where(hot[j], rank + starts, 0.0), axis=1, keepdims=True)
        starts = starts + sums[j]
        vals = jnp.where(r8 == 0, ehi[j : j + 1], jnp.where(r8 == 1, elo[j : j + 1], jnp.where(r8 == 2, t[j : j + 1], same[j : j + 1])))
        put = jnp.where(pos == slot, 1.0, 0.0).astype(BF)
        out = out + jnp.dot(vals.astype(BF), put, preferred_element_type=F32)
        selfrow = selfrow + jnp.dot(vals.astype(BF), hotf[j].astype(BF), preferred_element_type=F32)[3:4]
    code = out[2:3] * 512.0 + (float(NT) - (2.0 * out[0:1] + out[1:2]))
    codes[:, : SB * 128] = code.astype(jnp.int32)
    lane32 = lax.broadcasted_iota(jnp.int32, (32, 128), 1)
    row32 = lax.broadcasted_iota(jnp.int32, (32, 128), 0)
    n = jnp.broadcast_to(selfrow, (32, 128))
    even = jnp.sum(jnp.where(lane32 == 2 * row32, n, 0.0), axis=1, keepdims=True)
    odd = jnp.sum(jnp.where(lane32 == 2 * row32 + 1, n, 0.0), axis=1, keepdims=True)
    return jnp.where(lane32 < 64, even, odd)


NR = 160
UN = 8
NB = 4


def split3(x):
    a = x.astype(BF).astype(F32)
    r = x - a
    b = r.astype(BF).astype(F32)
    return a, b, r - b


def home_features(own, widths, L, CH):
    lane = lax.broadcasted_iota(jnp.int32, (8, 128), 1)
    row = lax.broadcasted_iota(jnp.int32, (8, 128), 0)
    low = lane < 64

    def halves(x):
        y = pltpu.roll(x, 64, 1)
        return jnp.where(low, x, y), jnp.where(low, y, x)

    st = jnp.zeros((8, 128), F32)
    for t in range(8):
        st = jnp.where(row == t, widths[t], st)
    st = st * st * 0.01

    def prep_home(r, carry):
        v = own[pl.ds(r, 8, stride=32), :]
        v = jnp.where(row < 3, v * 0.1, v)
        x = v[:, 0:1]
        y = v[:, 64:65]
        cen = jnp.where(low, jnp.broadcast_to(x, (8, 128)), jnp.broadcast_to(y, (8, 128)))
        cen = jnp.where(row < 3, cen, 0.0)
        a = v - cen
        n = jnp.sum(jnp.where(row < 3, a * a, 0.0), axis=0, keepdims=True) + 0.0025
        f = jnp.where(row < 3, -2.0 * a, jnp.where(row < 6, 1.0, jnp.where(row == 6, n, 0.0)))
        f1, f2, f3 = split3(f)
        si = jnp.sum(jnp.where(row.astype(F32) == v[5:6], st, 0.0), axis=0, keepdims=True)
        w1, w2, w3 = split3(lax.rsqrt(st + si))
        t = jnp.concatenate([f1, f1, f1, f2, f2, f3, w1, w2, jnp.zeros((64, 128), F32)], axis=0).T.astype(BF)
        L[r * 2] = t[:64]
        L[r * 2 + 1] = t[64:]
        c0, c1 = halves(cen)
        CH[r * 2] = c0
        CH[r * 2 + 1] = c1
        return carry

    lax.fori_loop(0, 32, prep_home, 0, unroll=8)


def pair_kernel(codes_h, widths, chi, hard, own_h, halo_h, feat_h, centre_h, fe, rf, codes, own, halo, L, CH, sem, G, C, acc, *bufs):
    loads = [
        pltpu.make_async_copy(s, d, sem.at[k])
        for k, (s, d) in enumerate(((own_h, own), (halo_h, halo), (codes_h, codes), (feat_h, L), (centre_h, CH)))
    ]
    for c in loads:
        c.start()
    lane = lax.broadcasted_iota(jnp.int32, (8, 128), 1)
    row = lax.broadcasted_iota(jnp.int32, (8, 128), 0)
    low = lane < 64
    DS, VS = bufs[:NB], bufs[NB:]
    for k in range(NB):
        DS[k][...] = jnp.ones_like(DS[k])
        VS[k][...] = jnp.zeros_like(VS[k])

    def clear(h, carry):
        acc[0, h] = jnp.zeros((64, 128), F32)
        acc[1, h] = jnp.zeros((64, 128), F32)
        return carry

    lax.fori_loop(0, 64, clear, 0, unroll=4)

    for c in loads[:2]:
        c.wait()
    for b in range(5):
        at = [own[pl.ds(32 * c, 32), :] if b == 0 else halo[b - 1, pl.ds(32 * c, 32), :] for c in range(6)]
        if b in (1, 2):
            at[0] = at[0] + (-16.0 if b == 1 else 16.0)
        if b in (3, 4):
            at[1] = at[1] + (-32.0 if b == 3 else 32.0)
        for c, x in enumerate((at[0] * 0.1, at[1] * 0.1, at[2] * 0.1, at[3] * 0.1, at[4] * 0.1, at[5])):
            G[pl.ds(c * NR + b * 32, 32), :] = x
    G[pl.ds(6 * NR, 2 * NR), :] = jnp.zeros((2 * NR, 128), F32)

    def halves(x):
        y = pltpu.roll(x, 64, 1)
        return jnp.where(low, x, y), jnp.where(low, y, x)

    def prep(g, carry):
        c0, c1 = halves(G[pl.ds(g, 8, stride=NR), :])
        C[g * 2] = c0
        C[g * 2 + 1] = c1
        return carry

    lax.fori_loop(0, NR, prep, 0, unroll=16)

    C[NT] = jnp.where((row == 3) | (row == 4), 0.0, C[0])

    for c in loads[2:]:
        c.wait()
    types8 = row.astype(F32)
    zeros16 = jnp.zeros((16, 128), BF)
    zeros48 = jnp.zeros((48, 128), BF)
    last = jnp.where(row == 6, 1.0, 0.0)

    def terms(i, D, V):
        for u in range(UN):
            h = lax.shift_right_logical(codes[0, 2 * UN * i + 2 * u], 9)
            xs = [jnp.broadcast_to(V[u, k : k + 1], (8, 128)) for k in range(3, 5)]
            for q in range(8):
                rows = pl.ds(8 * q, 8)
                d = D[u, rows, pl.ds(0, 128)]
                w = D[u, rows, pl.ds(128, 128)]
                r = lax.rsqrt(d)
                e = lax.erf(d * r * w)
                m = jnp.maximum(1.0025 - d, 0.0)
                kk = (e * r) * (m * m)
                acc[0, h, rows] = acc[0, h, rows] + kk * xs[0]
                acc[1, h, rows] = acc[1, h, rows] + kk * xs[1]

    def distances(i, D, V):
        for u in range(UN):
            k1 = codes[0, 2 * UN * i + 2 * u]
            k2 = codes[0, 2 * UN * i + 2 * u + 1]
            h = lax.shift_right_logical(k1, 9)
            v = jnp.where(low, C[k1 & 511], C[k2 & 511]) - CH[h]
            V[u] = v
            f = jnp.where(row < 3, v, jnp.where(row < 6, pltpu.roll(v * v, 3, 0), last))
            s1, s2, s3 = split3(f)
            g = jnp.concatenate([s1, s2, s3, s1, s2, s1], axis=0).astype(BF)
            oh = jnp.where(types8 == v[5:6], 1.0, 0.0)
            oh = jnp.concatenate([oh, oh], axis=0).astype(BF)
            g = jnp.concatenate(
                [jnp.concatenate([g, zeros16], axis=0), jnp.concatenate([zeros48, oh], axis=0)], axis=1
            )
            D[u] = jnp.dot(L[h, :, pl.ds(0, 64)], g, preferred_element_type=F32)

    def step(i, carry):
        for k in range(NB):
            terms(jnp.maximum(NB * i + k - 1, 0), DS[k - 1], VS[k - 1])
            distances(NB * i + k, DS[k], VS[k])
        return carry

    blocks = lax.div(codes[0, 1664] + UN - 1, UN)
    lax.fori_loop(0, lax.div(blocks + NB, NB), step, 0)

    def finish(r, carry):
        for f, ref in enumerate((fe, rf)):
            ref[pl.ds(r, 1), :] = jnp.sum(acc[f, pl.ds(2 * r, 2)].reshape(128, 128).T, axis=0, keepdims=True)
        return carry

    lax.fori_loop(0, 32, finish, 0, unroll=8)
    s2 = jnp.zeros((32, 128), F32)
    ch = jnp.zeros((32, 128), F32)
    eta = jnp.zeros((32, 128), F32)
    for t in range(8):
        hit = own[160:192] == float(t)
        s2 = jnp.where(hit, widths[t] * widths[t], s2)
        ch = jnp.where(hit, chi[t], ch)
        eta = jnp.where(hit, hard[t], eta)
    itself = own[192:224] * (2.0 * lax.erf(0.5 * lax.rsqrt(s2 + s2)))
    residual = rf[...] - itself * own[128:160]
    field = ch + (fe[...] - itself * own[96:128]) + residual
    rf[...] = residual
    fe[...] = field / eta


def pair_call(codes, widths, chi, hard, own, halo, feats, centres):
    sm = pl.BlockSpec(memory_space=pltpu.SMEM)
    vm = pl.BlockSpec(memory_space=pltpu.VMEM)
    hbm = pl.BlockSpec(memory_space=pl.ANY)
    return pl.pallas_call(
        pair_kernel,
        out_shape=[jax.ShapeDtypeStruct((32, 128), F32)] * 2,
        in_specs=[hbm] + [sm] * 3 + [hbm] * 4,
        out_specs=[vm, vm],
        scratch_shapes=[
            pltpu.SMEM(codes.shape, jnp.int32),
            pltpu.VMEM(own.shape, F32),
            pltpu.VMEM(halo.shape, F32),
            pltpu.VMEM(feats.shape, BF),
            pltpu.VMEM(centres.shape, F32),
            pltpu.SemaphoreType.DMA((5,)),
            pltpu.VMEM((8 * NR, 128), F32),
            pltpu.VMEM((NT + 1, 8, 128), F32),
            pltpu.VMEM((2, 64, 64, 128), F32),
            *[pltpu.VMEM((UN, 64, 256), F32)] * NB,
            *[pltpu.VMEM((UN, 8, 128), F32)] * NB,
        ],
        compiler_params=pltpu.CompilerParams(vmem_limit_bytes=60 * 2**20),
        name="pairs",
    )(codes, widths, chi, hard, own, halo, feats, centres)


def exchange_kernel(
    pos_h, aux_h, resid_h, types_h, owner_h, tiles_h, cands_h, hard, widths, count,
    own_h, halo_h, early_h, codes_h, feat_h, centre_h,
    pos, aux, resid, types, owner, tiles, cands, own, early, codes, L, CH, tr, cr, load, send, recv, store,
):
    nb, npl = lax.axis_size("brick"), lax.axis_size("plane")
    b, p = lax.axis_index("brick"), lax.axis_index("plane")
    below, above = lax.rem(b + nb - 1, nb), lax.rem(b + 1, nb)
    barrier = pltpu.get_barrier_semaphore()
    left, right = lax.rem(p + npl - 1, npl), lax.rem(p + 1, npl)
    for d in [(below, p), (above, p), (b, left), (b, right)]:
        pl.semaphore_signal(barrier, inc=1, device_id=d, device_id_type=MESH)
    ins = ((pos_h, pos), (aux_h, aux), (resid_h, resid), (types_h, types), (owner_h, owner), (tiles_h, tiles), (cands_h, cands))
    loads = [pltpu.make_async_copy(x, y, load.at[k]) for k, (x, y) in enumerate(ins)]
    for c in loads:
        c.start()
    for c in loads:
        c.wait()
    own[0:96, :] = pos[...]
    own[96:128, :] = aux[...]
    own[128:160, :] = resid[...]
    ty = types[...].astype(F32)
    own[160:192, :] = ty
    own[192:256, :] = jnp.zeros((64, 128), F32)
    pl.semaphore_wait(barrier, 4)

    def copy(s, d, k, to):
        return pltpu.make_async_remote_copy(
            src_ref=s, dst_ref=d, send_sem=send.at[k], recv_sem=recv.at[k], device_id=to, device_id_type=MESH
        )

    mine = own.at[pl.ds(0, 192)]
    copies = [
        copy(mine, halo_h.at[0], 0, (above, p)),
        copy(mine, halo_h.at[1], 1, (below, p)),
        copy(mine, halo_h.at[2], 2, (b, right)),
        copy(mine, halo_h.at[3], 3, (b, left)),
    ]
    for c in copies:
        c.start()
    inverse = jnp.zeros((32, 128), F32)
    for t in range(8):
        inverse = jnp.where(ty == float(t), 1.0 / jnp.full((32, 128), hard[t], F32), inverse)
    early[0:32, :] = aux[...]
    early[32:64, :] = inverse
    src = lax.broadcasted_iota(jnp.int32, (64, 128), 0)
    lane = lax.broadcasted_iota(jnp.int32, (64, 128), 1) - 32 * p
    inside = (lane >= 0) & (lane < 32)
    ids = jnp.broadcast_to(owner[...].astype(F32), (8, 64))
    evens = jnp.dot(ids, jnp.where(inside & (src == 2 * lane), 1.0, 0.0), precision=HI, preferred_element_type=F32)
    odds = jnp.dot(ids, jnp.where(inside & (src == 2 * lane + 1), 1.0, 0.0), precision=HI, preferred_element_type=F32)
    r8 = lax.broadcasted_iota(jnp.int32, (8, 128), 0)
    early[64:72, :] = jnp.where(r8 == 0, evens, odds)
    home_features(own, widths, L, CH)
    own[192:224, :] = order_pairs(tiles, cands, count, codes, tr, cr)
    outs = ((own, own_h), (early, early_h), (codes, codes_h), (L, feat_h), (CH, centre_h))
    stores = [pltpu.make_async_copy(x, y, store.at[k]) for k, (x, y) in enumerate(outs)]
    for c in stores:
        c.start()
    for c in stores:
        c.wait()
    for c in copies:
        c.wait()


def exchange(pos, aux, resid, types, owner, tiles, cands, hard, widths, count):
    hbm = pl.BlockSpec(memory_space=pl.ANY)
    dma = pltpu.SemaphoreType.DMA
    shape = jax.ShapeDtypeStruct
    ncodes = (SB + 1) * 128
    return pl.pallas_call(
        exchange_kernel,
        out_shape=[
            shape((256, 128), F32),
            shape((4, 192, 128), F32),
            shape((72, 128), F32),
            shape((1, ncodes), jnp.int32),
            shape((64, 64, 128), BF),
            shape((64, 8, 128), F32),
        ],
        in_specs=[hbm] * 7 + [pl.BlockSpec(memory_space=pltpu.SMEM)] * 3,
        out_specs=[hbm] * 6,
        scratch_shapes=[pltpu.VMEM(x.shape, x.dtype) for x in (pos, aux, resid, types, owner, tiles, cands)]
        + [
            pltpu.VMEM((256, 128), F32),
            pltpu.VMEM((72, 128), F32),
            pltpu.VMEM((1, ncodes), jnp.int32),
            pltpu.VMEM((64, 64, 128), BF),
            pltpu.VMEM((64, 8, 128), F32),
            pltpu.VMEM((128, 128), F32),
            pltpu.VMEM((16, 128), F32),
            dma((7,)), dma((4,)), dma((4,)), dma((5,)),
        ],
        compiler_params=pltpu.CompilerParams(collective_id=0, has_side_effects=True, vmem_limit_bytes=60 * 2**20),
        name="exchange",
    )(pos, aux, resid, types, owner, tiles, cands, hard, widths, count)


LINE, SHEET = 16, 32


def level_kernel(fe_h, early_h, out, fe, early, load, got, near, far, s1, r1, s2, r2, s3, r3, ready):
    npl = lax.axis_size("plane")
    b, p = lax.axis_index("brick"), lax.axis_index("plane")
    zhi = lax.rem(lax.div(b, 8), 4)
    z = npl * zhi + p
    w = 8 * lax.div(b, 32) + lax.rem(b, 8)

    def line(q):
        return (b + 8 * (lax.div(q, npl) - zhi), lax.rem(q, npl))

    def sheet(q):
        return (32 * lax.div(q, 8) + 8 * zhi + lax.rem(q, 8), p)

    lines = [lax.rem(z + k, LINE) for k in range(1, LINE)]
    sheets = [lax.rem(w + k, SHEET) for k in range(1, SHEET)]
    mates = [lax.rem(p + k, npl) for k in range(1, npl)]
    barrier = pltpu.get_barrier_semaphore()
    for k in (1, 2, 3, 4, 12, 13, 14, 15):
        pl.semaphore_signal(barrier, inc=1, device_id=line(lax.rem(z + k, LINE)), device_id_type=MESH)
    for q in sheets:
        pl.semaphore_signal(barrier, inc=1, device_id=sheet(q), device_id_type=MESH)
    ins = ((fe_h, fe), (early_h, early))
    loads = [pltpu.make_async_copy(x, y, load.at[k]) for k, (x, y) in enumerate(ins)]
    for c in loads:
        c.start()
    for c in loads:
        c.wait()
    got[p, 0:72, :] = early[...]
    got[p, 72:104, :] = fe[...]

    def fold(x):
        s = jnp.sum(x, axis=0, keepdims=True)
        return s + pltpu.roll(s, 64, 1)

    first_half = lax.broadcasted_iota(jnp.int32, (1, 128), 1) < 64
    near[w] = jnp.where(first_half, fold(early[0:32, :] + fe[...]), fold(early[32:64, :]))
    pl.semaphore_wait(barrier, 8 + SHEET - 1)
    for k in (4, 12):
        pl.semaphore_signal(ready, inc=1, device_id=line(lax.rem(z + k, LINE)), device_id_type=MESH)

    def copy(s, d, ss, rs, to):
        return pltpu.make_async_remote_copy(
            src_ref=s, dst_ref=d, send_sem=ss, recv_sem=rs, device_id=to, device_id_type=MESH
        )

    first = [copy(near.at[w], near.at[w], s1.at[k], r1.at[k], sheet(q)) for k, q in enumerate(sheets)]
    for c in first:
        c.start()
    tiles = [copy(got.at[p], got.at[p], s2.at[k], r2.at[k], (b, q)) for k, q in enumerate(mates)]
    for c in tiles:
        c.start()
    for c in first:
        c.wait()
    total = near[0]
    for k in range(1, SHEET):
        total = total + near[k]
    far[z] = total
    pl.semaphore_wait(ready, 2)
    second = [copy(far.at[z], far.at[z], s3.at[k], r3.at[k], line(q)) for k, q in enumerate(lines)]
    for c in second:
        c.start()
    for c in tiles:
        c.wait()
    evens = got[0, 64:65, :] + got[1, 64:65, :] + got[2, 64:65, :] + got[3, 64:65, :]
    odds = got[0, 65:66, :] + got[1, 65:66, :] + got[2, 65:66, :] + got[3, 65:66, :]
    slot = (64 * p + 2 * lax.broadcasted_iota(jnp.int32, (32, 128), 0)).astype(F32)
    place = jnp.concatenate(
        [
            jnp.where(evens == slot, 1.0, 0.0),
            jnp.where(odds == slot + 1.0, 1.0, 0.0),
            jnp.where(evens == slot + 1.0, 1.0, 0.0),
            jnp.where(odds == slot, 1.0, 0.0),
        ],
        axis=0,
    )
    low = lax.broadcasted_iota(jnp.int32, (32, 128), 1) < 64

    def placed(x):
        y = jnp.dot(place, x, precision=HI, preferred_element_type=F32)
        return jnp.where(low, y[0:32], y[32:64]) + pltpu.roll(jnp.where(low, y[64:96], y[96:128]), 64, 1)

    aux = placed(got[:, 0:32, :].reshape(128, 128))
    inverse = placed(got[:, 32:64, :].reshape(128, 128))
    moved = placed(got[:, 72:104, :].reshape(128, 128))
    out[0:32, :] = 2.0 * aux - kappa * (moved + aux)
    out[32:64, :] = kappa * inverse
    for c in second:
        c.wait()
    total = far[0]
    for k in range(1, LINE):
        total = total + far[k]
    top = jnp.sum(jnp.where(first_half, total, 0.0), axis=1, keepdims=True)
    bottom = jnp.sum(jnp.where(first_half, 0.0, total), axis=1, keepdims=True)
    out[64:72, :] = jnp.broadcast_to(top / bottom, (8, 128))


def finish(fe, early):
    vm = pl.BlockSpec(memory_space=pltpu.VMEM)
    dma = pltpu.SemaphoreType.DMA
    return pl.pallas_call(
        level_kernel,
        out_shape=jax.ShapeDtypeStruct((72, 128), F32),
        in_specs=[pl.BlockSpec(memory_space=pl.ANY)] * 2,
        out_specs=vm,
        scratch_shapes=[
            pltpu.VMEM((32, 128), F32),
            pltpu.VMEM((72, 128), F32),
            dma((2,)),
            pltpu.VMEM((4, 104, 128), F32),
            pltpu.VMEM((SHEET, 1, 128), F32),
            pltpu.VMEM((LINE, 1, 128), F32),
            dma((SHEET - 1,)), dma((SHEET - 1,)), dma((3,)), dma((3,)), dma((LINE - 1,)), dma((LINE - 1,)),
            pltpu.SemaphoreType.REGULAR,
        ],
        compiler_params=pltpu.CompilerParams(collective_id=1, has_side_effects=True, vmem_limit_bytes=60 * 2**20),
        name="level",
    )(fe, early)


def last_kernel(out, fe, early, prev, charges, nxt):
    level = jnp.broadcast_to(out[64:65, :], (32, 128))
    charges[...] = level * early[32:64, :] - fe[...]
    nxt[...] = out[0:32, :] - prev[...] + level * out[32:64, :]


def last_step(out, fe, early, prev):
    vm = pl.BlockSpec(memory_space=pltpu.VMEM)
    return pl.pallas_call(
        last_kernel,
        out_shape=[jax.ShapeDtypeStruct((32, 128), F32)] * 2,
        in_specs=[vm] * 4,
        out_specs=[vm] * 2,
        name="last_step",
    )(out, fe, early, prev)


def on_device(positions, aux, aux_prev, resid, types, pair_tiles, pair_cands, pair_count, owner_tile, electroneg, hardness, widths):
    own, halo, early, codes, feats, centres = exchange(
        positions.transpose(0, 2, 1, 3).reshape(96, 128),
        aux.reshape(32, 128),
        resid.reshape(32, 128),
        types.reshape(32, 128),
        owner_tile.reshape(1, -1),
        pair_tiles.reshape(1, -1),
        pair_cands.reshape(1, -1),
        hardness,
        widths,
        pair_count,
    )
    fe, rf = pair_call(codes, widths, electroneg, hardness, own, halo, feats, centres)
    out = finish(fe, early)
    charges, nxt = last_step(out, fe, early, aux_prev.reshape(32, 128))
    return charges.reshape(aux.shape), nxt.reshape(aux.shape), rf.reshape(aux.shape)


def solution(mesh):
    s4, s3, s2 = P("brick", "plane", None, None), P("brick", "plane", None), P("brick", "plane")
    return jax.shard_map(
        on_device,
        mesh=mesh,
        in_specs=(s4, s3, s3, s3, s3, s3, s3, s2, s3, P(), P(), P()),
        out_specs=(s3, s3, s3),
        check_vma=False,
    )
```

```python
import functools

import jax
import jax.numpy as jnp
from jax import lax
from jax.experimental import pallas as pl
from jax.experimental.pallas import tpu as pltpu
from jax.sharding import PartitionSpec as P

F32 = jnp.float32
BF = jnp.bfloat16
HI = lax.Precision.HIGHEST
MESH = pl.DeviceIdType.MESH
kappa = 1.86

PB = 12
SB = 13
NT = 320


def order_pairs(tiles, cands, count, codes, tr, cr):
    n = tiles.shape[1]
    one = lax.broadcasted_iota(jnp.int32, (1, 128), 1)
    tr[...] = jnp.full((128, 128), 64.0, F32)
    cr[...] = jnp.zeros((16, 128), F32)
    for j in range(PB):
        w = min(128, n - 128 * j)
        tr[j : j + 1, :w] = tiles[:, 128 * j : 128 * j + w].astype(F32)
        cr[j : j + 1, :w] = cands[:, 128 * j : 128 * j + w].astype(F32)
    prow = lax.broadcasted_iota(jnp.int32, (16, 128), 0) * 128 + lax.broadcasted_iota(jnp.int32, (16, 128), 1)
    used = prow < count[0, 0]
    t = jnp.where(used, tr[:16], 64.0)
    c = jnp.where(used, cr[...], 0.0)
    tr[:16] = t
    tcol = tr[...].T
    lane = lax.broadcasted_iota(jnp.int32, (128, 128), 1)
    rowi = lax.broadcasted_iota(jnp.int32, (128, 128), 0)
    lanef = lane.astype(F32)
    before = jnp.where(lane < rowi, 1.0, 0.0).astype(BF)
    hot = [tcol[:, j : j + 1] == lanef for j in range(PB)]
    hotf = [jnp.where(h, 1.0, 0.0) for h in hot]
    sums = [jnp.sum(h, axis=0, keepdims=True) for h in hotf]
    counts = sum(sums)
    counts = jnp.where(one < 64, counts, 0.0)
    half = jnp.floor((counts + 1.0) * 0.5)
    starts = 2.0 * jnp.dot(jnp.broadcast_to(half, (8, 128)), jnp.where(rowi < lane, 1.0, 0.0), precision=HI, preferred_element_type=F32)[:1]
    starts = jnp.where(one < 64, starts, 8192.0)
    codes[:, SB * 128 :] = jnp.broadcast_to(jnp.sum(half, axis=1, keepdims=True), (1, 128)).astype(jnp.int32)
    out = jnp.zeros((8, SB * 128), F32)
    slot = lax.broadcasted_iota(jnp.int32, (128, SB * 128), 1).astype(F32)
    selfrow = jnp.zeros((1, 128), F32)
    e = float(NT) - c
    e = jnp.where(used, e, 0.0)
    ehi = jnp.floor(e * 0.5)
    elo = e - 2.0 * ehi
    same = jnp.where(t == c, 1.0, 0.0)
    r8 = lax.broadcasted_iota(jnp.int32, (8, 128), 0)
    for j in range(PB):
        rank = jnp.dot(before, hotf[j].astype(BF), preferred_element_type=F32)
        pos = jnp.sum(jnp.where(hot[j], rank + starts, 0.0), axis=1, keepdims=True)
        starts = starts + sums[j]
        vals = jnp.where(r8 == 0, ehi[j : j + 1], jnp.where(r8 == 1, elo[j : j + 1], jnp.where(r8 == 2, t[j : j + 1], same[j : j + 1])))
        put = jnp.where(pos == slot, 1.0, 0.0).astype(BF)
        out = out + jnp.dot(vals.astype(BF), put, preferred_element_type=F32)
        selfrow = selfrow + jnp.dot(vals.astype(BF), hotf[j].astype(BF), preferred_element_type=F32)[3:4]
    code = out[2:3] * 512.0 + (float(NT) - (2.0 * out[0:1] + out[1:2]))
    codes[:, : SB * 128] = code.astype(jnp.int32)
    lane32 = lax.broadcasted_iota(jnp.int32, (32, 128), 1)
    row32 = lax.broadcasted_iota(jnp.int32, (32, 128), 0)
    n = jnp.broadcast_to(selfrow, (32, 128))
    even = jnp.sum(jnp.where(lane32 == 2 * row32, n, 0.0), axis=1, keepdims=True)
    odd = jnp.sum(jnp.where(lane32 == 2 * row32 + 1, n, 0.0), axis=1, keepdims=True)
    return jnp.where(lane32 < 64, even, odd)


NR = 160
UN = 8
NB = 2


def split3(x):
    a = x.astype(BF).astype(F32)
    r = x - a
    b = r.astype(BF).astype(F32)
    return a, b, r - b


def home_features(own, widths, L, CH):
    lane = lax.broadcasted_iota(jnp.int32, (8, 128), 1)
    row = lax.broadcasted_iota(jnp.int32, (8, 128), 0)
    low = lane < 64

    def halves(x):
        y = pltpu.roll(x, 64, 1)
        return jnp.where(low, x, y), jnp.where(low, y, x)

    st = jnp.zeros((8, 128), F32)
    for t in range(8):
        st = jnp.where(row == t, widths[t], st)
    st = st * st * 0.01

    def prep_home(r, carry):
        v = own[pl.ds(r, 8, stride=32), :]
        v = jnp.where(row < 3, v * 0.1, v)
        x = v[:, 0:1]
        y = v[:, 64:65]
        cen = jnp.where(low, jnp.broadcast_to(x, (8, 128)), jnp.broadcast_to(y, (8, 128)))
        cen = jnp.where(row < 3, cen, 0.0)
        a = v - cen
        n = jnp.sum(jnp.where(row < 3, a * a, 0.0), axis=0, keepdims=True) + 0.0025
        f = jnp.where(row < 3, -2.0 * a, jnp.where(row < 6, 1.0, jnp.where(row == 6, n, 0.0)))
        f1, f2, f3 = split3(f)
        si = jnp.sum(jnp.where(row.astype(F32) == v[5:6], st, 0.0), axis=0, keepdims=True)
        w1, w2, w3 = split3(lax.rsqrt(st + si))
        t = jnp.concatenate([f1, f1, f1, f2, f2, f3, w1, w2, jnp.zeros((64, 128), F32)], axis=0).T.astype(BF)
        L[r * 2] = t[:64]
        L[r * 2 + 1] = t[64:]
        c0, c1 = halves(cen)
        CH[r * 2] = c0
        CH[r * 2 + 1] = c1
        return carry

    lax.fori_loop(0, 32, prep_home, 0, unroll=8)


def pair_kernel(codes_h, widths, chi, hard, own_h, halo_h, feat_h, centre_h, fe, rf, codes, own, halo, L, CH, sem, G, C, acc, *bufs):
    loads = [
        pltpu.make_async_copy(s, d, sem.at[k])
        for k, (s, d) in enumerate(((own_h, own), (halo_h, halo), (codes_h, codes), (feat_h, L), (centre_h, CH)))
    ]
    for c in loads:
        c.start()
    lane = lax.broadcasted_iota(jnp.int32, (8, 128), 1)
    row = lax.broadcasted_iota(jnp.int32, (8, 128), 0)
    low = lane < 64
    DS, VS = bufs[:NB], bufs[NB:]
    for k in range(NB):
        DS[k][...] = jnp.ones_like(DS[k])
        VS[k][...] = jnp.zeros_like(VS[k])

    def clear(h, carry):
        acc[0, h] = jnp.zeros((64, 128), F32)
        acc[1, h] = jnp.zeros((64, 128), F32)
        return carry

    lax.fori_loop(0, 64, clear, 0, unroll=4)

    for c in loads[:2]:
        c.wait()
    for b in range(5):
        at = [own[pl.ds(32 * c, 32), :] if b == 0 else halo[b - 1, pl.ds(32 * c, 32), :] for c in range(6)]
        if b in (1, 2):
            at[0] = at[0] + (-16.0 if b == 1 else 16.0)
        if b in (3, 4):
            at[1] = at[1] + (-32.0 if b == 3 else 32.0)
        for c, x in enumerate((at[0] * 0.1, at[1] * 0.1, at[2] * 0.1, at[3] * 0.1, at[4] * 0.1, at[5])):
            G[pl.ds(c * NR + b * 32, 32), :] = x
    G[pl.ds(6 * NR, 2 * NR), :] = jnp.zeros((2 * NR, 128), F32)

    def halves(x):
        y = pltpu.roll(x, 64, 1)
        return jnp.where(low, x, y), jnp.where(low, y, x)

    def prep(g, carry):
        c0, c1 = halves(G[pl.ds(g, 8, stride=NR), :])
        C[g * 2] = c0
        C[g * 2 + 1] = c1
        return carry

    lax.fori_loop(0, NR, prep, 0, unroll=16)

    C[NT] = jnp.where((row == 3) | (row == 4), 0.0, C[0])

    for c in loads[2:]:
        c.wait()
    types8 = row.astype(F32)
    zeros16 = jnp.zeros((16, 128), BF)
    zeros48 = jnp.zeros((48, 128), BF)
    last = jnp.where(row == 6, 1.0, 0.0)

    def terms(i, D, V):
        for u in range(UN):
            h = lax.shift_right_logical(codes[0, 2 * UN * i + 2 * u], 9)
            xs = [jnp.broadcast_to(V[u, k : k + 1], (8, 128)) for k in range(3, 5)]
            for q in range(8):
                rows = pl.ds(8 * q, 8)
                d = D[u, rows, pl.ds(0, 128)]
                w = D[u, rows, pl.ds(128, 128)]
                r = lax.rsqrt(d)
                e = lax.erf(d * r * w)
                m = jnp.maximum(1.0025 - d, 0.0)
                kk = (e * r) * (m * m)
                acc[0, h, rows] = acc[0, h, rows] + kk * xs[0]
                acc[1, h, rows] = acc[1, h, rows] + kk * xs[1]

    def distances(i, D, V):
        for u in range(UN):
            k1 = codes[0, 2 * UN * i + 2 * u]
            k2 = codes[0, 2 * UN * i + 2 * u + 1]
            h = lax.shift_right_logical(k1, 9)
            v = jnp.where(low, C[k1 & 511], C[k2 & 511]) - CH[h]
            V[u] = v
            f = jnp.where(row < 3, v, jnp.where(row < 6, pltpu.roll(v * v, 3, 0), last))
            s1, s2, s3 = split3(f)
            g = jnp.concatenate([s1, s2, s3, s1, s2, s1], axis=0).astype(BF)
            oh = jnp.where(types8 == v[5:6], 1.0, 0.0)
            oh = jnp.concatenate([oh, oh], axis=0).astype(BF)
            g = jnp.concatenate(
                [jnp.concatenate([g, zeros16], axis=0), jnp.concatenate([zeros48, oh], axis=0)], axis=1
            )
            D[u] = jnp.dot(L[h, :, pl.ds(0, 64)], g, preferred_element_type=F32)

    def step(i, carry):
        for k in range(NB):
            terms(jnp.maximum(NB * i + k - 1, 0), DS[k - 1], VS[k - 1])
            distances(NB * i + k, DS[k], VS[k])
        return carry

    blocks = lax.div(codes[0, 1664] + UN - 1, UN)
    lax.fori_loop(0, lax.div(blocks + NB, NB), step, 0)

    def finish(r, carry):
        for f, ref in enumerate((fe, rf)):
            ref[pl.ds(r, 1), :] = jnp.sum(acc[f, pl.ds(2 * r, 2)].reshape(128, 128).T, axis=0, keepdims=True)
        return carry

    lax.fori_loop(0, 32, finish, 0, unroll=8)
    s2 = jnp.zeros((32, 128), F32)
    ch = jnp.zeros((32, 128), F32)
    eta = jnp.zeros((32, 128), F32)
    for t in range(8):
        hit = own[160:192] == float(t)
        s2 = jnp.where(hit, widths[t] * widths[t], s2)
        ch = jnp.where(hit, chi[t], ch)
        eta = jnp.where(hit, hard[t], eta)
    itself = own[192:224] * (2.0 * lax.erf(0.5 * lax.rsqrt(s2 + s2)))
    residual = rf[...] - itself * own[128:160]
    field = ch + (fe[...] - itself * own[96:128]) + residual
    rf[...] = residual
    fe[...] = field / eta


def pair_call(codes, widths, chi, hard, own, halo, feats, centres):
    sm = pl.BlockSpec(memory_space=pltpu.SMEM)
    vm = pl.BlockSpec(memory_space=pltpu.VMEM)
    hbm = pl.BlockSpec(memory_space=pl.ANY)
    return pl.pallas_call(
        pair_kernel,
        out_shape=[jax.ShapeDtypeStruct((32, 128), F32)] * 2,
        in_specs=[hbm] + [sm] * 3 + [hbm] * 4,
        out_specs=[vm, vm],
        scratch_shapes=[
            pltpu.SMEM(codes.shape, jnp.int32),
            pltpu.VMEM(own.shape, F32),
            pltpu.VMEM(halo.shape, F32),
            pltpu.VMEM(feats.shape, BF),
            pltpu.VMEM(centres.shape, F32),
            pltpu.SemaphoreType.DMA((5,)),
            pltpu.VMEM((8 * NR, 128), F32),
            pltpu.VMEM((NT + 1, 8, 128), F32),
            pltpu.VMEM((2, 64, 64, 128), F32),
            *[pltpu.VMEM((UN, 64, 256), F32)] * NB,
            *[pltpu.VMEM((UN, 8, 128), F32)] * NB,
        ],
        compiler_params=pltpu.CompilerParams(vmem_limit_bytes=60 * 2**20),
        name="pairs",
    )(codes, widths, chi, hard, own, halo, feats, centres)


def exchange_kernel(
    pos_h, aux_h, resid_h, types_h, owner_h, tiles_h, cands_h, hard, widths, count,
    own_h, halo_h, early_h, codes_h, feat_h, centre_h,
    pos, aux, resid, types, owner, tiles, cands, own, early, codes, L, CH, tr, cr, load, send, recv, store,
):
    nb, npl = lax.axis_size("brick"), lax.axis_size("plane")
    b, p = lax.axis_index("brick"), lax.axis_index("plane")
    below, above = lax.rem(b + nb - 1, nb), lax.rem(b + 1, nb)
    barrier = pltpu.get_barrier_semaphore()
    left, right = lax.rem(p + npl - 1, npl), lax.rem(p + 1, npl)
    for d in [(below, p), (above, p), (b, left), (b, right)]:
        pl.semaphore_signal(barrier, inc=1, device_id=d, device_id_type=MESH)
    ins = ((pos_h, pos), (aux_h, aux), (resid_h, resid), (types_h, types), (owner_h, owner), (tiles_h, tiles), (cands_h, cands))
    loads = [pltpu.make_async_copy(x, y, load.at[k]) for k, (x, y) in enumerate(ins)]
    for c in loads:
        c.start()
    for c in loads:
        c.wait()
    own[0:96, :] = pos[...]
    own[96:128, :] = aux[...]
    own[128:160, :] = resid[...]
    ty = types[...].astype(F32)
    own[160:192, :] = ty
    own[192:256, :] = jnp.zeros((64, 128), F32)
    pl.semaphore_wait(barrier, 4)

    def copy(s, d, k, to):
        return pltpu.make_async_remote_copy(
            src_ref=s, dst_ref=d, send_sem=send.at[k], recv_sem=recv.at[k], device_id=to, device_id_type=MESH
        )

    mine = own.at[pl.ds(0, 192)]
    copies = [
        copy(mine, halo_h.at[0], 0, (above, p)),
        copy(mine, halo_h.at[1], 1, (below, p)),
        copy(mine, halo_h.at[2], 2, (b, right)),
        copy(mine, halo_h.at[3], 3, (b, left)),
    ]
    for c in copies:
        c.start()
    inverse = jnp.zeros((32, 128), F32)
    for t in range(8):
        inverse = jnp.where(ty == float(t), 1.0 / jnp.full((32, 128), hard[t], F32), inverse)
    early[0:32, :] = aux[...]
    early[32:64, :] = inverse
    src = lax.broadcasted_iota(jnp.int32, (64, 128), 0)
    lane = lax.broadcasted_iota(jnp.int32, (64, 128), 1) - 32 * p
    inside = (lane >= 0) & (lane < 32)
    ids = jnp.broadcast_to(owner[...].astype(F32), (8, 64))
    evens = jnp.dot(ids, jnp.where(inside & (src == 2 * lane), 1.0, 0.0), precision=HI, preferred_element_type=F32)
    odds = jnp.dot(ids, jnp.where(inside & (src == 2 * lane + 1), 1.0, 0.0), precision=HI, preferred_element_type=F32)
    r8 = lax.broadcasted_iota(jnp.int32, (8, 128), 0)
    early[64:72, :] = jnp.where(r8 == 0, evens, odds)
    home_features(own, widths, L, CH)
    own[192:224, :] = order_pairs(tiles, cands, count, codes, tr, cr)
    outs = ((own, own_h), (early, early_h), (codes, codes_h), (L, feat_h), (CH, centre_h))
    stores = [pltpu.make_async_copy(x, y, store.at[k]) for k, (x, y) in enumerate(outs)]
    for c in stores:
        c.start()
    for c in stores:
        c.wait()
    for c in copies:
        c.wait()


def exchange(pos, aux, resid, types, owner, tiles, cands, hard, widths, count):
    hbm = pl.BlockSpec(memory_space=pl.ANY)
    dma = pltpu.SemaphoreType.DMA
    shape = jax.ShapeDtypeStruct
    ncodes = (SB + 1) * 128
    return pl.pallas_call(
        exchange_kernel,
        out_shape=[
            shape((256, 128), F32),
            shape((4, 192, 128), F32),
            shape((72, 128), F32),
            shape((1, ncodes), jnp.int32),
            shape((64, 64, 128), BF),
            shape((64, 8, 128), F32),
        ],
        in_specs=[hbm] * 7 + [pl.BlockSpec(memory_space=pltpu.SMEM)] * 3,
        out_specs=[hbm] * 6,
        scratch_shapes=[pltpu.VMEM(x.shape, x.dtype) for x in (pos, aux, resid, types, owner, tiles, cands)]
        + [
            pltpu.VMEM((256, 128), F32),
            pltpu.VMEM((72, 128), F32),
            pltpu.VMEM((1, ncodes), jnp.int32),
            pltpu.VMEM((64, 64, 128), BF),
            pltpu.VMEM((64, 8, 128), F32),
            pltpu.VMEM((128, 128), F32),
            pltpu.VMEM((16, 128), F32),
            dma((7,)), dma((4,)), dma((4,)), dma((5,)),
        ],
        compiler_params=pltpu.CompilerParams(collective_id=0, has_side_effects=True, vmem_limit_bytes=60 * 2**20),
        name="exchange",
    )(pos, aux, resid, types, owner, tiles, cands, hard, widths, count)


LINE, SHEET = 16, 32


def level_kernel(fe_h, early_h, out, fe, early, load, got, near, far, s1, r1, s2, r2, s3, r3, ready):
    npl = lax.axis_size("plane")
    b, p = lax.axis_index("brick"), lax.axis_index("plane")
    zhi = lax.rem(lax.div(b, 8), 4)
    z = npl * zhi + p
    w = 8 * lax.div(b, 32) + lax.rem(b, 8)

    def line(q):
        return (b + 8 * (lax.div(q, npl) - zhi), lax.rem(q, npl))

    def sheet(q):
        return (32 * lax.div(q, 8) + 8 * zhi + lax.rem(q, 8), p)

    lines = [lax.rem(z + k, LINE) for k in range(1, LINE)]
    sheets = [lax.rem(w + k, SHEET) for k in range(1, SHEET)]
    mates = [lax.rem(p + k, npl) for k in range(1, npl)]
    barrier = pltpu.get_barrier_semaphore()
    for k in (1, 2, 3, 4, 12, 13, 14, 15):
        pl.semaphore_signal(barrier, inc=1, device_id=line(lax.rem(z + k, LINE)), device_id_type=MESH)
    for q in sheets:
        pl.semaphore_signal(barrier, inc=1, device_id=sheet(q), device_id_type=MESH)
    ins = ((fe_h, fe), (early_h, early))
    loads = [pltpu.make_async_copy(x, y, load.at[k]) for k, (x, y) in enumerate(ins)]
    for c in loads:
        c.start()
    for c in loads:
        c.wait()
    got[p, 0:72, :] = early[...]
    got[p, 72:104, :] = fe[...]

    def fold(x):
        s = jnp.sum(x, axis=0, keepdims=True)
        return s + pltpu.roll(s, 64, 1)

    first_half = lax.broadcasted_iota(jnp.int32, (1, 128), 1) < 64
    near[w] = jnp.where(first_half, fold(early[0:32, :] + fe[...]), fold(early[32:64, :]))
    pl.semaphore_wait(barrier, 8 + SHEET - 1)
    for k in (4, 12):
        pl.semaphore_signal(ready, inc=1, device_id=line(lax.rem(z + k, LINE)), device_id_type=MESH)

    def copy(s, d, ss, rs, to):
        return pltpu.make_async_remote_copy(
            src_ref=s, dst_ref=d, send_sem=ss, recv_sem=rs, device_id=to, device_id_type=MESH
        )

    first = [copy(near.at[w], near.at[w], s1.at[k], r1.at[k], sheet(q)) for k, q in enumerate(sheets)]
    for c in first:
        c.start()
    tiles = [copy(got.at[p], got.at[p], s2.at[k], r2.at[k], (b, q)) for k, q in enumerate(mates)]
    for c in tiles:
        c.start()
    for c in first:
        c.wait()
    total = near[0]
    for k in range(1, SHEET):
        total = total + near[k]
    far[z] = total
    pl.semaphore_wait(ready, 2)
    second = [copy(far.at[z], far.at[z], s3.at[k], r3.at[k], line(q)) for k, q in enumerate(lines)]
    for c in second:
        c.start()
    for c in tiles:
        c.wait()
    evens = got[0, 64:65, :] + got[1, 64:65, :] + got[2, 64:65, :] + got[3, 64:65, :]
    odds = got[0, 65:66, :] + got[1, 65:66, :] + got[2, 65:66, :] + got[3, 65:66, :]
    slot = (64 * p + 2 * lax.broadcasted_iota(jnp.int32, (32, 128), 0)).astype(F32)
    place = jnp.concatenate(
        [
            jnp.where(evens == slot, 1.0, 0.0),
            jnp.where(odds == slot + 1.0, 1.0, 0.0),
            jnp.where(evens == slot + 1.0, 1.0, 0.0),
            jnp.where(odds == slot, 1.0, 0.0),
        ],
        axis=0,
    )
    low = lax.broadcasted_iota(jnp.int32, (32, 128), 1) < 64

    def placed(x):
        y = jnp.dot(place, x, precision=HI, preferred_element_type=F32)
        return jnp.where(low, y[0:32], y[32:64]) + pltpu.roll(jnp.where(low, y[64:96], y[96:128]), 64, 1)

    aux = placed(got[:, 0:32, :].reshape(128, 128))
    inverse = placed(got[:, 32:64, :].reshape(128, 128))
    moved = placed(got[:, 72:104, :].reshape(128, 128))
    out[0:32, :] = 2.0 * aux - kappa * (moved + aux)
    out[32:64, :] = kappa * inverse
    for c in second:
        c.wait()
    total = far[0]
    for k in range(1, LINE):
        total = total + far[k]
    top = jnp.sum(jnp.where(first_half, total, 0.0), axis=1, keepdims=True)
    bottom = jnp.sum(jnp.where(first_half, 0.0, total), axis=1, keepdims=True)
    out[64:72, :] = jnp.broadcast_to(top / bottom, (8, 128))


def finish(fe, early):
    vm = pl.BlockSpec(memory_space=pltpu.VMEM)
    dma = pltpu.SemaphoreType.DMA
    return pl.pallas_call(
        level_kernel,
        out_shape=jax.ShapeDtypeStruct((72, 128), F32),
        in_specs=[pl.BlockSpec(memory_space=pl.ANY)] * 2,
        out_specs=vm,
        scratch_shapes=[
            pltpu.VMEM((32, 128), F32),
            pltpu.VMEM((72, 128), F32),
            dma((2,)),
            pltpu.VMEM((4, 104, 128), F32),
            pltpu.VMEM((SHEET, 1, 128), F32),
            pltpu.VMEM((LINE, 1, 128), F32),
            dma((SHEET - 1,)), dma((SHEET - 1,)), dma((3,)), dma((3,)), dma((LINE - 1,)), dma((LINE - 1,)),
            pltpu.SemaphoreType.REGULAR,
        ],
        compiler_params=pltpu.CompilerParams(collective_id=1, has_side_effects=True, vmem_limit_bytes=60 * 2**20),
        name="level",
    )(fe, early)


def last_kernel(out, fe, early, prev, charges, nxt):
    level = jnp.broadcast_to(out[64:65, :], (32, 128))
    charges[...] = level * early[32:64, :] - fe[...]
    nxt[...] = out[0:32, :] - prev[...] + level * out[32:64, :]


def last_step(out, fe, early, prev):
    vm = pl.BlockSpec(memory_space=pltpu.VMEM)
    return pl.pallas_call(
        last_kernel,
        out_shape=[jax.ShapeDtypeStruct((32, 128), F32)] * 2,
        in_specs=[vm] * 4,
        out_specs=[vm] * 2,
        name="last_step",
    )(out, fe, early, prev)


def on_device(positions, aux, aux_prev, resid, types, pair_tiles, pair_cands, pair_count, owner_tile, electroneg, hardness, widths):
    own, halo, early, codes, feats, centres = exchange(
        positions.transpose(0, 2, 1, 3).reshape(96, 128),
        aux.reshape(32, 128),
        resid.reshape(32, 128),
        types.reshape(32, 128),
        owner_tile.reshape(1, -1),
        pair_tiles.reshape(1, -1),
        pair_cands.reshape(1, -1),
        hardness,
        widths,
        pair_count,
    )
    fe, rf = pair_call(codes, widths, electroneg, hardness, own, halo, feats, centres)
    out = finish(fe, early)
    charges, nxt = last_step(out, fe, early, aux_prev.reshape(32, 128))
    return charges.reshape(aux.shape), nxt.reshape(aux.shape), rf.reshape(aux.shape)


def solution(mesh):
    s4, s3, s2 = P("brick", "plane", None, None), P("brick", "plane", None), P("brick", "plane")
    return jax.shard_map(
        on_device,
        mesh=mesh,
        in_specs=(s4, s3, s3, s3, s3, s3, s3, s2, s3, P(), P(), P()),
        out_specs=(s3, s3, s3),
        check_vma=False,
    )
```

```python
import functools

import jax
import jax.numpy as jnp
from jax import lax
from jax.experimental import pallas as pl
from jax.experimental.pallas import tpu as pltpu
from jax.sharding import PartitionSpec as P

F32 = jnp.float32
BF = jnp.bfloat16
HI = lax.Precision.HIGHEST
MESH = pl.DeviceIdType.MESH
kappa = 1.86

PB = 12
SB = 13
NT = 320


def order_pairs(tiles, cands, count, codes, tr, cr):
    n = tiles.shape[1]
    one = lax.broadcasted_iota(jnp.int32, (1, 128), 1)
    tr[...] = jnp.full((128, 128), 64.0, F32)
    cr[...] = jnp.zeros((16, 128), F32)
    for j in range(PB):
        w = min(128, n - 128 * j)
        tr[j : j + 1, :w] = tiles[:, 128 * j : 128 * j + w].astype(F32)
        cr[j : j + 1, :w] = cands[:, 128 * j : 128 * j + w].astype(F32)
    prow = lax.broadcasted_iota(jnp.int32, (16, 128), 0) * 128 + lax.broadcasted_iota(jnp.int32, (16, 128), 1)
    used = prow < count[0, 0]
    t = jnp.where(used, tr[:16], 64.0)
    c = jnp.where(used, cr[...], 0.0)
    tr[:16] = t
    tcol = tr[...].T
    lane = lax.broadcasted_iota(jnp.int32, (128, 128), 1)
    rowi = lax.broadcasted_iota(jnp.int32, (128, 128), 0)
    lanef = lane.astype(F32)
    before = jnp.where(lane < rowi, 1.0, 0.0).astype(BF)
    hot = [tcol[:, j : j + 1] == lanef for j in range(PB)]
    hotf = [jnp.where(h, 1.0, 0.0) for h in hot]
    sums = [jnp.sum(h, axis=0, keepdims=True) for h in hotf]
    counts = sum(sums)
    counts = jnp.where(one < 64, counts, 0.0)
    half = jnp.floor((counts + 1.0) * 0.5)
    starts = 2.0 * jnp.dot(jnp.broadcast_to(half, (8, 128)), jnp.where(rowi < lane, 1.0, 0.0), precision=HI, preferred_element_type=F32)[:1]
    starts = jnp.where(one < 64, starts, 8192.0)
    codes[:, SB * 128 :] = jnp.broadcast_to(jnp.sum(half, axis=1, keepdims=True), (1, 128)).astype(jnp.int32)
    out = jnp.zeros((8, SB * 128), F32)
    slot = lax.broadcasted_iota(jnp.int32, (128, SB * 128), 1).astype(F32)
    selfrow = jnp.zeros((1, 128), F32)
    e = float(NT) - c
    e = jnp.where(used, e, 0.0)
    ehi = jnp.floor(e * 0.5)
    elo = e - 2.0 * ehi
    same = jnp.where(t == c, 1.0, 0.0)
    r8 = lax.broadcasted_iota(jnp.int32, (8, 128), 0)
    for j in range(PB):
        rank = jnp.dot(before, hotf[j].astype(BF), preferred_element_type=F32)
        pos = jnp.sum(jnp.where(hot[j], rank + starts, 0.0), axis=1, keepdims=True)
        starts = starts + sums[j]
        vals = jnp.where(r8 == 0, ehi[j : j + 1], jnp.where(r8 == 1, elo[j : j + 1], jnp.where(r8 == 2, t[j : j + 1], same[j : j + 1])))
        put = jnp.where(pos == slot, 1.0, 0.0).astype(BF)
        out = out + jnp.dot(vals.astype(BF), put, preferred_element_type=F32)
        selfrow = selfrow + jnp.dot(vals.astype(BF), hotf[j].astype(BF), preferred_element_type=F32)[3:4]
    code = out[2:3] * 512.0 + (float(NT) - (2.0 * out[0:1] + out[1:2]))
    codes[:, : SB * 128] = code.astype(jnp.int32)
    lane32 = lax.broadcasted_iota(jnp.int32, (32, 128), 1)
    row32 = lax.broadcasted_iota(jnp.int32, (32, 128), 0)
    n = jnp.broadcast_to(selfrow, (32, 128))
    even = jnp.sum(jnp.where(lane32 == 2 * row32, n, 0.0), axis=1, keepdims=True)
    odd = jnp.sum(jnp.where(lane32 == 2 * row32 + 1, n, 0.0), axis=1, keepdims=True)
    return jnp.where(lane32 < 64, even, odd)


NR = 160
UN = 8
NB = 2


def split3(x):
    a = x.astype(BF).astype(F32)
    r = x - a
    b = r.astype(BF).astype(F32)
    return a, b, r - b


def home_features(own, widths, L, CH):
    lane = lax.broadcasted_iota(jnp.int32, (8, 128), 1)
    row = lax.broadcasted_iota(jnp.int32, (8, 128), 0)
    low = lane < 64

    def halves(x):
        y = pltpu.roll(x, 64, 1)
        return jnp.where(low, x, y), jnp.where(low, y, x)

    st = jnp.zeros((8, 128), F32)
    for t in range(8):
        st = jnp.where(row == t, widths[t], st)
    st = st * st * 0.01

    def prep_home(r, carry):
        v = own[pl.ds(r, 8, stride=32), :]
        v = jnp.where(row < 3, v * 0.1, v)
        x = v[:, 0:1]
        y = v[:, 64:65]
        cen = jnp.where(low, jnp.broadcast_to(x, (8, 128)), jnp.broadcast_to(y, (8, 128)))
        cen = jnp.where(row < 3, cen, 0.0)
        a = v - cen
        n = jnp.sum(jnp.where(row < 3, a * a, 0.0), axis=0, keepdims=True) + 0.0025
        f = jnp.where(row < 3, -2.0 * a, jnp.where(row < 6, 1.0, jnp.where(row == 6, n, 0.0)))
        f1, f2, f3 = split3(f)
        si = jnp.sum(jnp.where(row.astype(F32) == v[5:6], st, 0.0), axis=0, keepdims=True)
        w1, w2, w3 = split3(lax.rsqrt(st + si))
        t = jnp.concatenate([f1, f1, f1, f2, f2, f3, w1, w2, jnp.zeros((64, 128), F32)], axis=0).T.astype(BF)
        L[r * 2] = t[:64]
        L[r * 2 + 1] = t[64:]
        c0, c1 = halves(cen)
        CH[r * 2] = c0
        CH[r * 2 + 1] = c1
        return carry

    lax.fori_loop(0, 32, prep_home, 0, unroll=8)


def pair_kernel(codes_h, widths, chi, hard, own_h, halo_h, feat_h, centre_h, fe, rf, codes, own, halo, L, CH, sem, G, C, acc, *bufs):
    loads = [
        pltpu.make_async_copy(s, d, sem.at[k])
        for k, (s, d) in enumerate(((own_h, own), (halo_h, halo), (codes_h, codes), (feat_h, L), (centre_h, CH)))
    ]
    for c in loads:
        c.start()
    lane = lax.broadcasted_iota(jnp.int32, (8, 128), 1)
    row = lax.broadcasted_iota(jnp.int32, (8, 128), 0)
    low = lane < 64
    DS, VS = bufs[:NB], bufs[NB:]
    for k in range(NB):
        DS[k][...] = jnp.ones_like(DS[k])
        VS[k][...] = jnp.zeros_like(VS[k])

    def clear(h, carry):
        acc[0, h] = jnp.zeros((64, 128), F32)
        acc[1, h] = jnp.zeros((64, 128), F32)
        return carry

    lax.fori_loop(0, 64, clear, 0, unroll=4)

    for c in loads[:2]:
        c.wait()
    for b in range(5):
        at = [own[pl.ds(32 * c, 32), :] if b == 0 else halo[b - 1, pl.ds(32 * c, 32), :] for c in range(6)]
        if b in (1, 2):
            at[0] = at[0] + (-16.0 if b == 1 else 16.0)
        if b in (3, 4):
            at[1] = at[1] + (-32.0 if b == 3 else 32.0)
        for c, x in enumerate((at[0] * 0.1, at[1] * 0.1, at[2] * 0.1, at[3] * 0.1, at[4] * 0.1, at[5])):
            G[pl.ds(c * NR + b * 32, 32), :] = x
    G[pl.ds(6 * NR, 2 * NR), :] = jnp.zeros((2 * NR, 128), F32)

    def halves(x):
        y = pltpu.roll(x, 64, 1)
        return jnp.where(low, x, y), jnp.where(low, y, x)

    def prep(g, carry):
        c0, c1 = halves(G[pl.ds(g, 8, stride=NR), :])
        C[g * 2] = c0
        C[g * 2 + 1] = c1
        return carry

    lax.fori_loop(0, NR, prep, 0, unroll=16)

    C[NT] = jnp.where((row == 3) | (row == 4), 0.0, C[0])

    for c in loads[2:]:
        c.wait()
    types8 = row.astype(F32)
    zeros16 = jnp.zeros((16, 128), BF)
    zeros48 = jnp.zeros((48, 128), BF)
    last = jnp.where(row == 6, 1.0, 0.0)

    def terms(i, D, V):
        for u in range(UN):
            h = lax.shift_right_logical(codes[0, 2 * UN * i + 2 * u], 9)
            xs = [jnp.broadcast_to(V[u, k : k + 1], (8, 128)) for k in range(3, 5)]
            for q in range(8):
                rows = pl.ds(8 * q, 8)
                d = D[u, rows, pl.ds(0, 128)]
                w = D[u, rows, pl.ds(128, 128)]
                r = lax.rsqrt(d)
                e = lax.erf(d * r * w)
                m = jnp.maximum(1.0025 - d, 0.0)
                kk = (e * r) * (m * m)
                acc[0, h, rows] = acc[0, h, rows] + kk * xs[0]
                acc[1, h, rows] = acc[1, h, rows] + kk * xs[1]

    def distances(i, D, V):
        for u in range(UN):
            k1 = codes[0, 2 * UN * i + 2 * u]
            k2 = codes[0, 2 * UN * i + 2 * u + 1]
            h = lax.shift_right_logical(k1, 9)
            v = jnp.where(low, C[k1 & 511], C[k2 & 511]) - CH[h]
            V[u] = v
            f = jnp.where(row < 3, v, jnp.where(row < 6, pltpu.roll(v * v, 3, 0), last))
            s1, s2, s3 = split3(f)
            g = jnp.concatenate([s1, s2, s3, s1, s2, s1], axis=0).astype(BF)
            oh = jnp.where(types8 == v[5:6], 1.0, 0.0)
            oh = jnp.concatenate([oh, oh], axis=0).astype(BF)
            g = jnp.concatenate(
                [jnp.concatenate([g, zeros16], axis=0), jnp.concatenate([zeros48, oh], axis=0)], axis=1
            )
            D[u] = jnp.dot(L[h, :, pl.ds(0, 64)], g, preferred_element_type=F32)

    def step(i, carry):
        for k in range(NB):
            terms(jnp.maximum(NB * i + k - 1, 0), DS[k - 1], VS[k - 1])
            distances(NB * i + k, DS[k], VS[k])
        return carry

    blocks = lax.div(codes[0, 1664] + UN - 1, UN)
    lax.fori_loop(0, lax.div(blocks + NB, NB), step, 0)

    def finish(r, carry):
        for f, ref in enumerate((fe, rf)):
            ref[pl.ds(r, 1), :] = jnp.sum(acc[f, pl.ds(2 * r, 2)].reshape(128, 128).T, axis=0, keepdims=True)
        return carry

    lax.fori_loop(0, 32, finish, 0, unroll=8)
    s2 = jnp.zeros((32, 128), F32)
    ch = jnp.zeros((32, 128), F32)
    eta = jnp.zeros((32, 128), F32)
    for t in range(8):
        hit = own[160:192] == float(t)
        s2 = jnp.where(hit, widths[t] * widths[t], s2)
        ch = jnp.where(hit, chi[t], ch)
        eta = jnp.where(hit, hard[t], eta)
    itself = own[192:224] * (2.0 * lax.erf(0.5 * lax.rsqrt(s2 + s2)))
    residual = rf[...] - itself * own[128:160]
    field = ch + (fe[...] - itself * own[96:128]) + residual
    rf[...] = residual
    fe[...] = field / eta


def pair_call(codes, widths, chi, hard, own, halo, feats, centres):
    sm = pl.BlockSpec(memory_space=pltpu.SMEM)
    vm = pl.BlockSpec(memory_space=pltpu.VMEM)
    hbm = pl.BlockSpec(memory_space=pl.ANY)
    return pl.pallas_call(
        pair_kernel,
        out_shape=[jax.ShapeDtypeStruct((32, 128), F32)] * 2,
        in_specs=[hbm] + [sm] * 3 + [hbm] * 4,
        out_specs=[vm, vm],
        scratch_shapes=[
            pltpu.SMEM(codes.shape, jnp.int32),
            pltpu.VMEM(own.shape, F32),
            pltpu.VMEM(halo.shape, F32),
            pltpu.VMEM(feats.shape, BF),
            pltpu.VMEM(centres.shape, F32),
            pltpu.SemaphoreType.DMA((5,)),
            pltpu.VMEM((8 * NR, 128), F32),
            pltpu.VMEM((NT + 1, 8, 128), F32),
            pltpu.VMEM((2, 64, 64, 128), F32),
            *[pltpu.VMEM((UN, 64, 256), F32)] * NB,
            *[pltpu.VMEM((UN, 8, 128), F32)] * NB,
        ],
        compiler_params=pltpu.CompilerParams(vmem_limit_bytes=60 * 2**20),
        name="pairs",
    )(codes, widths, chi, hard, own, halo, feats, centres)


def exchange_kernel(
    pos_h, aux_h, resid_h, types_h, owner_h, tiles_h, cands_h, hard, widths, count,
    own_h, halo_h, early_h, codes_h, feat_h, centre_h,
    pos, aux, resid, types, owner, tiles, cands, own, early, codes, L, CH, tr, cr, load, send, recv, store,
):
    nb, npl = lax.axis_size("brick"), lax.axis_size("plane")
    b, p = lax.axis_index("brick"), lax.axis_index("plane")
    below, above = lax.rem(b + nb - 1, nb), lax.rem(b + 1, nb)
    barrier = pltpu.get_barrier_semaphore()
    left, right = lax.rem(p + npl - 1, npl), lax.rem(p + 1, npl)
    for d in [(below, p), (above, p), (b, left), (b, right)]:
        pl.semaphore_signal(barrier, inc=1, device_id=d, device_id_type=MESH)
    ins = ((pos_h, pos), (aux_h, aux), (resid_h, resid), (types_h, types), (owner_h, owner), (tiles_h, tiles), (cands_h, cands))
    loads = [pltpu.make_async_copy(x, y, load.at[k]) for k, (x, y) in enumerate(ins)]
    for c in loads:
        c.start()
    for c in loads:
        c.wait()
    own[0:96, :] = pos[...]
    own[96:128, :] = aux[...]
    own[128:160, :] = resid[...]
    ty = types[...].astype(F32)
    own[160:192, :] = ty
    own[192:256, :] = jnp.zeros((64, 128), F32)
    pl.semaphore_wait(barrier, 4)

    def copy(s, d, k, to):
        return pltpu.make_async_remote_copy(
            src_ref=s, dst_ref=d, send_sem=send.at[k], recv_sem=recv.at[k], device_id=to, device_id_type=MESH
        )

    mine = own.at[pl.ds(0, 192)]
    copies = [
        copy(mine, halo_h.at[0], 0, (above, p)),
        copy(mine, halo_h.at[1], 1, (below, p)),
        copy(mine, halo_h.at[2], 2, (b, right)),
        copy(mine, halo_h.at[3], 3, (b, left)),
    ]
    for c in copies:
        c.start()
    inverse = jnp.zeros((32, 128), F32)
    for t in range(8):
        inverse = jnp.where(ty == float(t), 1.0 / jnp.full((32, 128), hard[t], F32), inverse)
    early[0:32, :] = aux[...]
    early[32:64, :] = inverse
    src = lax.broadcasted_iota(jnp.int32, (64, 128), 0)
    lane = lax.broadcasted_iota(jnp.int32, (64, 128), 1) - 32 * p
    inside = (lane >= 0) & (lane < 32)
    ids = jnp.broadcast_to(owner[...].astype(F32), (8, 64))
    evens = jnp.dot(ids, jnp.where(inside & (src == 2 * lane), 1.0, 0.0), precision=HI, preferred_element_type=F32)
    odds = jnp.dot(ids, jnp.where(inside & (src == 2 * lane + 1), 1.0, 0.0), precision=HI, preferred_element_type=F32)
    r8 = lax.broadcasted_iota(jnp.int32, (8, 128), 0)
    early[64:72, :] = jnp.where(r8 == 0, evens, odds)
    home_features(own, widths, L, CH)
    own[192:224, :] = order_pairs(tiles, cands, count, codes, tr, cr)
    outs = ((own, own_h), (early, early_h), (codes, codes_h), (L, feat_h), (CH, centre_h))
    stores = [pltpu.make_async_copy(x, y, store.at[k]) for k, (x, y) in enumerate(outs)]
    for c in stores:
        c.start()
    for c in stores:
        c.wait()
    for c in copies:
        c.wait()


def exchange(pos, aux, resid, types, owner, tiles, cands, hard, widths, count):
    hbm = pl.BlockSpec(memory_space=pl.ANY)
    dma = pltpu.SemaphoreType.DMA
    shape = jax.ShapeDtypeStruct
    ncodes = (SB + 1) * 128
    return pl.pallas_call(
        exchange_kernel,
        out_shape=[
            shape((256, 128), F32),
            shape((4, 192, 128), F32),
            shape((72, 128), F32),
            shape((1, ncodes), jnp.int32),
            shape((64, 64, 128), BF),
            shape((64, 8, 128), F32),
        ],
        in_specs=[hbm] * 7 + [pl.BlockSpec(memory_space=pltpu.SMEM)] * 3,
        out_specs=[hbm] * 6,
        scratch_shapes=[pltpu.VMEM(x.shape, x.dtype) for x in (pos, aux, resid, types, owner, tiles, cands)]
        + [
            pltpu.VMEM((256, 128), F32),
            pltpu.VMEM((72, 128), F32),
            pltpu.VMEM((1, ncodes), jnp.int32),
            pltpu.VMEM((64, 64, 128), BF),
            pltpu.VMEM((64, 8, 128), F32),
            pltpu.VMEM((128, 128), F32),
            pltpu.VMEM((16, 128), F32),
            dma((7,)), dma((4,)), dma((4,)), dma((5,)),
        ],
        compiler_params=pltpu.CompilerParams(collective_id=0, has_side_effects=True, vmem_limit_bytes=60 * 2**20),
        name="exchange",
    )(pos, aux, resid, types, owner, tiles, cands, hard, widths, count)


LINE, SHEET = 16, 32


def level_kernel(fe_h, early_h, out, fe, early, load, got, near, far, s1, r1, s2, r2, s3, r3, ready):
    npl = lax.axis_size("plane")
    b, p = lax.axis_index("brick"), lax.axis_index("plane")
    zhi = lax.rem(lax.div(b, 8), 4)
    z = npl * zhi + p
    w = 8 * lax.div(b, 32) + lax.rem(b, 8)

    def line(q):
        return (b + 8 * (lax.div(q, npl) - zhi), lax.rem(q, npl))

    def sheet(q):
        return (32 * lax.div(q, 8) + 8 * zhi + lax.rem(q, 8), p)

    lines = [lax.rem(z + k, LINE) for k in sorted(range(1, LINE), key=lambda k: abs(2 * k - LINE))]
    sheets = [lax.rem(w + k, SHEET) for k in sorted(range(1, SHEET), key=lambda k: abs(2 * k - SHEET))]
    mates = [lax.rem(p + k, npl) for k in range(1, npl)]
    barrier = pltpu.get_barrier_semaphore()
    for k in (4, 12, 3, 13, 2, 14, 1, 15):
        pl.semaphore_signal(barrier, inc=1, device_id=line(lax.rem(z + k, LINE)), device_id_type=MESH)
    for q in sheets:
        pl.semaphore_signal(barrier, inc=1, device_id=sheet(q), device_id_type=MESH)
    ins = ((fe_h, fe), (early_h, early))
    loads = [pltpu.make_async_copy(x, y, load.at[k]) for k, (x, y) in enumerate(ins)]
    for c in loads:
        c.start()
    for c in loads:
        c.wait()
    got[p, 0:72, :] = early[...]
    got[p, 72:104, :] = fe[...]

    def fold(x):
        s = jnp.sum(x, axis=0, keepdims=True)
        return s + pltpu.roll(s, 64, 1)

    first_half = lax.broadcasted_iota(jnp.int32, (1, 128), 1) < 64
    near[w] = jnp.where(first_half, fold(early[0:32, :] + fe[...]), fold(early[32:64, :]))
    pl.semaphore_wait(barrier, 8 + SHEET - 1)
    for k in (4, 12):
        pl.semaphore_signal(ready, inc=1, device_id=line(lax.rem(z + k, LINE)), device_id_type=MESH)

    def copy(s, d, ss, rs, to):
        return pltpu.make_async_remote_copy(
            src_ref=s, dst_ref=d, send_sem=ss, recv_sem=rs, device_id=to, device_id_type=MESH
        )

    first = [copy(near.at[w], near.at[w], s1.at[k], r1.at[k], sheet(q)) for k, q in enumerate(sheets)]
    for c in first:
        c.start()
    tiles = [copy(got.at[p], got.at[p], s2.at[k], r2.at[k], (b, q)) for k, q in enumerate(mates)]
    for c in tiles:
        c.start()
    for c in first:
        c.wait()
    total = near[0]
    for k in range(1, SHEET):
        total = total + near[k]
    far[z] = total
    pl.semaphore_wait(ready, 2)
    second = [copy(far.at[z], far.at[z], s3.at[k], r3.at[k], line(q)) for k, q in enumerate(lines)]
    for c in second:
        c.start()
    for c in tiles:
        c.wait()
    evens = got[0, 64:65, :] + got[1, 64:65, :] + got[2, 64:65, :] + got[3, 64:65, :]
    odds = got[0, 65:66, :] + got[1, 65:66, :] + got[2, 65:66, :] + got[3, 65:66, :]
    slot = (64 * p + 2 * lax.broadcasted_iota(jnp.int32, (32, 128), 0)).astype(F32)
    place = jnp.concatenate(
        [
            jnp.where(evens == slot, 1.0, 0.0),
            jnp.where(odds == slot + 1.0, 1.0, 0.0),
            jnp.where(evens == slot + 1.0, 1.0, 0.0),
            jnp.where(odds == slot, 1.0, 0.0),
        ],
        axis=0,
    )
    low = lax.broadcasted_iota(jnp.int32, (32, 128), 1) < 64

    def placed(x):
        y = jnp.dot(place, x, precision=HI, preferred_element_type=F32)
        return jnp.where(low, y[0:32], y[32:64]) + pltpu.roll(jnp.where(low, y[64:96], y[96:128]), 64, 1)

    aux = placed(got[:, 0:32, :].reshape(128, 128))
    inverse = placed(got[:, 32:64, :].reshape(128, 128))
    moved = placed(got[:, 72:104, :].reshape(128, 128))
    out[0:32, :] = 2.0 * aux - kappa * (moved + aux)
    out[32:64, :] = kappa * inverse
    for c in second:
        c.wait()
    total = far[0]
    for k in range(1, LINE):
        total = total + far[k]
    top = jnp.sum(jnp.where(first_half, total, 0.0), axis=1, keepdims=True)
    bottom = jnp.sum(jnp.where(first_half, 0.0, total), axis=1, keepdims=True)
    out[64:72, :] = jnp.broadcast_to(top / bottom, (8, 128))


def finish(fe, early):
    vm = pl.BlockSpec(memory_space=pltpu.VMEM)
    dma = pltpu.SemaphoreType.DMA
    return pl.pallas_call(
        level_kernel,
        out_shape=jax.ShapeDtypeStruct((72, 128), F32),
        in_specs=[pl.BlockSpec(memory_space=pl.ANY)] * 2,
        out_specs=vm,
        scratch_shapes=[
            pltpu.VMEM((32, 128), F32),
            pltpu.VMEM((72, 128), F32),
            dma((2,)),
            pltpu.VMEM((4, 104, 128), F32),
            pltpu.VMEM((SHEET, 1, 128), F32),
            pltpu.VMEM((LINE, 1, 128), F32),
            dma((SHEET - 1,)), dma((SHEET - 1,)), dma((3,)), dma((3,)), dma((LINE - 1,)), dma((LINE - 1,)),
            pltpu.SemaphoreType.REGULAR,
        ],
        compiler_params=pltpu.CompilerParams(collective_id=1, has_side_effects=True, vmem_limit_bytes=60 * 2**20),
        name="level",
    )(fe, early)


def last_kernel(out, fe, early, prev, charges, nxt):
    level = jnp.broadcast_to(out[64:65, :], (32, 128))
    charges[...] = level * early[32:64, :] - fe[...]
    nxt[...] = out[0:32, :] - prev[...] + level * out[32:64, :]


def last_step(out, fe, early, prev):
    vm = pl.BlockSpec(memory_space=pltpu.VMEM)
    return pl.pallas_call(
        last_kernel,
        out_shape=[jax.ShapeDtypeStruct((32, 128), F32)] * 2,
        in_specs=[vm] * 4,
        out_specs=[vm] * 2,
        name="last_step",
    )(out, fe, early, prev)


def on_device(positions, aux, aux_prev, resid, types, pair_tiles, pair_cands, pair_count, owner_tile, electroneg, hardness, widths):
    own, halo, early, codes, feats, centres = exchange(
        positions.transpose(0, 2, 1, 3).reshape(96, 128),
        aux.reshape(32, 128),
        resid.reshape(32, 128),
        types.reshape(32, 128),
        owner_tile.reshape(1, -1),
        pair_tiles.reshape(1, -1),
        pair_cands.reshape(1, -1),
        hardness,
        widths,
        pair_count,
    )
    fe, rf = pair_call(codes, widths, electroneg, hardness, own, halo, feats, centres)
    out = finish(fe, early)
    charges, nxt = last_step(out, fe, early, aux_prev.reshape(32, 128))
    return charges.reshape(aux.shape), nxt.reshape(aux.shape), rf.reshape(aux.shape)


def solution(mesh):
    s4, s3, s2 = P("brick", "plane", None, None), P("brick", "plane", None), P("brick", "plane")
    return jax.shard_map(
        on_device,
        mesh=mesh,
        in_specs=(s4, s3, s3, s3, s3, s3, s3, s2, s3, P(), P(), P()),
        out_specs=(s3, s3, s3),
        check_vma=False,
    )
```

```python
import functools

import jax
import jax.numpy as jnp
from jax import lax
from jax.experimental import pallas as pl
from jax.experimental.pallas import tpu as pltpu
from jax.sharding import PartitionSpec as P

F32 = jnp.float32
BF = jnp.bfloat16
HI = lax.Precision.HIGHEST
MESH = pl.DeviceIdType.MESH
kappa = 1.86

PB = 12
SB = 13
NT = 320


def order_pairs(tiles, cands, count, codes, tr, cr):
    n = tiles.shape[1]
    one = lax.broadcasted_iota(jnp.int32, (1, 128), 1)
    tr[...] = jnp.full((128, 128), 64.0, F32)
    cr[...] = jnp.zeros((16, 128), F32)
    for j in range(PB):
        w = min(128, n - 128 * j)
        tr[j : j + 1, :w] = tiles[:, 128 * j : 128 * j + w].astype(F32)
        cr[j : j + 1, :w] = cands[:, 128 * j : 128 * j + w].astype(F32)
    prow = lax.broadcasted_iota(jnp.int32, (16, 128), 0) * 128 + lax.broadcasted_iota(jnp.int32, (16, 128), 1)
    used = prow < count[0, 0]
    t = jnp.where(used, tr[:16], 64.0)
    c = jnp.where(used, cr[...], 0.0)
    tr[:16] = t
    tcol = tr[...].T
    lane = lax.broadcasted_iota(jnp.int32, (128, 128), 1)
    rowi = lax.broadcasted_iota(jnp.int32, (128, 128), 0)
    lanef = lane.astype(F32)
    before = jnp.where(lane < rowi, 1.0, 0.0).astype(BF)
    hot = [tcol[:, j : j + 1] == lanef for j in range(PB)]
    hotf = [jnp.where(h, 1.0, 0.0) for h in hot]
    sums = [jnp.sum(h, axis=0, keepdims=True) for h in hotf]
    counts = sum(sums)
    counts = jnp.where(one < 64, counts, 0.0)
    half = jnp.floor((counts + 1.0) * 0.5)
    starts = 2.0 * jnp.dot(jnp.broadcast_to(half, (8, 128)), jnp.where(rowi < lane, 1.0, 0.0), precision=HI, preferred_element_type=F32)[:1]
    starts = jnp.where(one < 64, starts, 8192.0)
    codes[:, SB * 128 :] = jnp.broadcast_to(jnp.sum(half, axis=1, keepdims=True), (1, 128)).astype(jnp.int32)
    out = jnp.zeros((8, SB * 128), F32)
    slot = lax.broadcasted_iota(jnp.int32, (128, SB * 128), 1).astype(F32)
    selfrow = jnp.zeros((1, 128), F32)
    e = float(NT) - c
    e = jnp.where(used, e, 0.0)
    ehi = jnp.floor(e * 0.5)
    elo = e - 2.0 * ehi
    same = jnp.where(t == c, 1.0, 0.0)
    r8 = lax.broadcasted_iota(jnp.int32, (8, 128), 0)
    for j in range(PB):
        rank = jnp.dot(before, hotf[j].astype(BF), preferred_element_type=F32)
        pos = jnp.sum(jnp.where(hot[j], rank + starts, 0.0), axis=1, keepdims=True)
        starts = starts + sums[j]
        vals = jnp.where(r8 == 0, ehi[j : j + 1], jnp.where(r8 == 1, elo[j : j + 1], jnp.where(r8 == 2, t[j : j + 1], same[j : j + 1])))
        put = jnp.where(pos == slot, 1.0, 0.0).astype(BF)
        out = out + jnp.dot(vals.astype(BF), put, preferred_element_type=F32)
        selfrow = selfrow + jnp.dot(vals.astype(BF), hotf[j].astype(BF), preferred_element_type=F32)[3:4]
    code = out[2:3] * 512.0 + (float(NT) - (2.0 * out[0:1] + out[1:2]))
    codes[:, : SB * 128] = code.astype(jnp.int32)
    lane32 = lax.broadcasted_iota(jnp.int32, (32, 128), 1)
    row32 = lax.broadcasted_iota(jnp.int32, (32, 128), 0)
    n = jnp.broadcast_to(selfrow, (32, 128))
    even = jnp.sum(jnp.where(lane32 == 2 * row32, n, 0.0), axis=1, keepdims=True)
    odd = jnp.sum(jnp.where(lane32 == 2 * row32 + 1, n, 0.0), axis=1, keepdims=True)
    return jnp.where(lane32 < 64, even, odd)


NR = 160
UN = 8
NB = 2


def split3(x):
    a = x.astype(BF).astype(F32)
    r = x - a
    b = r.astype(BF).astype(F32)
    return a, b, r - b


def home_features(own, widths, L, CH):
    lane = lax.broadcasted_iota(jnp.int32, (8, 128), 1)
    row = lax.broadcasted_iota(jnp.int32, (8, 128), 0)
    low = lane < 64

    def halves(x):
        y = pltpu.roll(x, 64, 1)
        return jnp.where(low, x, y), jnp.where(low, y, x)

    st = jnp.zeros((8, 128), F32)
    for t in range(8):
        st = jnp.where(row == t, widths[t], st)
    st = st * st * 0.01

    def prep_home(r, carry):
        v = own[pl.ds(r, 8, stride=32), :]
        v = jnp.where(row < 3, v * 0.1, v)
        x = v[:, 0:1]
        y = v[:, 64:65]
        cen = jnp.where(low, jnp.broadcast_to(x, (8, 128)), jnp.broadcast_to(y, (8, 128)))
        cen = jnp.where(row < 3, cen, 0.0)
        a = v - cen
        n = jnp.sum(jnp.where(row < 3, a * a, 0.0), axis=0, keepdims=True) + 0.0025
        f = jnp.where(row < 3, -2.0 * a, jnp.where(row < 6, 1.0, jnp.where(row == 6, n, 0.0)))
        f1, f2, f3 = split3(f)
        si = jnp.sum(jnp.where(row.astype(F32) == v[5:6], st, 0.0), axis=0, keepdims=True)
        w1, w2, w3 = split3(lax.rsqrt(st + si))
        t = jnp.concatenate([f1, f1, f1, f2, f2, f3, w1, w2, jnp.zeros((64, 128), F32)], axis=0).T.astype(BF)
        L[r * 2] = t[:64]
        L[r * 2 + 1] = t[64:]
        c0, c1 = halves(cen)
        CH[r * 2] = c0
        CH[r * 2 + 1] = c1
        return carry

    lax.fori_loop(0, 32, prep_home, 0, unroll=8)


def pair_kernel(codes_h, widths, chi, hard, own_h, halo_h, feat_h, centre_h, fe, rf, codes, own, halo, L, CH, sem, G, C, acc, *bufs):
    loads = [
        pltpu.make_async_copy(s, d, sem.at[k])
        for k, (s, d) in enumerate(((own_h, own), (halo_h, halo), (codes_h, codes), (feat_h, L), (centre_h, CH)))
    ]
    for c in loads:
        c.start()
    lane = lax.broadcasted_iota(jnp.int32, (8, 128), 1)
    row = lax.broadcasted_iota(jnp.int32, (8, 128), 0)
    low = lane < 64
    DS, VS = bufs[:NB], bufs[NB:]
    for k in range(NB):
        DS[k][...] = jnp.ones_like(DS[k])
        VS[k][...] = jnp.zeros_like(VS[k])

    def clear(h, carry):
        acc[0, h] = jnp.zeros((64, 128), F32)
        acc[1, h] = jnp.zeros((64, 128), F32)
        return carry

    lax.fori_loop(0, 64, clear, 0, unroll=4)

    for c in loads[:2]:
        c.wait()
    for b in range(5):
        at = [own[pl.ds(32 * c, 32), :] if b == 0 else halo[b - 1, pl.ds(32 * c, 32), :] for c in range(6)]
        if b in (1, 2):
            at[0] = at[0] + (-16.0 if b == 1 else 16.0)
        if b in (3, 4):
            at[1] = at[1] + (-32.0 if b == 3 else 32.0)
        for c, x in enumerate((at[0] * 0.1, at[1] * 0.1, at[2] * 0.1, at[3] * 0.1, at[4] * 0.1, at[5])):
            G[pl.ds(c * NR + b * 32, 32), :] = x
    G[pl.ds(6 * NR, 2 * NR), :] = jnp.zeros((2 * NR, 128), F32)

    def halves(x):
        y = pltpu.roll(x, 64, 1)
        return jnp.where(low, x, y), jnp.where(low, y, x)

    def prep(g, carry):
        c0, c1 = halves(G[pl.ds(g, 8, stride=NR), :])
        C[g * 2] = c0
        C[g * 2 + 1] = c1
        return carry

    lax.fori_loop(0, NR, prep, 0, unroll=16)

    C[NT] = jnp.where((row == 3) | (row == 4), 0.0, C[0])

    for c in loads[2:]:
        c.wait()
    types8 = row.astype(F32)
    zeros16 = jnp.zeros((16, 128), BF)
    zeros48 = jnp.zeros((48, 128), BF)
    last = jnp.where(row == 6, 1.0, 0.0)

    def terms(i, D, V):
        for u in range(UN):
            h = lax.shift_right_logical(codes[0, 2 * UN * i + 2 * u], 9)
            xs = [jnp.broadcast_to(V[u, k : k + 1], (8, 128)) for k in range(3, 5)]
            for q in range(8):
                rows = pl.ds(8 * q, 8)
                d = D[u, rows, pl.ds(0, 128)]
                w = D[u, rows, pl.ds(128, 128)]
                r = lax.rsqrt(d)
                e = lax.erf(d * r * w)
                m = jnp.maximum(1.0025 - d, 0.0)
                kk = (e * r) * (m * m)
                acc[0, h, rows] = acc[0, h, rows] + kk * xs[0]
                acc[1, h, rows] = acc[1, h, rows] + kk * xs[1]

    def distances(i, D, V):
        for u in range(UN):
            k1 = codes[0, 2 * UN * i + 2 * u]
            k2 = codes[0, 2 * UN * i + 2 * u + 1]
            h = lax.shift_right_logical(k1, 9)
            v = jnp.where(low, C[k1 & 511], C[k2 & 511]) - CH[h]
            V[u] = v
            f = jnp.where(row < 3, v, jnp.where(row < 6, pltpu.roll(v * v, 3, 0), last))
            s1, s2, s3 = split3(f)
            g = jnp.concatenate([s1, s2, s3, s1, s2, s1], axis=0).astype(BF)
            oh = jnp.where(types8 == v[5:6], 1.0, 0.0)
            oh = jnp.concatenate([oh, oh], axis=0).astype(BF)
            g = jnp.concatenate(
                [jnp.concatenate([g, zeros16], axis=0), jnp.concatenate([zeros48, oh], axis=0)], axis=1
            )
            D[u] = jnp.dot(L[h, :, pl.ds(0, 64)], g, preferred_element_type=F32)

    def step(i, carry):
        for k in range(NB):
            terms(jnp.maximum(NB * i + k - 1, 0), DS[k - 1], VS[k - 1])
            distances(NB * i + k, DS[k], VS[k])
        return carry

    blocks = lax.div(codes[0, 1664] + UN - 1, UN)
    lax.fori_loop(0, lax.div(blocks + NB, NB), step, 0)

    def finish(r, carry):
        for f, ref in enumerate((fe, rf)):
            ref[pl.ds(r, 1), :] = jnp.sum(acc[f, pl.ds(2 * r, 2)].reshape(128, 128).T, axis=0, keepdims=True)
        return carry

    lax.fori_loop(0, 32, finish, 0, unroll=16)
    s2 = jnp.zeros((32, 128), F32)
    ch = jnp.zeros((32, 128), F32)
    eta = jnp.zeros((32, 128), F32)
    for t in range(8):
        hit = own[160:192] == float(t)
        s2 = jnp.where(hit, widths[t] * widths[t], s2)
        ch = jnp.where(hit, chi[t], ch)
        eta = jnp.where(hit, hard[t], eta)
    itself = own[192:224] * (2.0 * lax.erf(0.5 * lax.rsqrt(s2 + s2)))
    residual = rf[...] - itself * own[128:160]
    field = ch + (fe[...] - itself * own[96:128]) + residual
    rf[...] = residual
    fe[...] = field / eta


def pair_call(codes, widths, chi, hard, own, halo, feats, centres):
    sm = pl.BlockSpec(memory_space=pltpu.SMEM)
    vm = pl.BlockSpec(memory_space=pltpu.VMEM)
    hbm = pl.BlockSpec(memory_space=pl.ANY)
    return pl.pallas_call(
        pair_kernel,
        out_shape=[jax.ShapeDtypeStruct((32, 128), F32)] * 2,
        in_specs=[hbm] + [sm] * 3 + [hbm] * 4,
        out_specs=[vm, vm],
        scratch_shapes=[
            pltpu.SMEM(codes.shape, jnp.int32),
            pltpu.VMEM(own.shape, F32),
            pltpu.VMEM(halo.shape, F32),
            pltpu.VMEM(feats.shape, BF),
            pltpu.VMEM(centres.shape, F32),
            pltpu.SemaphoreType.DMA((5,)),
            pltpu.VMEM((8 * NR, 128), F32),
            pltpu.VMEM((NT + 1, 8, 128), F32),
            pltpu.VMEM((2, 64, 64, 128), F32),
            *[pltpu.VMEM((UN, 64, 256), F32)] * NB,
            *[pltpu.VMEM((UN, 8, 128), F32)] * NB,
        ],
        compiler_params=pltpu.CompilerParams(vmem_limit_bytes=60 * 2**20),
        name="pairs",
    )(codes, widths, chi, hard, own, halo, feats, centres)


def exchange_kernel(
    pos_h, aux_h, resid_h, types_h, owner_h, tiles_h, cands_h, hard, widths, count,
    own_h, halo_h, early_h, codes_h, feat_h, centre_h,
    pos, aux, resid, types, owner, tiles, cands, own, early, codes, L, CH, tr, cr, load, send, recv, store,
):
    nb, npl = lax.axis_size("brick"), lax.axis_size("plane")
    b, p = lax.axis_index("brick"), lax.axis_index("plane")
    below, above = lax.rem(b + nb - 1, nb), lax.rem(b + 1, nb)
    barrier = pltpu.get_barrier_semaphore()
    left, right = lax.rem(p + npl - 1, npl), lax.rem(p + 1, npl)
    for d in [(below, p), (above, p), (b, left), (b, right)]:
        pl.semaphore_signal(barrier, inc=1, device_id=d, device_id_type=MESH)
    ins = ((pos_h, pos), (aux_h, aux), (resid_h, resid), (types_h, types), (owner_h, owner), (tiles_h, tiles), (cands_h, cands))
    loads = [pltpu.make_async_copy(x, y, load.at[k]) for k, (x, y) in enumerate(ins)]
    for c in loads:
        c.start()
    for c in loads:
        c.wait()
    own[0:96, :] = pos[...]
    own[96:128, :] = aux[...]
    own[128:160, :] = resid[...]
    ty = types[...].astype(F32)
    own[160:192, :] = ty
    own[192:256, :] = jnp.zeros((64, 128), F32)
    pl.semaphore_wait(barrier, 4)

    def copy(s, d, k, to):
        return pltpu.make_async_remote_copy(
            src_ref=s, dst_ref=d, send_sem=send.at[k], recv_sem=recv.at[k], device_id=to, device_id_type=MESH
        )

    mine = own.at[pl.ds(0, 192)]
    copies = [
        copy(mine, halo_h.at[0], 0, (above, p)),
        copy(mine, halo_h.at[1], 1, (below, p)),
        copy(mine, halo_h.at[2], 2, (b, right)),
        copy(mine, halo_h.at[3], 3, (b, left)),
    ]
    for c in copies:
        c.start()
    inverse = jnp.zeros((32, 128), F32)
    for t in range(8):
        inverse = jnp.where(ty == float(t), 1.0 / jnp.full((32, 128), hard[t], F32), inverse)
    early[0:32, :] = aux[...]
    early[32:64, :] = inverse
    src = lax.broadcasted_iota(jnp.int32, (64, 128), 0)
    lane = lax.broadcasted_iota(jnp.int32, (64, 128), 1) - 32 * p
    inside = (lane >= 0) & (lane < 32)
    ids = jnp.broadcast_to(owner[...].astype(F32), (8, 64))
    evens = jnp.dot(ids, jnp.where(inside & (src == 2 * lane), 1.0, 0.0), precision=HI, preferred_element_type=F32)
    odds = jnp.dot(ids, jnp.where(inside & (src == 2 * lane + 1), 1.0, 0.0), precision=HI, preferred_element_type=F32)
    r8 = lax.broadcasted_iota(jnp.int32, (8, 128), 0)
    early[64:72, :] = jnp.where(r8 == 0, evens, odds)
    home_features(own, widths, L, CH)
    own[192:224, :] = order_pairs(tiles, cands, count, codes, tr, cr)
    outs = ((own, own_h), (early, early_h), (codes, codes_h), (L, feat_h), (CH, centre_h))
    stores = [pltpu.make_async_copy(x, y, store.at[k]) for k, (x, y) in enumerate(outs)]
    for c in stores:
        c.start()
    for c in stores:
        c.wait()
    for c in copies:
        c.wait()


def exchange(pos, aux, resid, types, owner, tiles, cands, hard, widths, count):
    hbm = pl.BlockSpec(memory_space=pl.ANY)
    dma = pltpu.SemaphoreType.DMA
    shape = jax.ShapeDtypeStruct
    ncodes = (SB + 1) * 128
    return pl.pallas_call(
        exchange_kernel,
        out_shape=[
            shape((256, 128), F32),
            shape((4, 192, 128), F32),
            shape((72, 128), F32),
            shape((1, ncodes), jnp.int32),
            shape((64, 64, 128), BF),
            shape((64, 8, 128), F32),
        ],
        in_specs=[hbm] * 7 + [pl.BlockSpec(memory_space=pltpu.SMEM)] * 3,
        out_specs=[hbm] * 6,
        scratch_shapes=[pltpu.VMEM(x.shape, x.dtype) for x in (pos, aux, resid, types, owner, tiles, cands)]
        + [
            pltpu.VMEM((256, 128), F32),
            pltpu.VMEM((72, 128), F32),
            pltpu.VMEM((1, ncodes), jnp.int32),
            pltpu.VMEM((64, 64, 128), BF),
            pltpu.VMEM((64, 8, 128), F32),
            pltpu.VMEM((128, 128), F32),
            pltpu.VMEM((16, 128), F32),
            dma((7,)), dma((4,)), dma((4,)), dma((5,)),
        ],
        compiler_params=pltpu.CompilerParams(collective_id=0, has_side_effects=True, vmem_limit_bytes=60 * 2**20),
        name="exchange",
    )(pos, aux, resid, types, owner, tiles, cands, hard, widths, count)


LINE, SHEET = 16, 32


def level_kernel(fe_h, early_h, out, fe, early, load, got, near, far, s1, r1, s2, r2, s3, r3, ready):
    npl = lax.axis_size("plane")
    b, p = lax.axis_index("brick"), lax.axis_index("plane")
    zhi = lax.rem(lax.div(b, 8), 4)
    z = npl * zhi + p
    w = 8 * lax.div(b, 32) + lax.rem(b, 8)

    def line(q):
        return (b + 8 * (lax.div(q, npl) - zhi), lax.rem(q, npl))

    def sheet(q):
        return (32 * lax.div(q, 8) + 8 * zhi + lax.rem(q, 8), p)

    lines = [lax.rem(z + k, LINE) for k in sorted(range(1, LINE), key=lambda k: abs(2 * k - LINE))]
    sheets = [lax.rem(w + k, SHEET) for k in sorted(range(1, SHEET), key=lambda k: abs(2 * k - SHEET))]
    mates = [lax.rem(p + k, npl) for k in range(1, npl)]
    barrier = pltpu.get_barrier_semaphore()
    for k in (4, 12, 3, 13, 2, 14, 1, 15):
        pl.semaphore_signal(barrier, inc=1, device_id=line(lax.rem(z + k, LINE)), device_id_type=MESH)
    for q in sheets:
        pl.semaphore_signal(barrier, inc=1, device_id=sheet(q), device_id_type=MESH)
    ins = ((fe_h, fe), (early_h, early))
    loads = [pltpu.make_async_copy(x, y, load.at[k]) for k, (x, y) in enumerate(ins)]
    for c in loads:
        c.start()
    for c in loads:
        c.wait()
    got[p, 0:72, :] = early[...]
    got[p, 72:104, :] = fe[...]

    def fold(x):
        s = jnp.sum(x, axis=0, keepdims=True)
        return s + pltpu.roll(s, 64, 1)

    first_half = lax.broadcasted_iota(jnp.int32, (1, 128), 1) < 64
    near[w] = jnp.where(first_half, fold(early[0:32, :] + fe[...]), fold(early[32:64, :]))
    pl.semaphore_wait(barrier, 8 + SHEET - 1)
    for k in (4, 12):
        pl.semaphore_signal(ready, inc=1, device_id=line(lax.rem(z + k, LINE)), device_id_type=MESH)

    def copy(s, d, ss, rs, to):
        return pltpu.make_async_remote_copy(
            src_ref=s, dst_ref=d, send_sem=ss, recv_sem=rs, device_id=to, device_id_type=MESH
        )

    first = [copy(near.at[w], near.at[w], s1.at[k], r1.at[k], sheet(q)) for k, q in enumerate(sheets)]
    for c in first:
        c.start()
    tiles = [copy(got.at[p], got.at[p], s2.at[k], r2.at[k], (b, q)) for k, q in enumerate(mates)]
    for c in tiles:
        c.start()
    for c in first:
        c.wait()
    total = near[0]
    for k in range(1, SHEET):
        total = total + near[k]
    far[z] = total
    pl.semaphore_wait(ready, 2)
    second = [copy(far.at[z], far.at[z], s3.at[k], r3.at[k], line(q)) for k, q in enumerate(lines)]
    for c in second:
        c.start()
    for c in tiles:
        c.wait()
    evens = got[0, 64:65, :] + got[1, 64:65, :] + got[2, 64:65, :] + got[3, 64:65, :]
    odds = got[0, 65:66, :] + got[1, 65:66, :] + got[2, 65:66, :] + got[3, 65:66, :]
    slot = (64 * p + 2 * lax.broadcasted_iota(jnp.int32, (32, 128), 0)).astype(F32)
    place = jnp.concatenate(
        [
            jnp.where(evens == slot, 1.0, 0.0),
            jnp.where(odds == slot + 1.0, 1.0, 0.0),
            jnp.where(evens == slot + 1.0, 1.0, 0.0),
            jnp.where(odds == slot, 1.0, 0.0),
        ],
        axis=0,
    )
    low = lax.broadcasted_iota(jnp.int32, (32, 128), 1) < 64

    def placed(x):
        y = jnp.dot(place, x, precision=HI, preferred_element_type=F32)
        return jnp.where(low, y[0:32], y[32:64]) + pltpu.roll(jnp.where(low, y[64:96], y[96:128]), 64, 1)

    aux = placed(got[:, 0:32, :].reshape(128, 128))
    inverse = placed(got[:, 32:64, :].reshape(128, 128))
    moved = placed(got[:, 72:104, :].reshape(128, 128))
    out[0:32, :] = 2.0 * aux - kappa * (moved + aux)
    out[32:64, :] = kappa * inverse
    for c in second:
        c.wait()
    total = far[0]
    for k in range(1, LINE):
        total = total + far[k]
    top = jnp.sum(jnp.where(first_half, total, 0.0), axis=1, keepdims=True)
    bottom = jnp.sum(jnp.where(first_half, 0.0, total), axis=1, keepdims=True)
    out[64:72, :] = jnp.broadcast_to(top / bottom, (8, 128))


def finish(fe, early):
    vm = pl.BlockSpec(memory_space=pltpu.VMEM)
    dma = pltpu.SemaphoreType.DMA
    return pl.pallas_call(
        level_kernel,
        out_shape=jax.ShapeDtypeStruct((72, 128), F32),
        in_specs=[pl.BlockSpec(memory_space=pl.ANY)] * 2,
        out_specs=vm,
        scratch_shapes=[
            pltpu.VMEM((32, 128), F32),
            pltpu.VMEM((72, 128), F32),
            dma((2,)),
            pltpu.VMEM((4, 104, 128), F32),
            pltpu.VMEM((SHEET, 1, 128), F32),
            pltpu.VMEM((LINE, 1, 128), F32),
            dma((SHEET - 1,)), dma((SHEET - 1,)), dma((3,)), dma((3,)), dma((LINE - 1,)), dma((LINE - 1,)),
            pltpu.SemaphoreType.REGULAR,
        ],
        compiler_params=pltpu.CompilerParams(collective_id=1, has_side_effects=True, vmem_limit_bytes=60 * 2**20),
        name="level",
    )(fe, early)


def last_kernel(out, fe, early, prev, charges, nxt):
    level = jnp.broadcast_to(out[64:65, :], (32, 128))
    charges[...] = level * early[32:64, :] - fe[...]
    nxt[...] = out[0:32, :] - prev[...] + level * out[32:64, :]


def last_step(out, fe, early, prev):
    vm = pl.BlockSpec(memory_space=pltpu.VMEM)
    return pl.pallas_call(
        last_kernel,
        out_shape=[jax.ShapeDtypeStruct((32, 128), F32)] * 2,
        in_specs=[vm] * 4,
        out_specs=[vm] * 2,
        name="last_step",
    )(out, fe, early, prev)


def on_device(positions, aux, aux_prev, resid, types, pair_tiles, pair_cands, pair_count, owner_tile, electroneg, hardness, widths):
    own, halo, early, codes, feats, centres = exchange(
        positions.transpose(0, 2, 1, 3).reshape(96, 128),
        aux.reshape(32, 128),
        resid.reshape(32, 128),
        types.reshape(32, 128),
        owner_tile.reshape(1, -1),
        pair_tiles.reshape(1, -1),
        pair_cands.reshape(1, -1),
        hardness,
        widths,
        pair_count,
    )
    fe, rf = pair_call(codes, widths, electroneg, hardness, own, halo, feats, centres)
    out = finish(fe, early)
    charges, nxt = last_step(out, fe, early, aux_prev.reshape(32, 128))
    return charges.reshape(aux.shape), nxt.reshape(aux.shape), rf.reshape(aux.shape)


def solution(mesh):
    s4, s3, s2 = P("brick", "plane", None, None), P("brick", "plane", None), P("brick", "plane")
    return jax.shard_map(
        on_device,
        mesh=mesh,
        in_specs=(s4, s3, s3, s3, s3, s3, s3, s2, s3, P(), P(), P()),
        out_specs=(s3, s3, s3),
        check_vma=False,
    )
```
